32 devices in a mesh: dp: 4 (over y, core), mp: 8 (over z, x).
Axes of the slice: x: 2, y: 2, z: 4, core: 2. Of those that a mesh axis runs over, the one named last changes fastest.
Arguments:
- latents: float32 [128, 256, 16], P(('dp', 'mp')), may hold values from -6 to 6
- noise_draw: float32 [128, 256, 16], P(('dp', 'mp')), may hold values from -6 to 6
- alpha_bar: float32 [128], P('dp'), may hold values from 0.05 to 0.95
- timesteps: int32 [128], P('dp'), may hold values from 0 to 999
- labels: int32 [128], P('dp'), may hold values from 0 to 999
- lengths: int32 [128], replicated, may hold values from 1 to 256, as said below
- class_vectors: bfloat16 [1000, 1152], replicated, may hold values from -6 to 6
- embedder: float32 [16, 1152], replicated, may hold values from -1.5 to 1.5
- time_first: float32 [256, 1152], replicated, may hold values from -0.375 to 0.375
- time_second: float32 [1152, 1152], replicated, may hold values from -0.1875 to 0.1875
- modulator: float32 [1152, 6912], P(None, 'mp'), may hold values from -0.1875 to 0.1875
- mixer_input: float32 [1152, 3456], P(None, 'mp'), may hold values from -0.25 to 0.25
- mixer_output: float32 [1152, 1152], P('mp'), may hold values from -0.75 to 0.75
- expander: float32 [1152, 4608], P(None, 'mp'), may hold values from -0.1875 to 0.1875
- contractor: float32 [4608, 1152], P('mp'), may hold values from -0.09375 to 0.09375
- finisher: float32 [1152, 2304], P(None, 'mp'), may hold values from -0.1875 to 0.1875
- readout: float32 [1152, 16], replicated, may hold values from -0.1875 to 0.1875
- row_states: float32 [12944], replicated, may hold values from 8.8649465e-13 to 3.5459786e-12
- column_states: float32 [23056], replicated, may hold values from 8.8649465e-13 to 3.5459786e-12
Outputs:
- loss_sum: float32 [], replicated
- loss_count: float32 [], replicated
- grad_norm: float32 [], replicated
- embedder_next: float32 [16, 1152], replicated
- time_first_next: float32 [256, 1152], replicated
- time_second_next: float32 [1152, 1152], replicated
- modulator_next: float32 [1152, 6912], P(None, 'mp')
- mixer_input_next: float32 [1152, 3456], P(None, 'mp')
- mixer_output_next: float32 [1152, 1152], P('mp')
- expander_next: float32 [1152, 4608], P(None, 'mp')
- contractor_next: float32 [4608, 1152], P('mp')
- finisher_next: float32 [1152, 2304], P(None, 'mp')
- readout_next: float32 [1152, 16], replicated
- embedder_grad: float32 [16, 1152], replicated
- time_first_grad: float32 [256, 1152], replicated
- time_second_grad: float32 [1152, 1152], replicated
- modulator_grad: float32 [1152, 6912], P(None, 'mp')
- mixer_input_grad: float32 [1152, 3456], P(None, 'mp')
- mixer_output_grad: float32 [1152, 1152], P('mp')
- expander_grad: float32 [1152, 4608], P(None, 'mp')
- contractor_grad: float32 [4608, 1152], P('mp')
- finisher_grad: float32 [1152, 2304], P(None, 'mp')
- readout_grad: float32 [1152, 16], replicated
- row_stats: float32 [12944], replicated
- column_stats: float32 [23056], replicated
The draws below stay inside these ranges and needn't reach their ends.
Inputs may be any that keep to these rules, and one draw needn't show every extreme that they name: Patches 0 to lengths - 1 of an image are valid; at least one image is whole.
All inputs are finite; a program needn't handle non-finite values.
Results may differ from the reference program's by a relative error of at most 0.019.
The reference program's roundings to bfloat16 on the way count: a program that leaves them out, or rounds other values in their place, can miss the bound.
Values may be sent and summed in bfloat16 or wider, within the bound.
A program may use at most 576 MiB of HBM per device.

```python
import math
import jax
import jax.numpy as jnp
from jax import lax

D = 1152
HEADS = 16
HD = 72
FF = 4608
FREQ = 256
PIN = 16
LABELS = 1000
SIDE = 16
MICRO = 4
IMG_DEV = 1
IMAGES = 128
NR = 12944
NC = 23056
N_DP = 4
N_MP = 8


def draw_lengths(key, part):
    key = jax.random.fold_in(key, 7)
    images = IMG_DEV * MICRO * N_DP * N_MP
    image = jnp.arange(images, dtype=jnp.int32)
    device = image // (IMG_DEV * MICRO)
    rank_dp = device // N_MP
    rank_mp = device % N_MP
    span_dp = max(N_DP - 1, 1)
    span_mp = max(N_MP - 1, 1)
    whole = SIDE * SIDE
    ceiling = whole * (span_dp * span_mp + rank_dp * span_mp + rank_mp * span_dp) // (3 * span_dp * span_mp)
    drawn = jax.random.randint(key, (images,), 0, ceiling) + 1
    return drawn.at[images - 1].set(whole).astype(jnp.int32)


def set_ends(values, own_key, smallest, largest):
    longest = values.shape.index(max(values.shape))
    spots = []
    for shift in (0, 1):
        where = [jax.random.randint(jax.random.fold_in(own_key, axis), (), 0, length) for axis, length in enumerate(values.shape)]
        where[longest] = (where[longest] + shift) % values.shape[longest]
        spots.append(tuple(where))
    return values.at[spots[0]].set(smallest).at[spots[1]].set(largest)


def level_of(stream_key, shape, split, least, high):
    level, own = 1.0, jax.random.fold_in(stream_key, 6)
    for dim, blocks in split:
        steps = jnp.exp(jax.random.uniform(jax.random.fold_in(own, dim), (blocks,), jnp.float32, least / len(split), high / len(split)))
        level = level * jnp.repeat(steps, shape[dim] // blocks).reshape([-1 if axis == dim else 1 for axis in range(len(shape))])
    return level


def normal_values(own_key, extent, scale, most, shards=(), held_as=jnp.bfloat16):
    gain = level_of(own_key, extent, shards, -0.22, 0.18) if shards else 1.0
    values = jax.random.normal(own_key, extent, jnp.float32) * scale * gain
    return jnp.minimum(jnp.maximum(values, -most), most).astype(held_as)


def setup_inputs(seed: int = 0) -> dict:
    splits = jax.random.split(jax.random.key(seed), 20)
    latents = normal_values(splits[0], (IMAGES, SIDE * SIDE, PIN), 1.0, 6.0, ((0, 32),), jnp.float32)
    noise_draw = normal_values(splits[1], (IMAGES, SIDE * SIDE, PIN), 1.0, 6.0, ((0, 32),), jnp.float32)
    alpha_bar = jnp.clip(0.05 + 0.9 * jax.random.uniform(splits[2], (IMAGES,), jnp.float32) ** level_of(splits[2], (IMAGES,), ((0, 4),), -0.2, 0.2), 0.05, 0.95)
    timesteps = set_ends(jax.random.randint(splits[3], (IMAGES,), 0, 1000), jax.random.fold_in(splits[3], 1), 0, 999).astype(jnp.int32)
    labels = set_ends(jax.random.randint(splits[4], (IMAGES,), 0, LABELS), jax.random.fold_in(splits[4], 1), 0, LABELS - 1).astype(jnp.int32)
    lengths = draw_lengths(jax.random.fold_in(splits[19], 71), 0)
    class_vectors = normal_values(splits[6], (LABELS, D), 1.0, 6.0)
    embedder = normal_values(splits[7], (PIN, D), PIN ** -0.5, 1.5, (), jnp.float32)
    time_first = normal_values(splits[8], (FREQ, D), FREQ ** -0.5, 0.375, (), jnp.float32)
    time_second = normal_values(splits[9], (D, D), D ** -0.5, 0.1875, (), jnp.float32)
    modulator = normal_values(splits[10], (D, 6 * D), D ** -0.5, 0.1875, ((1, 8),), jnp.float32)
    mixer_input = normal_values(splits[11], (D, 3 * D), (D // 2) ** -0.5, 0.25, ((1, 8),), jnp.float32)
    mixer_output = normal_values(splits[12], (D, D), (D // 16) ** -0.5, 0.75, ((0, 8),), jnp.float32)
    expander = normal_values(splits[13], (D, FF), D ** -0.5, 0.1875, ((1, 8),), jnp.float32)
    contractor = normal_values(splits[14], (FF, D), FF ** -0.5, 0.09375, ((0, 8),), jnp.float32)
    finisher = normal_values(splits[15], (D, 2 * D), D ** -0.5, 0.1875, ((1, 8),), jnp.float32)
    readout = normal_values(splits[16], (D, PIN), D ** -0.5, 0.1875, (), jnp.float32)
    row_states = jnp.clip(jnp.exp(jax.random.uniform(splits[17], (NR,), jnp.float32, math.log(8.864946537262552e-13), math.log(3.545978614905021e-12))), 8.864946537262552e-13, 3.545978614905021e-12)
    column_states = jnp.clip(jnp.exp(jax.random.uniform(splits[18], (NC,), jnp.float32, math.log(8.864946537262552e-13), math.log(3.545978614905021e-12))), 8.864946537262552e-13, 3.545978614905021e-12)
    return dict(latents=latents, noise_draw=noise_draw, alpha_bar=alpha_bar, timesteps=timesteps, labels=labels, lengths=lengths, class_vectors=class_vectors, embedder=embedder, time_first=time_first, time_second=time_second, modulator=modulator, mixer_input=mixer_input, mixer_output=mixer_output, expander=expander, contractor=contractor, finisher=finisher, readout=readout, row_states=row_states, column_states=column_states)


@jax.custom_vjp
def low(v):
    return lax.optimization_barrier(v.astype(jnp.bfloat16)).astype(jnp.float32)

@jax.custom_vjp
def low_back(v):
    return v

def low_keep(v):
    return (low(v), None)

def low_pass(kept, grad):
    return (grad,)

def back_keep(v):
    return (v, None)

def back_low(kept, grad):
    return (low(grad),)
low.defvjp(low_keep, low_pass)
low_back.defvjp(back_keep, back_low)
highest = lax.Precision.HIGHEST
eps_norm = 1e-06
eps_factor = 1e-30
clip_limit = 0.005
state_decay = 0.5
step_rate = 1.5
neg_large = -1e+30

def matmul(operand, other_operand):
    return jnp.dot(operand, other_operand, precision=highest)

def rounded(values):
    return low(low_back(values))

def layer_norm(values):
    center = values - lax.optimization_barrier(jnp.mean(values, axis=-1, keepdims=True))
    return center * lax.rsqrt(lax.optimization_barrier(jnp.mean(center * center, axis=-1, keepdims=True)) + eps_norm)

def position_table(side, width):
    quarter = width // 4
    omega = jnp.exp(-math.log(10000.0) * jnp.arange(quarter, dtype=jnp.float32) / quarter)
    place = jnp.arange(side * side)
    column = (place % side).astype(jnp.float32)[:, None] * omega[None, :]
    row_angle = (place // side).astype(jnp.float32)[:, None] * omega[None, :]
    return jnp.concatenate([jnp.sin(column), jnp.cos(column), jnp.sin(row_angle), jnp.cos(row_angle)], axis=1)

def time_features(steps, width):
    half = width // 2
    freq = jnp.exp(-math.log(10000.0) * jnp.arange(half, dtype=jnp.float32) / half)
    angle = steps.astype(jnp.float32)[:, None] * freq[None, :]
    return jnp.concatenate([jnp.cos(angle), jnp.sin(angle)], axis=1)

def block_loss(weights, batch, class_table):
    embedder, time_first, time_second, modulator, mixer_input, mixer_output, expander, contractor, finisher, readout = weights
    latents, noise_draw, alpha_bar, timesteps, labels, lengths = batch
    images = latents.shape[0]
    patches = SIDE * SIDE
    root_keep = jnp.sqrt(alpha_bar)[:, None, None]
    root_noise = jnp.sqrt(1.0 - alpha_bar)[:, None, None]
    noisy = root_keep * latents + root_noise * noise_draw
    target = root_keep * noise_draw - root_noise * latents
    residual = low_back(matmul(low(noisy), low(embedder))) + position_table(SIDE, D)[None]
    hidden = jax.nn.silu(matmul(time_features(timesteps, FREQ), time_first))
    condition = matmul(hidden, time_second) + class_table[labels]
    signal = low(jax.nn.silu(condition))
    steering = rounded(matmul(signal, low(modulator))).reshape(images, 6, 1, D)
    final_steer = rounded(matmul(signal, low(finisher))).reshape(images, 2, 1, D)
    live = jnp.arange(patches)[None, :] < lengths[:, None]
    input_one = low(layer_norm(residual) * (1.0 + steering[:, 1]) + steering[:, 0])
    qkv_rows = rounded(matmul(input_one, low(mixer_input))).reshape(images, patches, HEADS, 3, HD)
    queries = qkv_rows[:, :, :, 0]
    key_part = qkv_rows[:, :, :, 1]
    value_part = qkv_rows[:, :, :, 2]
    scores = low_back(jnp.einsum('bqhe,bkhe->bhqk', queries, key_part, precision=highest) * HD ** (-0.5))
    scores = jnp.where(live[:, None, None, :], scores, neg_large)
    exponent = jnp.exp(scores - lax.optimization_barrier(jnp.max(scores, axis=-1, keepdims=True)))
    attend = exponent / lax.optimization_barrier(jnp.sum(exponent, axis=-1, keepdims=True))
    mixed_out = rounded(jnp.einsum('bhqk,bkhe->bqhe', low(attend), value_part, precision=highest)).reshape(images, patches, D)
    residual = residual + steering[:, 2] * low_back(matmul(mixed_out, low(mixer_output)))
    input_two = low(layer_norm(residual) * (1.0 + steering[:, 4]) + steering[:, 3])
    active = low(jax.nn.gelu(low_back(matmul(input_two, low(expander))), approximate=True))
    residual = residual + steering[:, 5] * low_back(matmul(active, low(contractor)))
    input_final = low(layer_norm(residual) * (1.0 + final_steer[:, 1]) + final_steer[:, 0])
    output = low_back(matmul(input_final, low(readout)))
    misfit = output - target
    return jnp.sum(jnp.where(live[:, :, None], misfit * misfit, 0.0))

def reference(latents, noise_draw, alpha_bar, timesteps, labels, lengths, class_vectors, embedder, time_first, time_second, modulator, mixer_input, mixer_output, expander, contractor, finisher, readout, row_states, column_states):
    weights = (embedder, time_first, time_second, modulator, mixer_input, mixer_output, expander, contractor, finisher, readout)
    class_table = class_vectors.astype(jnp.float32)
    group = IMG_DEV * N_MP
    blocks = latents.shape[0] // group
    batch = tuple((item.reshape((blocks, group) + item.shape[1:]) for item in (latents, noise_draw, alpha_bar, timesteps, labels, lengths)))
    loss_count = jnp.sum(lengths).astype(jnp.float32) * PIN

    def total_loss(*params):
        sums = lax.map(jax.checkpoint(lambda piece: block_loss(params, piece, class_table)), batch)
        summed = jnp.sum(sums)
        return (summed / loss_count, summed)
    loss_mean, pull, loss_sum = jax.vjp(total_loss, *weights, has_aux=True)
    gradients = pull(jnp.ones_like(loss_mean))
    grad_norm = jnp.sqrt(sum((jnp.sum(gradient * gradient) for gradient in gradients)))
    factor = clip_limit / jnp.maximum(grad_norm, clip_limit)
    next_list = []
    clipped_list = []
    row_list = []
    column_list = []
    row_at = 0
    column_at = 0
    for weight, gradient in zip(weights, gradients):
        many_rows, many_cols = weight.shape
        clipped = gradient * factor
        square = clipped * clipped
        row_next = state_decay * row_states[row_at:row_at + many_rows] + (1.0 - state_decay) * (lax.optimization_barrier(jnp.mean(square, axis=1)) + eps_factor)
        column_next = state_decay * column_states[column_at:column_at + many_cols] + (1.0 - state_decay) * (lax.optimization_barrier(jnp.mean(square, axis=0)) + eps_factor)
        row_at += many_rows
        column_at += many_cols
        update = clipped * lax.rsqrt(row_next[:, None] * column_next[None, :] / jnp.mean(row_next))
        update = update / jnp.maximum(1.0, jnp.sqrt(jnp.mean(update * update)))
        next_list.append(weight - step_rate / math.sqrt(many_rows) * update)
        clipped_list.append(clipped)
        row_list.append(row_next)
        column_list.append(column_next)
    return (loss_sum, loss_count, grad_norm, next_list[0], next_list[1], next_list[2], next_list[3], next_list[4], next_list[5], next_list[6], next_list[7], next_list[8], next_list[9], clipped_list[0], clipped_list[1], clipped_list[2], clipped_list[3], clipped_list[4], clipped_list[5], clipped_list[6], clipped_list[7], clipped_list[8], clipped_list[9], jnp.concatenate(row_list), jnp.concatenate(column_list))
```

```python
import math

import jax
import jax.numpy as jnp
from jax import lax
from jax.sharding import PartitionSpec as P

HD = 72
FREQ = 256
PIN = 16
SIDE = 16


eps_norm = 1e-06
eps_factor = 1e-30
clip_limit = 0.005
state_decay = 0.5
step_rate = 1.5
neg_large = -1e30
highest = lax.Precision.HIGHEST


def product(operand, other_operand):
    return jnp.dot(operand, other_operand, preferred_element_type=jnp.float32)


def product_right(operand, other_operand):
    return lax.dot_general(
        operand, other_operand, (((1,), (1,)), ((), ())), preferred_element_type=jnp.float32
    )


def product_left(operand, other_operand):
    return lax.dot_general(
        operand, other_operand, (((0,), (0,)), ((), ())), preferred_element_type=jnp.float32
    )


def layer_norm(values):
    center = values - jnp.mean(values, axis=-1, keepdims=True)
    return center * lax.rsqrt(jnp.mean(center * center, axis=-1, keepdims=True) + eps_norm)


def norm_back(values, upstream):
    center = values - jnp.mean(values, axis=-1, keepdims=True)
    inverse = lax.rsqrt(jnp.mean(center * center, axis=-1, keepdims=True) + eps_norm)
    normed = center * inverse
    return inverse * (
        upstream
        - jnp.mean(upstream, axis=-1, keepdims=True)
        - normed * jnp.mean(upstream * normed, axis=-1, keepdims=True)
    )


def position_table(side, width):
    quarter = width // 4
    omega = jnp.exp(-math.log(10000.0) * jnp.arange(quarter, dtype=jnp.float32) / quarter)
    place = jnp.arange(side * side)
    column = (place % side).astype(jnp.float32)[:, None] * omega[None, :]
    row_angle = (place // side).astype(jnp.float32)[:, None] * omega[None, :]
    return jnp.concatenate(
        [jnp.sin(column), jnp.cos(column), jnp.sin(row_angle), jnp.cos(row_angle)], axis=1
    )


def time_features(steps, width):
    half = width // 2
    freq = jnp.exp(-math.log(10000.0) * jnp.arange(half, dtype=jnp.float32) / half)
    angle = steps.astype(jnp.float32)[:, None] * freq[None, :]
    return jnp.concatenate([jnp.cos(angle), jnp.sin(angle)], axis=1)


def across(values, axes):
    return lax.all_gather(values, axes, axis=0, tiled=True)


def gather_weight(piece):
    return across(piece, ("dp", "mp"))


def reduce_weight(partial):
    piece = lax.psum_scatter(partial, ("dp", "mp"), scatter_dimension=0, tiled=True)
    return across(piece, "dp")


def body(
    latents,
    noise_draw,
    alpha_bar,
    timesteps,
    labels,
    lengths,
    class_vectors,
    embedder,
    time_first,
    time_second,
    modulator,
    mixer_input,
    mixer_output,
    expander,
    contractor,
    finisher,
    readout,
    row_states,
    column_states,
):
    copies = lax.axis_size("dp")
    groups = lax.axis_size("mp")
    copy = lax.axis_index("dp")
    member = lax.axis_index("mp")
    width = embedder.shape[1]
    patches = SIDE * SIDE
    images = latents.shape[0]
    rows = images * patches
    heads = width // HD
    heads_here = mixer_input.shape[1] // (3 * HD)
    hidden_here = expander.shape[1]
    valid_total = jnp.sum(lengths).astype(jnp.float32) * PIN
    own_lengths = lax.dynamic_slice_in_dim(lengths, (copy * groups + member) * images, images)
    own_alpha = lax.dynamic_slice_in_dim(alpha_bar, member * images, images)

    mixer_rows = (
        mixer_input.astype(jnp.bfloat16)
        .T.reshape(heads_here, 3, HD, width)
        .transpose(1, 0, 2, 3)
        .reshape(3 * heads_here * HD, width)
    )
    shards = (
        jnp.concatenate([mixer_rows, mixer_output.astype(jnp.bfloat16)], axis=0),
        expander.astype(jnp.bfloat16).T,
        contractor.astype(jnp.bfloat16),
    )
    gathered = []
    for shard in shards:
        piece_rows = shard.shape[0] // copies
        piece = lax.dynamic_slice_in_dim(shard, copy * piece_rows, piece_rows)
        gathered.append(gather_weight(piece))
    parts = copies // 4
    piece_rows = shards[0].shape[0] // copies
    mixer_all = (
        gathered[0]
        .reshape(4, parts, groups, piece_rows, width)
        .transpose(0, 2, 1, 3, 4)
        .reshape(4 * width, width)
    )
    inputs_use = mixer_all[: 3 * width]
    outputs_use = mixer_all[3 * width :]
    expand_use = gathered[1]
    contract_use = gathered[2]

    features = time_features(timesteps, FREQ)
    class_rows = jnp.take(class_vectors, labels, axis=0).astype(jnp.float32)
    hidden_pre = jnp.dot(features, time_first, precision=highest)
    condition = jnp.dot(jax.nn.silu(hidden_pre), time_second, precision=highest) + class_rows
    signal = jax.nn.silu(condition).astype(jnp.bfloat16)
    modulator_low = modulator.astype(jnp.bfloat16)
    finisher_low = finisher.astype(jnp.bfloat16)
    steer_part = product(signal, modulator_low).astype(jnp.bfloat16)
    final_part = product(signal, finisher_low).astype(jnp.bfloat16)
    steer_own = lax.all_to_all(steer_part, "mp", split_axis=0, concat_axis=1, tiled=True)
    final_own = lax.all_to_all(final_part, "mp", split_axis=0, concat_axis=1, tiled=True)
    steering = steer_own.astype(jnp.float32).reshape(images, 6, 1, width)
    final_steer = final_own.astype(jnp.float32).reshape(images, 2, 1, width)
    features_all = time_features(across(timesteps, "dp"), FREQ)
    hidden_pre_all = across(hidden_pre, "dp")
    condition_all = across(condition, "dp")
    signal_all = across(signal, "dp")

    embedder_low = embedder.astype(jnp.bfloat16)
    readout_low = readout.astype(jnp.bfloat16)
    place = jnp.arange(patches)
    live = place[None, :] < own_lengths[:, None]
    root_keep = jnp.sqrt(own_alpha)[:, None, None]
    root_noise = jnp.sqrt(1.0 - own_alpha)[:, None, None]
    noisy = (root_keep * latents + root_noise * noise_draw).astype(jnp.bfloat16).reshape(rows, PIN)
    target = (root_keep * noise_draw - root_noise * latents).reshape(rows, PIN)
    residual_zero = (
        product(noisy, embedder_low).reshape(images, patches, width)
        + position_table(SIDE, width)[None]
    )
    normed_one = layer_norm(residual_zero)
    input_one = (
        (normed_one * (1.0 + steering[:, 1]) + steering[:, 0])
        .astype(jnp.bfloat16)
        .reshape(rows, width)
    )
    qkv = product_right(input_one, inputs_use).astype(jnp.bfloat16)
    qkv = qkv.reshape(images, patches, 3, heads, HD)
    queries, key_part, value_part = qkv[:, :, 0], qkv[:, :, 1], qkv[:, :, 2]
    scores = (
        jnp.einsum("gqhe,gkhe->ghqk", queries, key_part, preferred_element_type=jnp.float32)
        * HD ** (-0.5)
    )
    scores = jnp.where(live[:, None, None, :], scores, neg_large)
    peak = jnp.max(scores, axis=-1, keepdims=True)
    exponent = jnp.exp(scores - peak)
    attend = exponent / jnp.sum(exponent, axis=-1, keepdims=True)
    mixed = jnp.einsum(
        "ghqk,gkhe->gqhe",
        attend.astype(jnp.bfloat16),
        value_part,
        preferred_element_type=jnp.float32,
    )
    mixed = mixed.astype(jnp.bfloat16).reshape(rows, width)
    branch_one = product(mixed, outputs_use).reshape(images, patches, width)
    residual_one = residual_zero + steering[:, 2] * branch_one
    normed_two = layer_norm(residual_one)
    input_two = (
        (normed_two * (1.0 + steering[:, 4]) + steering[:, 3])
        .astype(jnp.bfloat16)
        .reshape(rows, width)
    )
    pre_active = product_right(input_two, expand_use)
    active = jax.nn.gelu(pre_active, approximate=True).astype(jnp.bfloat16)
    branch_two = product(active, contract_use).reshape(images, patches, width)
    residual_two = residual_one + steering[:, 5] * branch_two
    normed_final = layer_norm(residual_two)
    input_final = (
        (normed_final * (1.0 + final_steer[:, 1]) + final_steer[:, 0])
        .astype(jnp.bfloat16)
        .reshape(rows, width)
    )
    misfit = product(input_final, readout_low) - target
    live_rows = live.reshape(rows, 1)
    loss_part = jnp.sum(jnp.where(live_rows, misfit * misfit, 0.0))

    output_grad = jnp.where(live_rows, 2.0 * misfit / valid_total, 0.0).astype(jnp.bfloat16)
    readout_part = product_left(input_final, output_grad)
    final_grad = product_right(output_grad, readout_low).reshape(images, patches, width)
    final_shift_grad = jnp.sum(final_grad, axis=1)
    final_scale_grad = jnp.sum(final_grad * normed_final, axis=1)
    grad_residual = norm_back(residual_two, final_grad * (1.0 + final_steer[:, 1]))
    gate_two_grad = jnp.sum(grad_residual * branch_two, axis=1)
    branch_two_grad = (steering[:, 5] * grad_residual).astype(jnp.bfloat16).reshape(rows, width)
    contract_part = product_left(active, branch_two_grad).astype(jnp.bfloat16)
    active_grad = product_right(branch_two_grad, contract_use)
    gelu_pull = jax.vjp(lambda inner: jax.nn.gelu(inner, approximate=True), pre_active)[1]
    pre_grad = gelu_pull(active_grad)[0].astype(jnp.bfloat16)
    expand_part = product_left(pre_grad, input_two).astype(jnp.bfloat16)
    input_two_grad = product(pre_grad, expand_use).reshape(images, patches, width)
    shift_two_grad = jnp.sum(input_two_grad, axis=1)
    scale_two_grad = jnp.sum(input_two_grad * normed_two, axis=1)
    grad_residual = grad_residual + norm_back(
        residual_one, input_two_grad * (1.0 + steering[:, 4])
    )
    gate_one_grad = jnp.sum(grad_residual * branch_one, axis=1)
    branch_one_grad = (steering[:, 2] * grad_residual).astype(jnp.bfloat16).reshape(rows, width)
    outputs_part = product_left(mixed, branch_one_grad).astype(jnp.bfloat16)
    mixed_grad = (
        product_right(branch_one_grad, outputs_use)
        .astype(jnp.bfloat16)
        .reshape(images, patches, heads, HD)
    )
    attend_grad = jnp.einsum(
        "gqhe,gkhe->ghqk", mixed_grad, value_part, preferred_element_type=jnp.float32
    )
    score_grad = (
        attend * (attend_grad - jnp.sum(attend * attend_grad, axis=-1, keepdims=True))
    ).astype(jnp.bfloat16)
    query_grad = (
        jnp.einsum("ghqk,gkhe->gqhe", score_grad, key_part, preferred_element_type=jnp.float32)
        * HD ** (-0.5)
    )
    key_grad = (
        jnp.einsum("ghqk,gqhe->gkhe", score_grad, queries, preferred_element_type=jnp.float32)
        * HD ** (-0.5)
    )
    value_grad = jnp.einsum(
        "ghqk,gqhe->gkhe",
        attend.astype(jnp.bfloat16),
        mixed_grad,
        preferred_element_type=jnp.float32,
    )
    qkv_grad = (
        jnp.stack([query_grad, key_grad, value_grad], axis=2)
        .astype(jnp.bfloat16)
        .reshape(rows, 3 * width)
    )
    inputs_part = product_left(qkv_grad, input_one).astype(jnp.bfloat16)
    input_one_grad = product(qkv_grad, inputs_use).reshape(images, patches, width)
    shift_one_grad = jnp.sum(input_one_grad, axis=1)
    scale_one_grad = jnp.sum(input_one_grad * normed_one, axis=1)
    grad_residual = grad_residual + norm_back(
        residual_zero, input_one_grad * (1.0 + steering[:, 1])
    )
    embed_part = product_left(noisy, grad_residual.reshape(rows, width).astype(jnp.bfloat16))

    mixer_part = jnp.concatenate([inputs_part, outputs_part], axis=0)
    mixer_part = (
        mixer_part.reshape(4, groups, parts, piece_rows, width)
        .transpose(0, 2, 1, 3, 4)
        .reshape(4 * width, width)
    )
    contract_sum = reduce_weight(contract_part).astype(jnp.float32)
    expand_sum = reduce_weight(expand_part).astype(jnp.float32).T
    mixer_sum = reduce_weight(mixer_part).astype(jnp.float32)
    held = heads_here * HD
    inputs_sum = (
        mixer_sum[: 3 * held]
        .reshape(3, heads_here, HD, width)
        .transpose(1, 0, 2, 3)
        .reshape(3 * held, width)
        .T
    )
    outputs_sum = mixer_sum[3 * held :]

    steer_back = jnp.stack(
        [
            shift_one_grad,
            scale_one_grad,
            gate_one_grad,
            shift_two_grad,
            scale_two_grad,
            gate_two_grad,
        ],
        axis=1,
    )
    steer_back = steer_back.reshape(images, 6 * width).astype(jnp.bfloat16)
    final_back = jnp.stack([final_shift_grad, final_scale_grad], axis=1)
    final_back = final_back.reshape(images, 2 * width).astype(jnp.bfloat16)
    steer_cols = lax.all_to_all(steer_back, "mp", split_axis=1, concat_axis=0, tiled=True)
    final_cols = lax.all_to_all(final_back, "mp", split_axis=1, concat_axis=0, tiled=True)
    signal_grad = product_right(steer_cols, modulator_low) + product_right(final_cols, finisher_low)
    signal_grad = across(lax.psum(signal_grad, "mp"), "dp")
    modulator_sum = product_left(signal_all, across(steer_cols, "dp"))
    finisher_sum = product_left(signal_all, across(final_cols, "dp"))
    hidden_all, hidden_pull = jax.vjp(jax.nn.silu, hidden_pre_all)
    condition_grad = jax.vjp(jax.nn.silu, condition_all)[1](signal_grad)[0]
    time_second_sum = lax.dot_general(
        hidden_all, condition_grad, (((0,), (0,)), ((), ())), precision=highest
    )
    hidden_grad = hidden_pull(
        lax.dot_general(condition_grad, time_second, (((1,), (1,)), ((), ())), precision=highest)
    )[0]
    time_first_sum = lax.dot_general(
        features_all, hidden_grad, (((0,), (0,)), ((), ())), precision=highest
    )
    embed_sum, readout_sum, loss_sum = lax.psum((embed_part, readout_part, loss_part), ("dp", "mp"))

    gradients = (
        embed_sum,
        time_first_sum,
        time_second_sum,
        modulator_sum,
        inputs_sum,
        outputs_sum,
        expand_sum,
        contract_sum,
        finisher_sum,
        readout_sum,
    )
    weights = (
        embedder,
        time_first,
        time_second,
        modulator,
        mixer_input,
        mixer_output,
        expander,
        contractor,
        finisher,
        readout,
    )
    layouts = (
        "whole",
        "whole",
        "whole",
        "columns",
        "columns",
        "rows",
        "columns",
        "rows",
        "columns",
        "whole",
    )
    row_squares = [jnp.sum(gradient * gradient, axis=1) for gradient in gradients]
    column_squares = [jnp.sum(gradient * gradient, axis=0) for gradient in gradients]
    split_slots = [slot for slot in range(10) if layouts[slot] != "whole"]
    local_square = sum(jnp.sum(row_squares[slot]) for slot in range(10) if slot not in split_slots)
    split_square = sum(jnp.sum(row_squares[slot]) for slot in split_slots)
    crossing = [
        row_squares[slot] if layouts[slot] == "columns" else column_squares[slot]
        for slot in split_slots
    ]
    lengths_out = [part.shape[0] for part in crossing]
    crossed = lax.psum(jnp.concatenate(crossing + [split_square[None]]), "mp")
    grad_norm = jnp.sqrt(crossed[-1] + local_square)
    factor = clip_limit / jnp.maximum(grad_norm, clip_limit)
    factor_square = factor * factor
    start = 0
    for slot, length in zip(split_slots, lengths_out):
        part = crossed[start : start + length]
        start += length
        if layouts[slot] == "columns":
            row_squares[slot] = part
        else:
            column_squares[slot] = part

    row_at = 0
    column_at = 0
    records = []
    for slot in range(10):
        layout = layouts[slot]
        local_rows, local_cols = weights[slot].shape
        many_rows = local_rows * (groups if layout == "rows" else 1)
        many_cols = local_cols * (groups if layout == "columns" else 1)
        row_mean = row_squares[slot] * factor_square / many_cols + eps_factor
        column_mean = column_squares[slot] * factor_square / many_rows + eps_factor
        row_start = row_at + (member * local_rows if layout == "rows" else 0)
        column_start = column_at + (member * local_cols if layout == "columns" else 0)
        row_old = lax.dynamic_slice_in_dim(row_states, row_start, local_rows)
        column_old = lax.dynamic_slice_in_dim(column_states, column_start, local_cols)
        row_next = state_decay * row_old + (1.0 - state_decay) * row_mean
        column_next = state_decay * column_old + (1.0 - state_decay) * column_mean
        if layout == "rows":
            row_average = state_decay * jnp.mean(row_states[row_at : row_at + many_rows]) + (
                1.0 - state_decay
            ) * jnp.mean(column_mean)
        else:
            row_average = jnp.mean(row_next)
        clipped = gradients[slot] * factor
        update = clipped * lax.rsqrt(row_next[:, None] * column_next[None, :] / row_average)
        records.append(
            (clipped, update, jnp.sum(update * update), row_next, column_next, many_rows, many_cols)
        )
        row_at += many_rows
        column_at += many_cols
    shares = [jnp.stack([records[slot][2] for slot in split_slots])]
    for slot in split_slots:
        shares.append(records[slot][4] if layouts[slot] == "columns" else records[slot][3])
    spread = lax.all_gather(jnp.concatenate(shares), "mp", axis=0)
    energies = jnp.sum(spread[:, : len(split_slots)], axis=0)
    start = len(split_slots)
    next_list = []
    row_list = []
    column_list = []
    for slot in range(10):
        clipped, update, energy, row_next, column_next, many_rows, many_cols = records[slot]
        if layouts[slot] != "whole":
            energy = energies[split_slots.index(slot)]
            length = column_next.shape[0] if layouts[slot] == "columns" else row_next.shape[0]
            joined = spread[:, start : start + length].reshape(-1)
            start += length
            if layouts[slot] == "columns":
                column_next = joined
            else:
                row_next = joined
        scale_down = jnp.maximum(1.0, jnp.sqrt(energy / (many_rows * many_cols)))
        next_list.append(weights[slot] - step_rate / math.sqrt(many_rows) * (update / scale_down))
        row_list.append(row_next)
        column_list.append(column_next)
    return (
        loss_sum,
        valid_total,
        grad_norm,
        *next_list,
        *[record[0] for record in records],
        jnp.concatenate(row_list),
        jnp.concatenate(column_list),
    )


def solution(mesh):
    in_specs = (
        P(("dp", "mp"), None, None),
        P(("dp", "mp"), None, None),
        P("dp"),
        P("dp"),
        P("dp"),
        P(),
        P(),
        P(),
        P(),
        P(),
        P(None, "mp"),
        P(None, "mp"),
        P("mp", None),
        P(None, "mp"),
        P("mp", None),
        P(None, "mp"),
        P(),
        P(),
        P(),
    )
    out_specs = (
        P(),
        P(),
        P(),
        P(),
        P(),
        P(),
        P(None, "mp"),
        P(None, "mp"),
        P("mp", None),
        P(None, "mp"),
        P("mp", None),
        P(None, "mp"),
        P(),
        P(),
        P(),
        P(),
        P(None, "mp"),
        P(None, "mp"),
        P("mp", None),
        P(None, "mp"),
        P("mp", None),
        P(None, "mp"),
        P(),
        P(),
        P(),
    )
    return jax.shard_map(body, mesh=mesh, in_specs=in_specs, out_specs=out_specs, check_vma=False)
```

```python
import functools
import math

import jax
import jax.numpy as jnp
from jax import lax
from jax.experimental import pallas as pl
from jax.experimental.pallas import tpu as pltpu
from jax.sharding import PartitionSpec as P

HD = 72
FREQ = 256
PIN = 16
SIDE = 16


eps_norm = 1e-06
eps_factor = 1e-30
clip_limit = 0.005
state_decay = 0.5
step_rate = 1.5
neg_large = -1e30
highest = lax.Precision.HIGHEST
MESH = pl.DeviceIdType.MESH


def product(operand, other_operand):
    return jnp.dot(operand, other_operand, preferred_element_type=jnp.float32)


def product_right(operand, other_operand):
    return lax.dot_general(
        operand, other_operand, (((1,), (1,)), ((), ())), preferred_element_type=jnp.float32
    )


def product_left(operand, other_operand):
    return lax.dot_general(
        operand, other_operand, (((0,), (0,)), ((), ())), preferred_element_type=jnp.float32
    )


def layer_norm(values):
    center = values - jnp.mean(values, axis=-1, keepdims=True)
    return center * lax.rsqrt(jnp.mean(center * center, axis=-1, keepdims=True) + eps_norm)


def norm_back(values, upstream):
    center = values - jnp.mean(values, axis=-1, keepdims=True)
    inverse = lax.rsqrt(jnp.mean(center * center, axis=-1, keepdims=True) + eps_norm)
    normed = center * inverse
    return inverse * (
        upstream
        - jnp.mean(upstream, axis=-1, keepdims=True)
        - normed * jnp.mean(upstream * normed, axis=-1, keepdims=True)
    )


def position_table(side, width):
    quarter = width // 4
    omega = jnp.exp(-math.log(10000.0) * jnp.arange(quarter, dtype=jnp.float32) / quarter)
    place = jnp.arange(side * side)
    column = (place % side).astype(jnp.float32)[:, None] * omega[None, :]
    row_angle = (place // side).astype(jnp.float32)[:, None] * omega[None, :]
    return jnp.concatenate(
        [jnp.sin(column), jnp.cos(column), jnp.sin(row_angle), jnp.cos(row_angle)], axis=1
    )


def time_features(steps, width):
    half = width // 2
    freq = jnp.exp(-math.log(10000.0) * jnp.arange(half, dtype=jnp.float32) / half)
    angle = steps.astype(jnp.float32)[:, None] * freq[None, :]
    return jnp.concatenate([jnp.cos(angle), jnp.sin(angle)], axis=1)


def peers(span):
    dp, mp = lax.axis_index("dp"), lax.axis_index("mp")
    copies, groups = lax.axis_size("dp"), lax.axis_size("mp")
    if span == "mp":
        return mp, groups, lambda place: (dp, place)
    if span == "dp":
        return dp, copies, lambda place: (place, mp)
    return dp * groups + mp, copies * groups, lambda place: (place // groups, lax.rem(place, groups))


def greet(span):
    here, size, device = peers(span)
    barrier = pltpu.get_barrier_semaphore()

    @pl.loop(1, size)
    def _(step):
        pl.semaphore_signal(
            barrier,
            inc=1,
            device_id=device(lax.rem(here + step, size)),
            device_id_type=MESH,
        )

    pl.semaphore_wait(barrier, size - 1)


def to_all(span, pick, landing, send_sems, recv_sems):
    here, size, device = peers(span)

    def copy(step):
        place = lax.rem(here + step, size)
        return pltpu.make_async_remote_copy(
            src_ref=pick(place),
            dst_ref=landing(here),
            send_sem=send_sems.at[step],
            recv_sem=recv_sems.at[step],
            device_id=device(place),
            device_id_type=MESH,
        )

    @pl.loop(1, size)
    def _(step):
        copy(step).start()

    def wait():
        @pl.loop(1, size)
        def _(step):
            copy(step).wait()

    return wait


def sum_over(ref):
    return lax.fori_loop(1, ref.shape[0], lambda index, total: total + ref[index], ref[0])


def swap_kernel(span, per_target, groups, x_ref, out_ref, send_sems, recv_sems):
    here, _, _ = peers(span)

    def pick(place):
        return x_ref.at[lax.rem(place, groups)] if per_target else x_ref

    greet(span)
    wait = to_all(span, pick, lambda place: out_ref.at[place], send_sems, recv_sems)
    out_ref[here] = x_ref[lax.rem(here, groups)] if per_target else x_ref[...]
    wait()


def total_kernel(span, x_ref, out_ref, land, send_sems, recv_sems):
    here, _, _ = peers(span)
    greet(span)
    wait = to_all(span, lambda place: x_ref, lambda place: land.at[place], send_sems, recv_sems)
    land[here] = x_ref[...]
    wait()
    out_ref[...] = sum_over(land)


def both_kernel(all_ref, mp_ref, all_out, mp_out, all_land, mp_land, send_sems, recv_sems):
    here, _, _ = peers("all")
    member, _, _ = peers("mp")
    greet("all")
    wait_all = to_all(
        "all",
        lambda place: all_ref.at[place],
        lambda place: all_land.at[place],
        send_sems.at[0],
        recv_sems.at[0],
    )
    wait_mp = to_all(
        "mp",
        lambda place: mp_ref.at[place],
        lambda place: mp_land.at[place],
        send_sems.at[1],
        recv_sems.at[1],
    )
    all_land[here] = all_ref[here]
    mp_land[member] = mp_ref[member]
    wait_mp()
    mp_out[here] = sum_over(mp_land)
    wait_mp = to_all(
        "all",
        lambda place: mp_out.at[here],
        lambda place: mp_out.at[place],
        send_sems.at[2],
        recv_sems.at[2],
    )
    wait_all()
    all_out[here] = sum_over(all_land)
    wait_all = to_all(
        "all",
        lambda place: all_out.at[here],
        lambda place: all_out.at[place],
        send_sems.at[3],
        recv_sems.at[3],
    )
    wait_mp()
    wait_all()


def group_size(span):
    sizes = {"dp": lax.axis_size("dp"), "mp": lax.axis_size("mp")}
    return sizes.get(span, sizes["dp"] * sizes["mp"])


def call(kernel, inputs, out_shapes, scratch, collective_id):
    return pl.pallas_call(
        kernel,
        out_shape=[jax.ShapeDtypeStruct(shape, jnp.float32) for shape in out_shapes],
        in_specs=[pl.BlockSpec(memory_space=pltpu.VMEM)] * len(inputs),
        out_specs=[pl.BlockSpec(memory_space=pltpu.VMEM)] * len(out_shapes),
        scratch_shapes=scratch,
        compiler_params=pltpu.CompilerParams(
            collective_id=collective_id, has_side_effects=True, vmem_limit_bytes=32 * 1024 * 1024
        ),
    )(*inputs)


def swap(values, span, collective_id, per_target=True):
    size = group_size(span)
    slab = values.shape[-2:]
    (result,) = call(
        functools.partial(swap_kernel, span, per_target, lax.axis_size("mp")),
        [values],
        [(size,) + slab],
        [pltpu.SemaphoreType.DMA((size,)), pltpu.SemaphoreType.DMA((size,))],
        collective_id,
    )
    return result


def total(values, span, collective_id):
    size = group_size(span)
    (result,) = call(
        functools.partial(total_kernel, span),
        [values],
        [values.shape],
        [
            pltpu.VMEM((size,) + values.shape, jnp.float32),
            pltpu.SemaphoreType.DMA((size,)),
            pltpu.SemaphoreType.DMA((size,)),
        ],
        collective_id,
    )
    return result


def both_totals(for_all, for_mp, collective_id):
    size = group_size("all")
    return call(
        both_kernel,
        [for_all, for_mp],
        [for_all.shape, (size,) + for_mp.shape[1:]],
        [
            pltpu.VMEM(for_all.shape, jnp.float32),
            pltpu.VMEM(for_mp.shape, jnp.float32),
            pltpu.SemaphoreType.DMA((4, size)),
            pltpu.SemaphoreType.DMA((4, size)),
        ],
        collective_id,
    )


def slabs(flat, blocks):
    chunk = 1024 * blocks
    short = (-flat.shape[0]) % chunk
    return jnp.pad(flat, (0, short)).reshape(blocks, -1, 128)


def reduce_kernel(counts, *refs):
    copies, groups = counts
    lines = {"a": 4, "b": groups // 4, "y": copies // 2}
    chunks = (len(refs) - 8) // 2
    parts = refs[:chunks]
    outs = refs[chunks : 2 * chunks]
    held, twin, first_b, first_y, second, third, send_sems, recv_sems = refs[2 * chunks :]
    splits = parts[0].shape[4]
    dp, mp = lax.axis_index("dp"), lax.axis_index("mp")
    at = {"a": mp // lines["b"], "b": lax.rem(mp, lines["b"]), "y": dp // 2}
    core = lax.rem(dp, 2)

    def device(**moved):
        place = {**at, "core": core, **moved}
        return (place["y"] * 2 + place["core"], place["a"] * lines["b"] + place["b"])

    barrier = pltpu.get_barrier_semaphore()
    pl.semaphore_signal(barrier, inc=1, device_id=device(core=1 - core), device_id_type=MESH)
    for axis, size in lines.items():
        for step in range(1, size):
            if axis != "y" and step not in (1, size - 1):
                continue
            other = lax.rem(at[axis] + step, size)
            pl.semaphore_signal(
                barrier, inc=1, device_id=device(**{axis: other}), device_id_type=MESH
            )
    total = 1 + sum(
        (size - 1) if axis == "y" else len({1, size - 1} - {0}) for axis, size in lines.items()
    )
    pl.semaphore_wait(barrier, total)

    units = [(chunk, split) for chunk in range(chunks) for split in range(splits)]
    slots = {}

    def sems(unit, name):
        slot = slots.setdefault(name, len(slots))
        return send_sems.at[unit, slot], recv_sems.at[unit, slot]

    def add_into(target, source):
        @pl.loop(0, target.shape[0])
        def _(index):
            target[index] = target[index] + source[index]

    def twin_copy(unit):
        chunk, split = units[unit]
        send, recv = sems(unit, "twin")
        return pltpu.make_async_remote_copy(
            src_ref=parts[chunk].at[:, 1 - core, :, :, split],
            dst_ref=twin.at[unit],
            send_sem=send,
            recv_sem=recv,
            device_id=device(core=1 - core),
            device_id_type=MESH,
        )

    def held_copy(unit):
        chunk, split = units[unit]
        return pltpu.make_async_copy(
            parts[chunk].at[:, core, :, :, split], held.at[unit], sems(unit, "held")[1]
        )

    def line_steps(unit, axis, name, pick, landing):
        size, here = lines[axis], at[axis]
        tasks = []

        def slot_of(up, hop):
            return 0 if size == 2 else hop - 1 + (size - 1 if up else 0)

        def copy(up, hop):
            target = here + hop if up else here - hop
            send, recv = sems(unit, (name, up, hop))
            slot = slot_of(up, hop)
            safe = lax.rem(target + size, size)
            beside = here + 1 if up else here - 1
            beside = lax.rem(beside + size, size)
            return pltpu.make_async_remote_copy(
                src_ref=pick(safe),
                dst_ref=landing(slot),
                send_sem=send,
                recv_sem=recv,
                device_id=device(**{axis: beside}),
                device_id_type=MESH,
            )

        def sends(up, hop):
            return here + hop <= size - 1 if up else here - hop >= 0

        def arrives(up, hop):
            if up:
                return (here >= 1) & (here + hop - 1 <= size - 1)
            return (here <= size - 2) & (here - hop + 1 >= 0)

        def take(up, hop):
            @pl.when(arrives(up, hop))
            def _():
                copy(up, hop).wait_recv()
                slot = slot_of(up, hop)
                target = here + hop - 1 if up else here - hop + 1
                add_into(pick(lax.rem(target + size, size)), landing(slot))

        def give(up, hop):
            @pl.when(sends(up, hop))
            def _():
                copy(up, hop).start()

        def finish(up, hop):
            @pl.when(sends(up, hop))
            def _():
                copy(up, hop).wait_send()

        for hop in range(size - 1, 0, -1):

            def begin(hop=hop):
                for up in (True, False):
                    if hop < size - 1:
                        take(up, hop + 1)
                    give(up, hop)

            tasks.append(begin)

        def close():
            for up in (True, False):
                take(up, 1)

        def drain():
            for hop in range(1, size):
                for up in (True, False):
                    finish(up, hop)

        return tasks, close, drain

    def unit_tasks(unit):
        chunk, split = units[unit]
        block = held.at[unit]
        halves = []
        drains = []
        for half, order in ((0, ("b", "y")), (1, ("y", "b"))):
            rows_a = pl.ds(2 * half, 2)

            def pick_one(target, axis=order[0], rows_a=rows_a):
                if axis == "b":
                    return block.at[:, rows_a, target]
                return block.at[target, rows_a]

            def pick_two(target, axis=order[1], rows_a=rows_a):
                if axis == "b":
                    return block.at[at["y"], rows_a, target]
                return block.at[target, rows_a, at["b"]]

            one = line_steps(
                unit,
                order[0],
                ("one", half),
                pick_one,
                lambda slot, axis=order[0]: (first_b if axis == "b" else first_y).at[unit, slot],
            )
            two = line_steps(
                unit,
                order[1],
                ("two", half),
                pick_two,
                lambda slot, half=half: second.at[unit, half, slot],
            )
            steps = list(one[0])
            joined = two[0][0]

            def pass_on(close=one[1], go=joined):
                close()
                go()

            steps += [pass_on] + list(two[0][1:])
            halves.append((steps, two[1]))
            drains += [one[2], two[2]]
        last = line_steps(
            unit,
            "a",
            "last",
            lambda target: block.at[at["y"], target, pl.ds(at["b"], 1)],
            lambda slot: third.at[unit, slot],
        )
        drains.append(last[2])
        out = outs[chunk]

        def spread_copy(owner, to):
            send, recv = sems(unit, ("spread", owner[2], to[2]))
            return pltpu.make_async_remote_copy(
                src_ref=out.at[owner[0], owner[1], split],
                dst_ref=out.at[owner[0], owner[1], split],
                send_sem=send,
                recv_sem=recv,
                device_id=device(y=to[0], core=to[1]),
                device_id_type=MESH,
            )

        size_y = lines["y"]
        me = (at["y"], core, 0)
        twin_place = (at["y"], 1 - core, "twin")

        def far(step):
            return (lax.rem(at["y"] + step, size_y), core, step)

        def start():
            held_copy(unit).wait()
            twin_copy(unit).wait_recv()

            @pl.loop(0, block.shape[0])
            def _(row):
                @pl.loop(0, block.shape[1])
                def _(group):
                    block[row, group] = block[row, group] + twin[unit, row, group]

            for steps, _ in halves:
                steps[0]()

        tasks = [start]
        for index in range(1, len(halves[0][0])):

            def middle(index=index):
                for steps, _ in halves:
                    steps[index]()

            tasks.append(middle)

        def to_last():
            for _, close in halves:
                close()
            last[0][0]()

        tasks.append(to_last)
        tasks += list(last[0][1:])

        def sum_done():
            last[1]()
            out[at["y"], core, split] = block[at["y"], at["a"], at["b"]]
            for step in range(1, size_y):
                spread_copy(me, far(step)).start()
            spread_copy(me, twin_place).start()

        tasks.append(sum_done)

        def before(step):
            return (lax.rem(at["y"] + size_y - step, size_y), core, step)

        def forward():
            for step in range(1, size_y):
                spread_copy((at["y"], core, 0), far(step)).wait_recv()
                source = before(step)
                spread_copy(source, twin_place).start()

        tasks.append(forward)

        def end():
            spread_copy(me, twin_place).wait()
            for step in range(1, size_y):
                spread_copy(before(step), twin_place).wait()
                spread_copy(me, far(step)).wait_send()
            twin_copy(unit).wait_send()
            for drain in drains:
                drain()

        tasks.append(end)
        return tasks

    for unit in range(len(units)):
        twin_copy(unit).start()
        held_copy(unit).start()
    queues = [unit_tasks(unit) for unit in range(len(units))]
    depth = len(queues[0])
    for tick in range(len(units) + depth - 1):
        for unit in reversed(range(len(units))):
            task = tick - unit
            if 0 <= task < depth:
                queues[unit][task]()


def reduce_weights(partials, collective_id):
    copies, groups = lax.axis_size("dp"), lax.axis_size("mp")
    rows, width = partials[0].shape
    size_b, size_y = groups // 4, copies // 2
    piece = rows // (copies * groups)
    share = 48 if piece % 48 == 0 else piece
    splits = piece // share
    shaped = [
        part.reshape(size_y, 2, 4, size_b, splits, share, width) for part in partials
    ]
    units = splits * len(partials)
    slab = (share, width)
    slots_b = 1 if size_b == 2 else 2 * (size_b - 1)
    slots_y = 1 if size_y == 2 else 2 * (size_y - 1)
    scratch = [
        pltpu.VMEM((units, size_y, 4, size_b) + slab, jnp.bfloat16),
        pltpu.VMEM((units, size_y, 4, size_b) + slab, jnp.bfloat16),
        pltpu.VMEM((units, slots_b, size_y, 2) + slab, jnp.bfloat16),
        pltpu.VMEM((units, slots_y, 2, size_b) + slab, jnp.bfloat16),
        pltpu.VMEM((units, 2, max(slots_b, slots_y), 2) + slab, jnp.bfloat16),
        pltpu.VMEM((units, 6, 1) + slab, jnp.bfloat16),
        pltpu.SemaphoreType.DMA((units, 40)),
        pltpu.SemaphoreType.DMA((units, 40)),
    ]
    results = pl.pallas_call(
        functools.partial(reduce_kernel, (copies, groups)),
        out_shape=[jax.ShapeDtypeStruct((size_y, 2, splits) + slab, jnp.bfloat16)] * len(partials),
        in_specs=[pl.BlockSpec(memory_space=pl.ANY)] * len(partials),
        out_specs=[pl.BlockSpec(memory_space=pltpu.VMEM)] * len(partials),
        scratch_shapes=scratch,
        compiler_params=pltpu.CompilerParams(
            collective_id=collective_id, has_side_effects=True, vmem_limit_bytes=60 * 1024 * 1024
        ),
    )(*shaped)
    return [result.reshape(copies * piece, width) for result in results]


def weights_of(keys, queries, live):
    scores = product_left(keys, queries) * HD ** (-0.5)
    scores = jnp.where(live, scores, neg_large)
    exponent = jnp.exp(scores - jnp.max(scores, axis=0, keepdims=True))
    return exponent / jnp.sum(exponent, axis=0, keepdims=True)


def attend_kernel(length_ref, q_ref, k_ref, v_ref, out_ref):
    patches = q_ref.shape[1]
    pair = 2 * HD
    live = lax.broadcasted_iota(jnp.int32, (patches, patches), 0) < length_ref[pl.program_id(0)]
    upper = lax.broadcasted_iota(jnp.int32, (pair, patches), 0) < HD

    @pl.loop(0, q_ref.shape[0] // pair)
    def _(index):
        rows = pl.ds(pl.multiple_of(index * pair, 16), pair)
        queries, keys, values = q_ref[rows, :], k_ref[rows, :], v_ref[rows, :]
        zero = jnp.zeros_like(queries)
        mixed = []
        for half in range(2):
            own = upper if half == 0 else ~upper
            probs = weights_of(keys, jnp.where(own, queries, zero), live)
            mixed.append(product(values, probs.astype(jnp.bfloat16)))
        out_ref[rows, :] = jnp.where(upper, mixed[0], mixed[1]).astype(jnp.bfloat16)


def attend_back_kernel(length_ref, q_ref, k_ref, v_ref, up_ref, down_ref):
    patches = q_ref.shape[1]
    pair = 2 * HD
    live = lax.broadcasted_iota(jnp.int32, (patches, patches), 0) < length_ref[pl.program_id(0)]
    upper = lax.broadcasted_iota(jnp.int32, (pair, patches), 0) < HD

    @pl.loop(0, q_ref.shape[0] // pair)
    def _(index):
        rows = pl.ds(pl.multiple_of(index * pair, 16), pair)
        queries, keys, values, upstream = (
            q_ref[rows, :],
            k_ref[rows, :],
            v_ref[rows, :],
            up_ref[rows, :],
        )
        zero = jnp.zeros_like(queries)
        found = []
        for half in range(2):
            own = upper if half == 0 else ~upper
            probs = weights_of(keys, jnp.where(own, queries, zero), live)
            probs_grad = product_left(values, jnp.where(own, upstream, zero))
            weighted = probs * probs_grad
            score_grad = (
                weighted - probs * jnp.sum(weighted, axis=0, keepdims=True)
            ).astype(jnp.bfloat16)
            found.append(
                (
                    product(keys, score_grad),
                    product_right(queries, score_grad),
                    product_right(upstream, probs.astype(jnp.bfloat16)),
                )
            )
        scale = HD ** (-0.5)
        down_ref[0, rows, :] = (jnp.where(upper, found[0][0], found[1][0]) * scale).astype(jnp.bfloat16)
        down_ref[1, rows, :] = (jnp.where(upper, found[0][1], found[1][1]) * scale).astype(jnp.bfloat16)
        down_ref[2, rows, :] = jnp.where(upper, found[0][2], found[1][2]).astype(jnp.bfloat16)


def _specs(width, patches):
    def spec(block):
        return pl.BlockSpec((width, patches), lambda image, lengths: (block, image))

    return spec


def attend(qkv, lengths, images):
    width, rows = qkv.shape[0] // 3, qkv.shape[1]
    patches = rows // images
    spec = _specs(width, patches)
    return pl.pallas_call(
        attend_kernel,
        grid_spec=pltpu.PrefetchScalarGridSpec(
            num_scalar_prefetch=1,
            grid=(images,),
            in_specs=[spec(0), spec(1), spec(2)],
            out_specs=spec(0),
        ),
        out_shape=jax.ShapeDtypeStruct((width, rows), jnp.bfloat16),
        compiler_params=pltpu.CompilerParams(vmem_limit_bytes=48 * 1024 * 1024),
        cost_estimate=pl.CostEstimate(flops=4 * rows * patches * width, bytes_accessed=8 * rows * width, transcendentals=0),
    )(lengths, qkv, qkv, qkv)


def attend_back(qkv, upstream, lengths, images):
    width, rows = upstream.shape
    patches = rows // images
    spec = _specs(width, patches)
    return pl.pallas_call(
        attend_back_kernel,
        grid_spec=pltpu.PrefetchScalarGridSpec(
            num_scalar_prefetch=1,
            grid=(images,),
            in_specs=[spec(0), spec(1), spec(2), spec(0)],
            out_specs=pl.BlockSpec((3, width, patches), lambda image, lengths: (0, 0, image)),
        ),
        out_shape=jax.ShapeDtypeStruct((3, width, rows), jnp.bfloat16),
        compiler_params=pltpu.CompilerParams(vmem_limit_bytes=48 * 1024 * 1024),
        cost_estimate=pl.CostEstimate(flops=10 * rows * patches * width, bytes_accessed=14 * rows * width, transcendentals=0),
    )(lengths, qkv, qkv, qkv, upstream).reshape(3 * width, rows)


def across(values, axes):
    return lax.all_gather(values, axes, axis=0, tiled=True)


def gather_weight(piece):
    return across(piece, ("dp", "mp"))


def reduce_weight(partial):
    piece = lax.psum_scatter(partial, ("dp", "mp"), scatter_dimension=0, tiled=True)
    return across(piece, "dp")


def body(
    latents,
    noise_draw,
    alpha_bar,
    timesteps,
    labels,
    lengths,
    class_vectors,
    embedder,
    time_first,
    time_second,
    modulator,
    mixer_input,
    mixer_output,
    expander,
    contractor,
    finisher,
    readout,
    row_states,
    column_states,
):
    copies = lax.axis_size("dp")
    groups = lax.axis_size("mp")
    copy = lax.axis_index("dp")
    member = lax.axis_index("mp")
    width = embedder.shape[1]
    patches = SIDE * SIDE
    images = latents.shape[0]
    rows = images * patches
    heads = width // HD
    heads_here = mixer_input.shape[1] // (3 * HD)
    hidden_here = expander.shape[1]
    valid_total = jnp.sum(lengths).astype(jnp.float32) * PIN
    own_lengths = lax.dynamic_slice_in_dim(lengths, (copy * groups + member) * images, images)
    own_alpha = lax.dynamic_slice_in_dim(alpha_bar, member * images, images)

    mixer_rows = (
        mixer_input.astype(jnp.bfloat16)
        .T.reshape(heads_here, 3, HD, width)
        .transpose(1, 0, 2, 3)
        .reshape(3 * heads_here * HD, width)
    )
    shards = (
        jnp.concatenate([mixer_rows, mixer_output.astype(jnp.bfloat16)], axis=0),
        expander.astype(jnp.bfloat16).T,
        contractor.astype(jnp.bfloat16),
    )
    gathered = []
    for shard in shards:
        piece_rows = shard.shape[0] // copies
        piece = lax.dynamic_slice_in_dim(shard, copy * piece_rows, piece_rows)
        gathered.append(gather_weight(piece))
    parts = copies // 4
    piece_rows = shards[0].shape[0] // copies
    mixer_all = (
        gathered[0]
        .reshape(4, parts, groups, piece_rows, width)
        .transpose(0, 2, 1, 3, 4)
        .reshape(4 * width, width)
    )
    inputs_use = mixer_all[: 3 * width]
    outputs_use = mixer_all[3 * width :]
    expand_use = gathered[1]
    contract_use = gathered[2]

    group_images = groups * images
    asked = jnp.stack([timesteps, labels]).astype(jnp.float32)
    asked = jnp.pad(asked, ((0, 6), (0, 128 - group_images)))
    asked = swap(asked, "dp", 1, per_target=False)[:, :2, :group_images]
    steps_all, labels_all = asked.transpose(1, 0, 2).reshape(2, copies * group_images).astype(jnp.int32)
    features = time_features(steps_all, FREQ)
    class_rows = jnp.take(class_vectors, labels_all, axis=0).astype(jnp.float32)
    hidden_pre = jnp.dot(features, time_first, precision=highest)
    condition = jnp.dot(jax.nn.silu(hidden_pre), time_second, precision=highest) + class_rows
    signal_all = jax.nn.silu(condition).astype(jnp.bfloat16)
    signal = lax.dynamic_slice_in_dim(signal_all, copy * group_images, group_images)
    modulator_low = modulator.astype(jnp.bfloat16)
    finisher_low = finisher.astype(jnp.bfloat16)
    steer_here, final_here = modulator.shape[1], finisher.shape[1]
    mods_part = jnp.concatenate(
        [product(signal, modulator_low), product(signal, finisher_low)], axis=1
    )
    mods_part = mods_part.astype(jnp.bfloat16).astype(jnp.float32)
    mods_own = swap(mods_part.reshape(groups, -1, 128), "mp", 2)
    mods_own = mods_own.reshape(groups, images, steer_here + final_here).transpose(1, 0, 2)
    steering = mods_own[:, :, :steer_here].reshape(images, 6, 1, width)
    final_steer = mods_own[:, :, steer_here:].reshape(images, 2, 1, width)

    embedder_low = embedder.astype(jnp.bfloat16)
    readout_low = readout.astype(jnp.bfloat16)
    place = jnp.arange(patches)
    live = place[None, :] < own_lengths[:, None]
    root_keep = jnp.sqrt(own_alpha)[:, None, None]
    root_noise = jnp.sqrt(1.0 - own_alpha)[:, None, None]
    noisy = (root_keep * latents + root_noise * noise_draw).astype(jnp.bfloat16).reshape(rows, PIN)
    target = (root_keep * noise_draw - root_noise * latents).reshape(rows, PIN)
    residual_zero = (
        product(noisy, embedder_low).reshape(images, patches, width)
        + position_table(SIDE, width)[None]
    )
    normed_one = layer_norm(residual_zero)
    input_one = (
        (normed_one * (1.0 + steering[:, 1]) + steering[:, 0])
        .astype(jnp.bfloat16)
        .reshape(rows, width)
    )
    qkv = product_right(inputs_use, input_one).astype(jnp.bfloat16)
    mixed = attend(qkv, own_lengths, images)
    branch_one = product_left(mixed, outputs_use).reshape(images, patches, width)
    residual_one = residual_zero + steering[:, 2] * branch_one
    normed_two = layer_norm(residual_one)
    input_two = (
        (normed_two * (1.0 + steering[:, 4]) + steering[:, 3])
        .astype(jnp.bfloat16)
        .reshape(rows, width)
    )
    pre_active = product_right(input_two, expand_use)
    active = jax.nn.gelu(pre_active, approximate=True).astype(jnp.bfloat16)
    branch_two = product(active, contract_use).reshape(images, patches, width)
    residual_two = residual_one + steering[:, 5] * branch_two
    normed_final = layer_norm(residual_two)
    input_final = (
        (normed_final * (1.0 + final_steer[:, 1]) + final_steer[:, 0])
        .astype(jnp.bfloat16)
        .reshape(rows, width)
    )
    misfit = product(input_final, readout_low) - target
    live_rows = live.reshape(rows, 1)
    loss_part = jnp.sum(jnp.where(live_rows, misfit * misfit, 0.0))

    output_grad = jnp.where(live_rows, 2.0 * misfit / valid_total, 0.0).astype(jnp.bfloat16)
    readout_part = product_left(input_final, output_grad)
    final_grad = product_right(output_grad, readout_low).reshape(images, patches, width)
    final_shift_grad = jnp.sum(final_grad, axis=1)
    final_scale_grad = jnp.sum(final_grad * normed_final, axis=1)
    grad_residual = norm_back(residual_two, final_grad * (1.0 + final_steer[:, 1]))
    gate_two_grad = jnp.sum(grad_residual * branch_two, axis=1)
    branch_two_grad = (steering[:, 5] * grad_residual).astype(jnp.bfloat16).reshape(rows, width)
    contract_part = product_left(active, branch_two_grad).astype(jnp.bfloat16)
    active_grad = product_right(branch_two_grad, contract_use)
    gelu_pull = jax.vjp(lambda inner: jax.nn.gelu(inner, approximate=True), pre_active)[1]
    pre_grad = gelu_pull(active_grad)[0].astype(jnp.bfloat16)
    expand_part = product_left(pre_grad, input_two).astype(jnp.bfloat16)
    input_two_grad = product(pre_grad, expand_use).reshape(images, patches, width)
    shift_two_grad = jnp.sum(input_two_grad, axis=1)
    scale_two_grad = jnp.sum(input_two_grad * normed_two, axis=1)
    grad_residual = grad_residual + norm_back(
        residual_one, input_two_grad * (1.0 + steering[:, 4])
    )
    gate_one_grad = jnp.sum(grad_residual * branch_one, axis=1)
    branch_one_grad = (steering[:, 2] * grad_residual).astype(jnp.bfloat16).reshape(rows, width)
    outputs_part = product(mixed, branch_one_grad).astype(jnp.bfloat16)
    mixed_grad = product_right(outputs_use, branch_one_grad).astype(jnp.bfloat16)
    qkv_grad = attend_back(qkv, mixed_grad, own_lengths, images)
    inputs_part = product(qkv_grad, input_one).astype(jnp.bfloat16)
    input_one_grad = product_left(qkv_grad, inputs_use).reshape(images, patches, width)
    shift_one_grad = jnp.sum(input_one_grad, axis=1)
    scale_one_grad = jnp.sum(input_one_grad * normed_one, axis=1)
    grad_residual = grad_residual + norm_back(
        residual_zero, input_one_grad * (1.0 + steering[:, 1])
    )
    embed_part = product_left(noisy, grad_residual.reshape(rows, width).astype(jnp.bfloat16))

    mixer_part = jnp.concatenate([inputs_part, outputs_part], axis=0)
    mixer_part = (
        mixer_part.reshape(4, groups, parts, piece_rows, width)
        .transpose(0, 2, 1, 3, 4)
        .reshape(4 * width, width)
    )
    contract_sum = reduce_weight(contract_part).astype(jnp.float32)
    expand_sum, mixer_sum = reduce_weights([expand_part, mixer_part], 3)
    expand_sum = expand_sum.astype(jnp.float32).T
    mixer_sum = mixer_sum.astype(jnp.float32)
    held = heads_here * HD
    inputs_sum = (
        mixer_sum[: 3 * held]
        .reshape(3, heads_here, HD, width)
        .transpose(1, 0, 2, 3)
        .reshape(3 * held, width)
        .T
    )
    outputs_sum = mixer_sum[3 * held :]

    steer_back = jnp.stack(
        [
            shift_one_grad,
            scale_one_grad,
            gate_one_grad,
            shift_two_grad,
            scale_two_grad,
            gate_two_grad,
        ],
        axis=1,
    )
    steer_back = steer_back.reshape(images, 6 * width).astype(jnp.bfloat16)
    final_back = jnp.stack([final_shift_grad, final_scale_grad], axis=1)
    final_back = final_back.reshape(images, 2 * width).astype(jnp.bfloat16)
    back = jnp.concatenate(
        [
            steer_back.reshape(images, groups, steer_here),
            final_back.reshape(images, groups, final_here),
        ],
        axis=2,
    )
    back = back.transpose(1, 0, 2).astype(jnp.float32).reshape(groups, -1, 128)
    cols_all = swap(back, "all", 4).astype(jnp.bfloat16)
    cols_all = cols_all.reshape(copies * group_images, steer_here + final_here)
    cols = lax.dynamic_slice_in_dim(cols_all, copy * group_images, group_images)
    signal_grad = product_right(cols[:, :steer_here], modulator_low) + product_right(
        cols[:, steer_here:], finisher_low
    )
    shared = slabs(
        jnp.concatenate([embed_part.reshape(-1), readout_part.reshape(-1), loss_part[None]]),
        copies * groups,
    )
    shared, signal_grad = both_totals(shared, signal_grad.reshape(groups, -1, 128), 5)
    shared = shared.reshape(-1)
    embed_sum = shared[: embedder.size].reshape(embedder.shape)
    readout_sum = shared[embedder.size : embedder.size + readout.size].reshape(readout.shape)
    loss_sum = shared[embedder.size + readout.size]
    signal_grad = signal_grad.reshape(copies * group_images, width)
    modulator_sum = product_left(signal_all, cols_all[:, :steer_here])
    finisher_sum = product_left(signal_all, cols_all[:, steer_here:])
    hidden, hidden_pull = jax.vjp(jax.nn.silu, hidden_pre)
    condition_grad = jax.vjp(jax.nn.silu, condition)[1](signal_grad)[0]
    time_second_sum = lax.dot_general(
        hidden, condition_grad, (((0,), (0,)), ((), ())), precision=highest
    )
    hidden_grad = hidden_pull(
        lax.dot_general(condition_grad, time_second, (((1,), (1,)), ((), ())), precision=highest)
    )[0]
    time_first_sum = lax.dot_general(
        features, hidden_grad, (((0,), (0,)), ((), ())), precision=highest
    )

    gradients = (
        embed_sum,
        time_first_sum,
        time_second_sum,
        modulator_sum,
        inputs_sum,
        outputs_sum,
        expand_sum,
        contract_sum,
        finisher_sum,
        readout_sum,
    )
    weights = (
        embedder,
        time_first,
        time_second,
        modulator,
        mixer_input,
        mixer_output,
        expander,
        contractor,
        finisher,
        readout,
    )
    layouts = (
        "whole",
        "whole",
        "whole",
        "columns",
        "columns",
        "rows",
        "columns",
        "rows",
        "columns",
        "whole",
    )
    row_squares = [jnp.sum(gradient * gradient, axis=1) for gradient in gradients]
    column_squares = [jnp.sum(gradient * gradient, axis=0) for gradient in gradients]
    split_slots = [slot for slot in range(10) if layouts[slot] != "whole"]
    local_square = sum(jnp.sum(row_squares[slot]) for slot in range(10) if slot not in split_slots)
    split_square = sum(jnp.sum(row_squares[slot]) for slot in split_slots)
    crossing = [
        row_squares[slot] if layouts[slot] == "columns" else column_squares[slot]
        for slot in split_slots
    ]
    lengths_out = [part.shape[0] for part in crossing]
    crossing = jnp.concatenate(crossing + [split_square[None]])
    crossed = total(slabs(crossing, 1)[0], "mp", 6).reshape(-1)
    grad_norm = jnp.sqrt(crossed[crossing.shape[0] - 1] + local_square)
    factor = clip_limit / jnp.maximum(grad_norm, clip_limit)
    factor_square = factor * factor
    start = 0
    for slot, length in zip(split_slots, lengths_out):
        part = crossed[start : start + length]
        start += length
        if layouts[slot] == "columns":
            row_squares[slot] = part
        else:
            column_squares[slot] = part

    row_at = 0
    column_at = 0
    records = []
    for slot in range(10):
        layout = layouts[slot]
        local_rows, local_cols = weights[slot].shape
        many_rows = local_rows * (groups if layout == "rows" else 1)
        many_cols = local_cols * (groups if layout == "columns" else 1)
        row_mean = row_squares[slot] * factor_square / many_cols + eps_factor
        column_mean = column_squares[slot] * factor_square / many_rows + eps_factor
        row_start = row_at + (member * local_rows if layout == "rows" else 0)
        column_start = column_at + (member * local_cols if layout == "columns" else 0)
        row_old = lax.dynamic_slice_in_dim(row_states, row_start, local_rows)
        column_old = lax.dynamic_slice_in_dim(column_states, column_start, local_cols)
        row_next = state_decay * row_old + (1.0 - state_decay) * row_mean
        column_next = state_decay * column_old + (1.0 - state_decay) * column_mean
        if layout == "rows":
            row_average = state_decay * jnp.mean(row_states[row_at : row_at + many_rows]) + (
                1.0 - state_decay
            ) * jnp.mean(column_mean)
        else:
            row_average = jnp.mean(row_next)
        clipped = gradients[slot] * factor
        update = clipped * lax.rsqrt(row_next[:, None] * column_next[None, :] / row_average)
        records.append(
            (clipped, update, jnp.sum(update * update), row_next, column_next, many_rows, many_cols)
        )
        row_at += many_rows
        column_at += many_cols
    shares = [jnp.stack([records[slot][2] for slot in split_slots])]
    for slot in split_slots:
        shares.append(records[slot][4] if layouts[slot] == "columns" else records[slot][3])
    spread = swap(slabs(jnp.concatenate(shares), 1)[0], "mp", 7, per_target=False)
    spread = spread.reshape(groups, -1)
    energies = jnp.sum(spread[:, : len(split_slots)], axis=0)
    start = len(split_slots)
    next_list = []
    row_list = []
    column_list = []
    for slot in range(10):
        clipped, update, energy, row_next, column_next, many_rows, many_cols = records[slot]
        if layouts[slot] != "whole":
            energy = energies[split_slots.index(slot)]
            length = column_next.shape[0] if layouts[slot] == "columns" else row_next.shape[0]
            joined = spread[:, start : start + length].reshape(-1)
            start += length
            if layouts[slot] == "columns":
                column_next = joined
            else:
                row_next = joined
        scale_down = jnp.maximum(1.0, jnp.sqrt(energy / (many_rows * many_cols)))
        next_list.append(weights[slot] - step_rate / math.sqrt(many_rows) * (update / scale_down))
        row_list.append(row_next)
        column_list.append(column_next)
    return (
        loss_sum,
        valid_total,
        grad_norm,
        *next_list,
        *[record[0] for record in records],
        jnp.concatenate(row_list),
        jnp.concatenate(column_list),
    )


def solution(mesh):
    in_specs = (
        P(("dp", "mp"), None, None),
        P(("dp", "mp"), None, None),
        P("dp"),
        P("dp"),
        P("dp"),
        P(),
        P(),
        P(),
        P(),
        P(),
        P(None, "mp"),
        P(None, "mp"),
        P("mp", None),
        P(None, "mp"),
        P("mp", None),
        P(None, "mp"),
        P(),
        P(),
        P(),
    )
    out_specs = (
        P(),
        P(),
        P(),
        P(),
        P(),
        P(),
        P(None, "mp"),
        P(None, "mp"),
        P("mp", None),
        P(None, "mp"),
        P("mp", None),
        P(None, "mp"),
        P(),
        P(),
        P(),
        P(),
        P(None, "mp"),
        P(None, "mp"),
        P("mp", None),
        P(None, "mp"),
        P("mp", None),
        P(None, "mp"),
        P(),
        P(),
        P(),
    )
    return jax.shard_map(body, mesh=mesh, in_specs=in_specs, out_specs=out_specs, check_vma=False)
```

```python
import functools
import math

import jax
import jax.numpy as jnp
from jax import lax
from jax.experimental import pallas as pl
from jax.experimental.pallas import tpu as pltpu
from jax.sharding import PartitionSpec as P

HD = 72
FREQ = 256
PIN = 16
SIDE = 16


eps_norm = 1e-06
eps_factor = 1e-30
clip_limit = 0.005
state_decay = 0.5
step_rate = 1.5
neg_large = -1e30
highest = lax.Precision.HIGHEST
MESH = pl.DeviceIdType.MESH


def product(operand, other_operand):
    return jnp.dot(operand, other_operand, preferred_element_type=jnp.float32)


def product_right(operand, other_operand):
    return lax.dot_general(
        operand, other_operand, (((1,), (1,)), ((), ())), preferred_element_type=jnp.float32
    )


def product_left(operand, other_operand):
    return lax.dot_general(
        operand, other_operand, (((0,), (0,)), ((), ())), preferred_element_type=jnp.float32
    )


def layer_norm(values):
    center = values - jnp.mean(values, axis=-1, keepdims=True)
    return center * lax.rsqrt(jnp.mean(center * center, axis=-1, keepdims=True) + eps_norm)


def norm_back(values, upstream):
    center = values - jnp.mean(values, axis=-1, keepdims=True)
    inverse = lax.rsqrt(jnp.mean(center * center, axis=-1, keepdims=True) + eps_norm)
    normed = center * inverse
    return inverse * (
        upstream
        - jnp.mean(upstream, axis=-1, keepdims=True)
        - normed * jnp.mean(upstream * normed, axis=-1, keepdims=True)
    )


def position_table(side, width):
    quarter = width // 4
    omega = jnp.exp(-math.log(10000.0) * jnp.arange(quarter, dtype=jnp.float32) / quarter)
    place = jnp.arange(side * side)
    column = (place % side).astype(jnp.float32)[:, None] * omega[None, :]
    row_angle = (place // side).astype(jnp.float32)[:, None] * omega[None, :]
    return jnp.concatenate(
        [jnp.sin(column), jnp.cos(column), jnp.sin(row_angle), jnp.cos(row_angle)], axis=1
    )


def time_features(steps, width):
    half = width // 2
    freq = jnp.exp(-math.log(10000.0) * jnp.arange(half, dtype=jnp.float32) / half)
    angle = steps.astype(jnp.float32)[:, None] * freq[None, :]
    return jnp.concatenate([jnp.cos(angle), jnp.sin(angle)], axis=1)


def peers(span):
    dp, mp = lax.axis_index("dp"), lax.axis_index("mp")
    copies, groups = lax.axis_size("dp"), lax.axis_size("mp")
    if span == "mp":
        return mp, groups, lambda place: (dp, place)
    if span == "dp":
        return dp, copies, lambda place: (place, mp)
    return dp * groups + mp, copies * groups, lambda place: (place // groups, lax.rem(place, groups))


def greet(span):
    here, size, device = peers(span)
    barrier = pltpu.get_barrier_semaphore()

    @pl.loop(1, size)
    def _(step):
        pl.semaphore_signal(
            barrier,
            inc=1,
            device_id=device(lax.rem(here + step, size)),
            device_id_type=MESH,
        )

    pl.semaphore_wait(barrier, size - 1)


def to_all(span, pick, landing, send_sems, recv_sems):
    here, size, device = peers(span)

    def copy(step):
        place = lax.rem(here + step, size)
        return pltpu.make_async_remote_copy(
            src_ref=pick(place),
            dst_ref=landing(here),
            send_sem=send_sems.at[step],
            recv_sem=recv_sems.at[step],
            device_id=device(place),
            device_id_type=MESH,
        )

    @pl.loop(1, size)
    def _(step):
        copy(step).start()

    def wait():
        @pl.loop(1, size)
        def _(step):
            copy(step).wait()

    return wait


def sum_over(ref):
    return lax.fori_loop(1, ref.shape[0], lambda index, total: total + ref[index], ref[0])


def swap_kernel(span, per_target, groups, x_ref, out_ref, send_sems, recv_sems):
    here, _, _ = peers(span)

    def pick(place):
        return x_ref.at[lax.rem(place, groups)] if per_target else x_ref

    greet(span)
    wait = to_all(span, pick, lambda place: out_ref.at[place], send_sems, recv_sems)
    out_ref[here] = x_ref[lax.rem(here, groups)] if per_target else x_ref[...]
    wait()


def group_size(span):
    sizes = {"dp": lax.axis_size("dp"), "mp": lax.axis_size("mp")}
    return sizes.get(span, sizes["dp"] * sizes["mp"])


def call(kernel, inputs, out_shapes, scratch, collective_id):
    return pl.pallas_call(
        kernel,
        out_shape=[jax.ShapeDtypeStruct(shape, jnp.float32) for shape in out_shapes],
        in_specs=[pl.BlockSpec(memory_space=pltpu.VMEM)] * len(inputs),
        out_specs=[pl.BlockSpec(memory_space=pltpu.VMEM)] * len(out_shapes),
        scratch_shapes=scratch,
        compiler_params=pltpu.CompilerParams(
            collective_id=collective_id, has_side_effects=True, vmem_limit_bytes=32 * 1024 * 1024
        ),
    )(*inputs)


def swap(values, span, collective_id, per_target=True):
    size = group_size(span)
    slab = values.shape[-2:]
    (result,) = call(
        functools.partial(swap_kernel, span, per_target, lax.axis_size("mp")),
        [values],
        [(size,) + slab],
        [pltpu.SemaphoreType.DMA((size,)), pltpu.SemaphoreType.DMA((size,))],
        collective_id,
    )
    return result


def slabs(flat, blocks):
    chunk = 1024 * blocks
    short = (-flat.shape[0]) % chunk
    return jnp.pad(flat, (0, short)).reshape(blocks, -1, 128)


def reduce_kernel(counts, *refs):
    copies, groups = counts
    lines = {"a": 4, "b": groups // 4, "y": copies // 2}
    chunks = (len(refs) - 20) // 2
    parts = refs[:chunks]
    back_ref, low_ref, shared_ref = refs[chunks : chunks + 3]
    outs = refs[chunks + 3 : 2 * chunks + 3]
    cols_out, shared_out, signal_out = refs[2 * chunks + 3 : 2 * chunks + 6]
    held, twin, first_b, first_y, second, third, send_sems, recv_sems = refs[
        2 * chunks + 6 : 2 * chunks + 14
    ]
    shared_land, signal_land, signal_part, stack, side_sends, side_recvs = refs[2 * chunks + 14 :]
    splits = parts[0].shape[4]
    dp, mp = lax.axis_index("dp"), lax.axis_index("mp")
    at = {"a": mp // lines["b"], "b": lax.rem(mp, lines["b"]), "y": dp // 2}
    core = lax.rem(dp, 2)

    def device(**moved):
        place = {**at, "core": core, **moved}
        return (place["y"] * 2 + place["core"], place["a"] * lines["b"] + place["b"])

    greet("all")

    here = dp * groups + mp
    waits = []

    def side(slot, span, pick, landing):
        waits.append(to_all(span, pick, landing, side_sends.at[slot], side_recvs.at[slot]))

    def side_start():
        side(0, "all", lambda place: back_ref.at[lax.rem(place, groups)], cols_out_at)
        side(1, "all", lambda place: shared_ref.at[place], lambda place: shared_land.at[place])
        cols_out[here] = back_ref[mp]
        shared_land[here] = shared_ref[here]

    def cols_out_at(place):
        return cols_out.at[place]

    def side_signal():
        waits[0]()
        images = cols_out.shape[1]
        stack[...] = jnp.zeros_like(stack)
        for member in range(groups):
            stack[8 * member : 8 * member + images] = cols_out[dp * groups + member]
        found = product_right(stack[...].astype(jnp.bfloat16), low_ref[...])
        for member in range(groups):
            signal_part[member] = found[8 * member : 8 * member + images]
        signal_land[mp] = signal_part[mp]
        side(2, "mp", lambda place: signal_part.at[place], lambda place: signal_land.at[place])

    def side_show():
        waits[1]()
        shared_out[here] = sum_over(shared_land)
        side(3, "all", lambda place: shared_out.at[here], lambda place: shared_out.at[place])
        waits[2]()
        signal_out[here] = sum_over(signal_land)
        side(4, "all", lambda place: signal_out.at[here], lambda place: signal_out.at[place])

    def side_end():
        waits[3]()
        waits[4]()

    units = [(chunk, split) for chunk in range(chunks) for split in range(splits)]
    slots = {}

    def sems(unit, name):
        slot = slots.setdefault(name, len(slots))
        return send_sems.at[unit, slot], recv_sems.at[unit, slot]

    def add_into(target, source):
        @pl.loop(0, target.shape[0])
        def _(index):
            target[index] = target[index] + source[index]

    def twin_copy(unit):
        chunk, split = units[unit]
        send, recv = sems(unit, "twin")
        return pltpu.make_async_remote_copy(
            src_ref=parts[chunk].at[:, 1 - core, :, :, split],
            dst_ref=twin.at[unit],
            send_sem=send,
            recv_sem=recv,
            device_id=device(core=1 - core),
            device_id_type=MESH,
        )

    def held_copy(unit):
        chunk, split = units[unit]
        return pltpu.make_async_copy(
            parts[chunk].at[:, core, :, :, split], held.at[unit], sems(unit, "held")[1]
        )

    def line_steps(unit, axis, name, pick, landing):
        size, here = lines[axis], at[axis]
        tasks = []

        def slot_of(up, hop):
            return 0 if size == 2 else hop - 1 + (size - 1 if up else 0)

        def copy(up, hop):
            target = here + hop if up else here - hop
            send, recv = sems(unit, (name, up, hop))
            slot = slot_of(up, hop)
            safe = lax.rem(target + size, size)
            beside = here + 1 if up else here - 1
            beside = lax.rem(beside + size, size)
            return pltpu.make_async_remote_copy(
                src_ref=pick(safe),
                dst_ref=landing(slot),
                send_sem=send,
                recv_sem=recv,
                device_id=device(**{axis: beside}),
                device_id_type=MESH,
            )

        def sends(up, hop):
            return here + hop <= size - 1 if up else here - hop >= 0

        def arrives(up, hop):
            if up:
                return (here >= 1) & (here + hop - 1 <= size - 1)
            return (here <= size - 2) & (here - hop + 1 >= 0)

        def take(up, hop):
            @pl.when(arrives(up, hop))
            def _():
                copy(up, hop).wait_recv()
                slot = slot_of(up, hop)
                target = here + hop - 1 if up else here - hop + 1
                add_into(pick(lax.rem(target + size, size)), landing(slot))

        def give(up, hop):
            @pl.when(sends(up, hop))
            def _():
                copy(up, hop).start()

        def finish(up, hop):
            @pl.when(sends(up, hop))
            def _():
                copy(up, hop).wait_send()

        for hop in range(size - 1, 0, -1):

            def begin(hop=hop):
                for up in (True, False):
                    if hop < size - 1:
                        take(up, hop + 1)
                    give(up, hop)

            tasks.append(begin)

        def close():
            for up in (True, False):
                take(up, 1)

        def drain():
            for hop in range(1, size):
                for up in (True, False):
                    finish(up, hop)

        return tasks, close, drain

    def unit_tasks(unit):
        chunk, split = units[unit]
        block = held.at[unit]
        halves = []
        drains = []
        for half, order in ((0, ("b", "y")), (1, ("y", "b"))):
            rows_a = pl.ds(2 * half, 2)

            def pick_one(target, axis=order[0], rows_a=rows_a):
                if axis == "b":
                    return block.at[:, rows_a, target]
                return block.at[target, rows_a]

            def pick_two(target, axis=order[1], rows_a=rows_a):
                if axis == "b":
                    return block.at[at["y"], rows_a, target]
                return block.at[target, rows_a, at["b"]]

            one = line_steps(
                unit,
                order[0],
                ("one", half),
                pick_one,
                lambda slot, axis=order[0]: (first_b if axis == "b" else first_y).at[unit, slot],
            )
            two = line_steps(
                unit,
                order[1],
                ("two", half),
                pick_two,
                lambda slot, half=half: second.at[unit, half, slot],
            )
            steps = list(one[0])
            joined = two[0][0]

            def pass_on(close=one[1], go=joined):
                close()
                go()

            steps += [pass_on] + list(two[0][1:])
            halves.append((steps, two[1]))
            drains += [one[2], two[2]]
        last = line_steps(
            unit,
            "a",
            "last",
            lambda target: block.at[at["y"], target, pl.ds(at["b"], 1)],
            lambda slot: third.at[unit, slot],
        )
        drains.append(last[2])
        out = outs[chunk]

        def spread_copy(owner, to):
            send, recv = sems(unit, ("spread", owner[2], to[2]))
            return pltpu.make_async_remote_copy(
                src_ref=out.at[owner[0], owner[1], split],
                dst_ref=out.at[owner[0], owner[1], split],
                send_sem=send,
                recv_sem=recv,
                device_id=device(y=to[0], core=to[1]),
                device_id_type=MESH,
            )

        size_y = lines["y"]
        me = (at["y"], core, 0)
        twin_place = (at["y"], 1 - core, "twin")

        def far(step):
            return (lax.rem(at["y"] + step, size_y), core, step)

        def start():
            held_copy(unit).wait()
            twin_copy(unit).wait_recv()

            @pl.loop(0, block.shape[0])
            def _(row):
                @pl.loop(0, block.shape[1])
                def _(group):
                    block[row, group] = block[row, group] + twin[unit, row, group]

            for steps, _ in halves:
                steps[0]()

        tasks = [start]
        for index in range(1, len(halves[0][0])):

            def middle(index=index):
                for steps, _ in halves:
                    steps[index]()

            tasks.append(middle)

        def to_last():
            for _, close in halves:
                close()
            last[0][0]()

        tasks.append(to_last)
        tasks += list(last[0][1:])

        def sum_done():
            last[1]()
            out[at["y"], core, split] = block[at["y"], at["a"], at["b"]]
            for step in range(1, size_y):
                spread_copy(me, far(step)).start()
            spread_copy(me, twin_place).start()

        tasks.append(sum_done)

        def before(step):
            return (lax.rem(at["y"] + size_y - step, size_y), core, step)

        def forward():
            for step in range(1, size_y):
                spread_copy((at["y"], core, 0), far(step)).wait_recv()
                source = before(step)
                spread_copy(source, twin_place).start()

        tasks.append(forward)

        def end():
            spread_copy(me, twin_place).wait()
            for step in range(1, size_y):
                spread_copy(before(step), twin_place).wait()
                spread_copy(me, far(step)).wait_send()
            twin_copy(unit).wait_send()
            for drain in drains:
                drain()

        tasks.append(end)
        return tasks

    for unit in range(len(units)):
        twin_copy(unit).start()
        held_copy(unit).start()
    side_start()
    queues = [unit_tasks(unit) for unit in range(len(units))]
    depth = len(queues[0])
    for tick in range(len(units) + depth - 1):
        for unit in reversed(range(len(units))):
            task = tick - unit
            if 0 <= task < depth:
                queues[unit][task]()
        if tick == 1:
            side_signal()
        if tick == 3:
            side_show()
    side_end()


def reduce_weights(partials, back, low_weights, shared, collective_id):
    copies, groups = lax.axis_size("dp"), lax.axis_size("mp")
    rows, width = partials[0].shape
    size_b, size_y = groups // 4, copies // 2
    piece = rows // (copies * groups)
    share = 48 if piece % 48 == 0 else piece
    splits = piece // share
    shaped = [
        part.reshape(size_y, 2, 4, size_b, splits, share, width) for part in partials
    ]
    units = splits * len(partials)
    slab = (share, width)
    slots_b = 1 if size_b == 2 else 2 * (size_b - 1)
    slots_y = 1 if size_y == 2 else 2 * (size_y - 1)
    scratch = [
        pltpu.VMEM((units, size_y, 4, size_b) + slab, jnp.bfloat16),
        pltpu.VMEM((units, size_y, 4, size_b) + slab, jnp.bfloat16),
        pltpu.VMEM((units, slots_b, size_y, 2) + slab, jnp.bfloat16),
        pltpu.VMEM((units, slots_y, 2, size_b) + slab, jnp.bfloat16),
        pltpu.VMEM((units, 2, max(slots_b, slots_y), 2) + slab, jnp.bfloat16),
        pltpu.VMEM((units, 6, 1) + slab, jnp.bfloat16),
        pltpu.SemaphoreType.DMA((units, 40)),
        pltpu.SemaphoreType.DMA((units, 40)),
        pltpu.VMEM(shared.shape, jnp.float32),
        pltpu.VMEM((groups, back.shape[1], width), jnp.float32),
        pltpu.VMEM((groups, back.shape[1], width), jnp.float32),
        pltpu.VMEM((8 * groups, back.shape[2]), jnp.float32),
        pltpu.SemaphoreType.DMA((5, copies * groups)),
        pltpu.SemaphoreType.DMA((5, copies * groups)),
    ]
    results = pl.pallas_call(
        functools.partial(reduce_kernel, (copies, groups)),
        out_shape=[jax.ShapeDtypeStruct((size_y, 2, splits) + slab, jnp.bfloat16)] * len(partials)
        + [
            jax.ShapeDtypeStruct((copies * groups,) + back.shape[1:], jnp.float32),
            jax.ShapeDtypeStruct(shared.shape, jnp.float32),
            jax.ShapeDtypeStruct((copies * groups, back.shape[1], width), jnp.float32),
        ],
        in_specs=[pl.BlockSpec(memory_space=pl.ANY)] * len(partials)
        + [pl.BlockSpec(memory_space=pltpu.VMEM)] * 3,
        out_specs=[pl.BlockSpec(memory_space=pltpu.VMEM)] * (len(partials) + 3),
        scratch_shapes=scratch,
        compiler_params=pltpu.CompilerParams(
            collective_id=collective_id, has_side_effects=True, vmem_limit_bytes=60 * 1024 * 1024
        ),
    )(*shaped, back, low_weights, shared)
    sums = [result.reshape(copies * piece, width) for result in results[: len(partials)]]
    return sums, *results[len(partials) :]


def gather_kernel(counts, piece_ref, out_ref, send_sems, recv_sems, local_sems):
    copies, groups = counts
    size_a, size_b, size_y = 4, groups // 4, copies // 2
    splits = piece_ref.shape[0]
    dp, mp = lax.axis_index("dp"), lax.axis_index("mp")
    a, b, y, core = mp // size_b, lax.rem(mp, size_b), dp // 2, lax.rem(dp, 2)

    def device(a=a, b=b, y=y, core=core):
        return (y * 2 + core, a * size_b + b)

    def along(axis, step):
        if axis == "a":
            return device(a=lax.rem(a + step, size_a))
        if axis == "b":
            return device(b=lax.rem(b + step, size_b))
        return device(y=lax.rem(y + step, size_y))

    lines = {"a": size_a, "b": size_b, "y": size_y}
    barrier = pltpu.get_barrier_semaphore()
    pl.semaphore_signal(barrier, inc=1, device_id=device(core=1 - core), device_id_type=MESH)
    for axis, size in lines.items():
        for step in range(1, size):
            pl.semaphore_signal(
                barrier, inc=1, device_id=along(axis, step), device_id_type=MESH
            )
    pl.semaphore_wait(barrier, 1 + sum(size - 1 for size in lines.values()))
    slots = {}

    def place(split, ys, cores, as_, bs):
        return out_ref.at[ys, cores, as_, bs, split]

    def own_copy(split):
        return pltpu.make_async_copy(
            piece_ref.at[split], place(split, y, core, a, b), local_sems.at[split]
        )

    def a_copies(split):
        copies_ = []
        for step in range(1, size_a):
            slot = slots.setdefault(("a", step), len(slots))
            copies_.append(
                pltpu.make_async_remote_copy(
                    src_ref=piece_ref.at[split],
                    dst_ref=place(split, y, core, a, b),
                    send_sem=send_sems.at[split, slot],
                    recv_sem=recv_sems.at[split, slot],
                    device_id=along("a", step),
                    device_id_type=MESH,
                )
            )
        return copies_

    low, high = pl.ds(0, 2), pl.ds(2, 2)
    every_b, every_y, every_a = pl.ds(0, size_b), pl.ds(0, size_y), pl.ds(0, size_a)

    def spread(split, name, axis, source):
        copies_ = []
        for step in range(1, lines[axis]):
            slot = slots.setdefault((name, step), len(slots))
            copies_.append(
                pltpu.make_async_remote_copy(
                    src_ref=source,
                    dst_ref=source,
                    send_sem=send_sems.at[split, slot],
                    recv_sem=recv_sems.at[split, slot],
                    device_id=along(axis, step),
                    device_id_type=MESH,
                )
            )
        return copies_

    def first(split):
        return (
            spread(split, "low_b", "b", place(split, y, core, low, b)),
            spread(split, "high_y", "y", place(split, y, core, high, b)),
        )

    def second(split):
        return (
            spread(split, "low_y", "y", place(split, y, core, low, every_b)),
            spread(split, "high_b", "b", place(split, every_y, core, high, b)),
        )

    def twin(split):
        slot = slots.setdefault("twin", len(slots))
        source = place(split, every_y, core, every_a, every_b)
        return pltpu.make_async_remote_copy(
            src_ref=source,
            dst_ref=source,
            send_sem=send_sems.at[split, slot],
            recv_sem=recv_sems.at[split, slot],
            device_id=device(core=1 - core),
            device_id_type=MESH,
        )

    for split in range(splits):
        own_copy(split).start()
        for item in a_copies(split):
            item.start()

    def to_first(split):
        own_copy(split).wait()
        for item in a_copies(split):
            item.wait_recv()
        for items in first(split):
            for item in items:
                item.start()

    def to_second(split):
        for items, following in zip(first(split), second(split)):
            for item in items:
                item.wait_recv()
            for item in following:
                item.start()

    def to_twin(split):
        for items in second(split):
            for item in items:
                item.wait_recv()
        twin(split).start()

    stages = (to_first, to_second, to_twin)
    for tick in range(splits + len(stages) - 1):
        for split in reversed(range(splits)):
            if 0 <= tick - split < len(stages):
                stages[tick - split](split)
    for split in range(splits):
        twin(split).wait()
        for item in a_copies(split):
            item.wait_send()
        for items in first(split) + second(split):
            for item in items:
                item.wait_send()


def gather_pieces(piece, collective_id):
    copies, groups = lax.axis_size("dp"), lax.axis_size("mp")
    rows, width = piece.shape
    share = 48 if rows % 48 == 0 else rows
    splits = rows // share
    size_b, size_y = groups // 4, copies // 2
    sems = 4 + 2 * (size_b + size_y)
    gathered = pl.pallas_call(
        functools.partial(gather_kernel, (copies, groups)),
        out_shape=jax.ShapeDtypeStruct(
            (size_y, 2, 4, size_b, splits, share, width), jnp.bfloat16
        ),
        in_specs=[pl.BlockSpec(memory_space=pl.ANY)],
        out_specs=pl.BlockSpec(memory_space=pl.ANY),
        scratch_shapes=[
            pltpu.SemaphoreType.DMA((splits, sems)),
            pltpu.SemaphoreType.DMA((splits, sems)),
            pltpu.SemaphoreType.DMA((splits,)),
        ],
        compiler_params=pltpu.CompilerParams(collective_id=collective_id, has_side_effects=True),
    )(piece.reshape(splits, share, width))
    return gathered.reshape(copies * groups * rows, width)


def row_block(rows):
    for block in (128, 144):
        if rows % block == 0:
            return block
    return rows


def scale_kernel(layouts, flipped, *refs):
    slots = len(layouts)
    grads = refs[:slots]
    row_old, column_old = refs[slots : slots + 2]
    row_coef, column_coef, row_new, column_new, shown, norms = refs[slots + 2 : slots + 8]
    by_row, land, mine, send_sems, recv_sems = refs[slots + 8 :]
    member, groups, _ = peers("mp")
    wide = row_old.shape[1]
    lane = lax.broadcasted_iota(jnp.int32, (1, 128), 1)
    place = lax.broadcasted_iota(jnp.int32, (1, wide), 1)
    split = [slot for slot in range(slots) if layouts[slot] != "whole"]
    one = jnp.ones((1, 1), jnp.float32)

    def all_sum(values):
        return jnp.sum(jnp.sum(values, axis=1, keepdims=True), axis=0, keepdims=True)

    greet("mp")
    by_row[...] = jnp.zeros_like(by_row)
    column_sums = []
    squares = []
    for slot in range(slots):
        count, across_ = grads[slot].shape
        block = row_block(count)

        def step(index, total, slot=slot, block=block):
            at = pl.ds(pl.multiple_of(index * block, block), block)
            values = grads[slot][at, :].astype(jnp.float32)
            square = values * values
            by_row[at, :] += jnp.where(lane == slot, jnp.sum(square, axis=1, keepdims=True), 0.0)
            return total + jnp.sum(square, axis=0, keepdims=True)

        total = lax.fori_loop(0, count // block, step, jnp.zeros((1, across_), jnp.float32))
        column_sums.append(total)
        squares.append(jnp.sum(total, axis=1, keepdims=True))
    row_sums = by_row[...].T

    mine[...] = jnp.zeros_like(mine)
    for index, slot in enumerate(split):
        mine[0, index : index + 1, :] = column_sums[slot]
    mine[0, 6:7, :] = sum(squares[slot] for slot in split) * jnp.ones((1, wide), jnp.float32)
    wait = to_all(
        "mp",
        lambda place_: mine.at[0],
        lambda place_: land.at[place_],
        send_sems.at[0],
        recv_sems.at[0],
    )
    land[member] = mine[0]
    wait()
    crossed = sum_over(land)
    local_square = sum(squares[slot] for slot in range(slots) if slot not in split)
    norm = jnp.sqrt(crossed[6:7, :1] + local_square)
    factor = clip_limit / jnp.maximum(norm, clip_limit)
    factor_square = factor * factor
    norms[...] = jnp.where(lax.broadcasted_iota(jnp.int32, (8, 128), 0) == 0, norm, factor)

    averages = []
    many = []
    next_rows = []
    next_columns = []
    inverse = [jnp.ones((1, wide), jnp.float32)] * slots
    for slot, layout in enumerate(layouts):
        count, across_ = grads[slot].shape
        many_rows = count * (groups if layout == "rows" else 1)
        many_columns = across_
        many.append((many_rows, many_columns))
        row_sum = row_sums[slot : slot + 1, :]
        column_sum = column_sums[slot]
        if layout == "rows":
            column_sum = crossed[split.index(slot) : split.index(slot) + 1, :]
        row_mean = row_sum * factor_square / many_columns + eps_factor
        column_mean = column_sum * factor_square / many_rows + eps_factor
        next_row = state_decay * row_old[slot : slot + 1, :] + (1.0 - state_decay) * row_mean
        next_column = (
            state_decay * column_old[slot : slot + 1, :across_] + (1.0 - state_decay) * column_mean
        )
        if flipped[slot]:
            average = jnp.sum(next_column, axis=1, keepdims=True) / across_
        elif layout == "rows":
            first = slots + sum(
                many[other][0] // wide for other in split if other < slot and not flipped[other]
            )
            old = row_old[first : first + many_rows // wide, :]
            average = (
                state_decay * all_sum(old) / many_rows
                + (1.0 - state_decay) * jnp.sum(column_mean, axis=1, keepdims=True) / across_
            )
        else:
            average = (
                jnp.sum(jnp.where(place < count, next_row, 0.0), axis=1, keepdims=True) / many_rows
            )
        averages.append(average)
        next_rows.append(next_row)
        next_columns.append(next_column)
        row_new[slot : slot + 1, :] = next_row
        column_new[slot : slot + 1, :] = next_column
        inverse[slot] = jnp.where(place < count, 1.0 / next_row, 0.0)
    blank = jnp.zeros((128 - slots, wide), jnp.float32)
    by_row[...] = jnp.concatenate(inverse + [blank], axis=0).T

    energies = []
    for slot in range(slots):
        count, across_ = grads[slot].shape
        block = row_block(count)
        inverse_column = 1.0 / next_columns[slot]

        def step(index, total, slot=slot, block=block, inverse_column=inverse_column):
            at = pl.ds(pl.multiple_of(index * block, block), block)
            values = grads[slot][at, :].astype(jnp.float32)
            weighted = jnp.sum(values * values * inverse_column, axis=1, keepdims=True)
            return total + jnp.sum(
                jnp.where(lane == slot, by_row[at, :], 0.0) * weighted, axis=0, keepdims=True
            )

        total = lax.fori_loop(0, count // block, step, jnp.zeros((1, 128), jnp.float32))
        energies.append(
            jnp.sum(total, axis=1, keepdims=True) * factor_square * averages[slot]
        )

    mine[1, :, :] = jnp.zeros_like(mine[1])
    for index, slot in enumerate(split):
        mine[1, index : index + 1, :] = next_rows[slot]
    spread = jnp.zeros((1, wide), jnp.float32)
    for slot in split:
        spread = jnp.where(place == slot, energies[slot], spread)
    mine[1, 6:7, :] = spread
    wait = to_all(
        "mp",
        lambda place_: mine.at[1],
        lambda place_: shown.at[place_],
        send_sems.at[1],
        recv_sems.at[1],
    )
    shown[member] = mine[1]
    wait()
    spread = sum_over(shown)[6:7, :]
    coefs = []
    for slot, layout in enumerate(layouts):
        many_rows, many_columns = many[slot]
        energy = energies[slot]
        if layout != "whole":
            energy = jnp.sum(jnp.where(place == slot, spread, 0.0), axis=1, keepdims=True)
        scale_down = jnp.maximum(one, jnp.sqrt(energy / (many_rows * many_columns)))
        shrink = (
            step_rate / math.sqrt(many[slot][1 if flipped[slot] else 0]) * factor * jnp.sqrt(averages[slot]) / scale_down
        )
        coefs.append(shrink * lax.rsqrt(next_rows[slot]))
        column_coef[slot : slot + 1, :] = lax.rsqrt(next_columns[slot])
    row_coef[...] = jnp.concatenate(coefs + [blank], axis=0).T


def scales(gradients, row_old, column_old, layouts, flipped, collective_id):
    groups = lax.axis_size("mp")
    wide = row_old.shape[1]
    shape = lambda *dims: jax.ShapeDtypeStruct(dims, jnp.float32)
    vmem = pl.BlockSpec(memory_space=pltpu.VMEM)
    return pl.pallas_call(
        functools.partial(scale_kernel, layouts, flipped),
        out_shape=[
            shape(wide, 128),
            shape(16, wide),
            shape(16, wide),
            shape(16, wide),
            shape(groups, 8, wide),
            shape(8, 128),
        ],
        in_specs=[vmem] * (len(gradients) + 2),
        out_specs=[vmem] * 6,
        scratch_shapes=[
            pltpu.VMEM((wide, 128), jnp.float32),
            pltpu.VMEM((groups, 8, wide), jnp.float32),
            pltpu.VMEM((2, 8, wide), jnp.float32),
            pltpu.SemaphoreType.DMA((2, groups)),
            pltpu.SemaphoreType.DMA((2, groups)),
        ],
        compiler_params=pltpu.CompilerParams(
            collective_id=collective_id, has_side_effects=True, vmem_limit_bytes=56 * 1024 * 1024
        ),
    )(*gradients, row_old, column_old)


def apply_kernel(layouts, flipped, groups, *refs):
    slots = len(layouts)
    grads, weights = refs[:slots], refs[slots : 2 * slots]
    row_coef, column_coef, row_new, column_new, shown, norms = refs[2 * slots : 2 * slots + 6]
    rest = refs[2 * slots + 6 :]
    nexts, clips = rest[:slots], rest[slots : 2 * slots]
    row_stats, column_stats = rest[2 * slots : 2 * slots + 2]
    held, clipped = rest[2 * slots + 2 : 3 * slots + 2], rest[3 * slots + 2 : 4 * slots + 2]
    sems = rest[4 * slots + 2]
    low = [grads[slot].dtype == jnp.bfloat16 for slot in range(slots)]
    order = sorted(range(slots), key=lambda slot: -weights[slot].size)

    def weight_in(slot):
        return pltpu.make_async_copy(weights[slot], held[slot], sems.at[0, slot])

    def grad_in(slot):
        return pltpu.make_async_copy(grads[slot], clipped[slot], sems.at[1, slot])

    def weight_out(slot):
        return pltpu.make_async_copy(held[slot], nexts[slot], sems.at[2, slot])

    def grad_out(slot):
        return pltpu.make_async_copy(clipped[slot], clips[slot], sems.at[3, slot])

    for slot in order:
        weight_in(slot).start()
        if not low[slot]:
            grad_in(slot).start()

    split = [slot for slot in range(slots) if layouts[slot] != "whole"]
    ends = [0, 0]
    for slot, layout in enumerate(layouts):
        count, across_ = weights[slot].shape
        own, other = (column_stats, row_stats) if flipped[slot] else (row_stats, column_stats)
        own_end, other_end = (1, 0) if flipped[slot] else (0, 1)
        at = ends[own_end]
        if layout == "rows":
            spot = split.index(slot)
            for member in range(groups):
                own[:, at : at + count] = shown[member, spot : spot + 1, :count]
                at += count
        else:
            own[:, at : at + count] = row_new[slot : slot + 1, :count]
            at += count
        ends[own_end] = at
        other[:, ends[other_end] : ends[other_end] + across_] = column_new[slot : slot + 1, :]
        ends[other_end] += across_

    factor = norms[1:2, :1]
    for slot in order:
        count, across_ = weights[slot].shape
        block = row_block(count)
        weight_in(slot).wait()
        if not low[slot]:
            grad_in(slot).wait()
        source = grads[slot] if low[slot] else clipped[slot]
        by_column = column_coef[slot : slot + 1, :across_]

        @pl.loop(0, count // block)
        def _(index, slot=slot, block=block, source=source, by_column=by_column):
            at = pl.ds(pl.multiple_of(index * block, block), block)
            gradient = source[at, :].astype(jnp.float32)
            step_size = row_coef[at, slot : slot + 1] * by_column
            held[slot][at, :] = held[slot][at, :] - gradient * step_size
            clipped[slot][at, :] = gradient * factor

        weight_out(slot).start()
        grad_out(slot).start()
    for slot in order:
        weight_out(slot).wait()
        grad_out(slot).wait()


def apply_scales(gradients, weights, found, layouts, flipped):
    groups = lax.axis_size("mp")
    vmem = pl.BlockSpec(memory_space=pltpu.VMEM)
    stay = pl.BlockSpec(memory_space=pl.ANY)
    many_rows = 0
    many_columns = 0
    for weight, layout, flip in zip(weights, layouts, flipped):
        extents = (weight.shape[0] * (groups if layout == "rows" else 1), weight.shape[1])
        many_rows += extents[1 if flip else 0]
        many_columns += extents[0 if flip else 1]
    shapes = [jax.ShapeDtypeStruct(weight.shape, jnp.float32) for weight in weights]
    buffers = [pltpu.VMEM(weight.shape, jnp.float32) for weight in weights]
    size = sum(weight.size for weight in weights)
    results = pl.pallas_call(
        functools.partial(apply_kernel, layouts, flipped, groups),
        out_shape=shapes
        + shapes
        + [
            jax.ShapeDtypeStruct((1, many_rows), jnp.float32),
            jax.ShapeDtypeStruct((1, many_columns), jnp.float32),
        ],
        in_specs=[vmem if part.dtype == jnp.bfloat16 else stay for part in gradients]
        + [stay] * len(weights)
        + [vmem] * 6,
        out_specs=[stay] * (2 * len(weights)) + [vmem] * 2,
        scratch_shapes=buffers + buffers + [pltpu.SemaphoreType.DMA((4, len(weights)))],
        compiler_params=pltpu.CompilerParams(vmem_limit_bytes=58 * 1024 * 1024),
        cost_estimate=pl.CostEstimate(flops=4 * size, bytes_accessed=16 * size, transcendentals=0),
    )(*gradients, *weights, *found)
    count = len(weights)
    return (
        results[:count],
        results[count : 2 * count],
        results[2 * count].reshape(-1),
        results[2 * count + 1].reshape(-1),
    )


def weights_of(keys, queries, live):
    scores = product_left(keys, queries) * HD ** (-0.5)
    scores = jnp.where(live, scores, neg_large)
    exponent = jnp.exp(scores - jnp.max(scores, axis=0, keepdims=True))
    return exponent / jnp.sum(exponent, axis=0, keepdims=True)


def attend_kernel(length_ref, q_ref, k_ref, v_ref, out_ref):
    patches = q_ref.shape[1]
    pair = 2 * HD
    live = lax.broadcasted_iota(jnp.int32, (patches, patches), 0) < length_ref[pl.program_id(0)]
    upper = lax.broadcasted_iota(jnp.int32, (pair, patches), 0) < HD

    @pl.loop(0, q_ref.shape[0] // pair, unroll=4)
    def _(index):
        rows = pl.ds(pl.multiple_of(index * pair, 16), pair)
        queries, keys, values = q_ref[rows, :], k_ref[rows, :], v_ref[rows, :]
        zero = jnp.zeros_like(queries)
        mixed = []
        for half in range(2):
            own = upper if half == 0 else ~upper
            probs = weights_of(keys, jnp.where(own, queries, zero), live)
            mixed.append(product(values, probs.astype(jnp.bfloat16)))
        out_ref[rows, :] = jnp.where(upper, mixed[0], mixed[1]).astype(jnp.bfloat16)


def attend_back_kernel(length_ref, q_ref, k_ref, v_ref, up_ref, down_ref):
    patches = q_ref.shape[1]
    pair = 2 * HD
    live = lax.broadcasted_iota(jnp.int32, (patches, patches), 0) < length_ref[pl.program_id(0)]
    upper = lax.broadcasted_iota(jnp.int32, (pair, patches), 0) < HD

    @pl.loop(0, q_ref.shape[0] // pair, unroll=4)
    def _(index):
        rows = pl.ds(pl.multiple_of(index * pair, 16), pair)
        queries, keys, values, upstream = (
            q_ref[rows, :],
            k_ref[rows, :],
            v_ref[rows, :],
            up_ref[rows, :],
        )
        zero = jnp.zeros_like(queries)
        found = []
        for half in range(2):
            own = upper if half == 0 else ~upper
            probs = weights_of(keys, jnp.where(own, queries, zero), live)
            probs_grad = product_left(values, jnp.where(own, upstream, zero))
            weighted = probs * probs_grad
            score_grad = (
                weighted - probs * jnp.sum(weighted, axis=0, keepdims=True)
            ).astype(jnp.bfloat16)
            found.append(
                (
                    product(keys, score_grad),
                    product_right(queries, score_grad),
                    product_right(upstream, probs.astype(jnp.bfloat16)),
                )
            )
        scale = HD ** (-0.5)
        down_ref[0, rows, :] = (jnp.where(upper, found[0][0], found[1][0]) * scale).astype(jnp.bfloat16)
        down_ref[1, rows, :] = (jnp.where(upper, found[0][1], found[1][1]) * scale).astype(jnp.bfloat16)
        down_ref[2, rows, :] = jnp.where(upper, found[0][2], found[1][2]).astype(jnp.bfloat16)


def _specs(width, patches):
    def spec(block):
        return pl.BlockSpec((width, patches), lambda image, lengths: (block, image))

    return spec


def attend(qkv, lengths, images):
    width, rows = qkv.shape[0] // 3, qkv.shape[1]
    patches = rows // images
    spec = _specs(width, patches)
    return pl.pallas_call(
        attend_kernel,
        grid_spec=pltpu.PrefetchScalarGridSpec(
            num_scalar_prefetch=1,
            grid=(images,),
            in_specs=[spec(0), spec(1), spec(2)],
            out_specs=spec(0),
        ),
        out_shape=jax.ShapeDtypeStruct((width, rows), jnp.bfloat16),
        compiler_params=pltpu.CompilerParams(vmem_limit_bytes=48 * 1024 * 1024),
        cost_estimate=pl.CostEstimate(flops=4 * rows * patches * width, bytes_accessed=8 * rows * width, transcendentals=0),
    )(lengths, qkv, qkv, qkv)


def attend_back(qkv, upstream, lengths, images):
    width, rows = upstream.shape
    patches = rows // images
    spec = _specs(width, patches)
    return pl.pallas_call(
        attend_back_kernel,
        grid_spec=pltpu.PrefetchScalarGridSpec(
            num_scalar_prefetch=1,
            grid=(images,),
            in_specs=[spec(0), spec(1), spec(2), spec(0)],
            out_specs=pl.BlockSpec((3, width, patches), lambda image, lengths: (0, 0, image)),
        ),
        out_shape=jax.ShapeDtypeStruct((3, width, rows), jnp.bfloat16),
        compiler_params=pltpu.CompilerParams(vmem_limit_bytes=48 * 1024 * 1024),
        cost_estimate=pl.CostEstimate(flops=10 * rows * patches * width, bytes_accessed=14 * rows * width, transcendentals=0),
    )(lengths, qkv, qkv, qkv, upstream).reshape(3 * width, rows)


def across(values, axes):
    return lax.all_gather(values, axes, axis=0, tiled=True)


def gather_weight(piece):
    return across(piece, ("dp", "mp"))


def reduce_weight(partial):
    piece = lax.psum_scatter(partial, ("dp", "mp"), scatter_dimension=0, tiled=True)
    return across(piece, "dp")


def body(
    latents,
    noise_draw,
    alpha_bar,
    timesteps,
    labels,
    lengths,
    class_vectors,
    embedder,
    time_first,
    time_second,
    modulator,
    mixer_input,
    mixer_output,
    expander,
    contractor,
    finisher,
    readout,
    row_states,
    column_states,
):
    copies = lax.axis_size("dp")
    groups = lax.axis_size("mp")
    copy = lax.axis_index("dp")
    member = lax.axis_index("mp")
    width = embedder.shape[1]
    patches = SIDE * SIDE
    images = latents.shape[0]
    rows = images * patches
    heads = width // HD
    heads_here = mixer_input.shape[1] // (3 * HD)
    hidden_here = expander.shape[1]
    valid_total = jnp.sum(lengths).astype(jnp.float32) * PIN
    own_lengths = lax.dynamic_slice_in_dim(lengths, (copy * groups + member) * images, images)
    own_alpha = lax.dynamic_slice_in_dim(alpha_bar, member * images, images)

    mixer_rows = (
        mixer_input.astype(jnp.bfloat16)
        .T.reshape(heads_here, 3, HD, width)
        .transpose(1, 0, 2, 3)
        .reshape(3 * heads_here * HD, width)
    )
    shards = (
        jnp.concatenate([mixer_rows, mixer_output.astype(jnp.bfloat16)], axis=0),
        expander.astype(jnp.bfloat16).T,
        contractor.astype(jnp.bfloat16),
    )
    gathered = []
    for slot, shard in enumerate(shards):
        piece_rows = shard.shape[0] // copies
        piece = lax.dynamic_slice_in_dim(shard, copy * piece_rows, piece_rows)
        gathered.append(gather_pieces(piece, 8) if slot == 0 else gather_weight(piece))
    parts = copies // 4
    piece_rows = shards[0].shape[0] // copies
    mixer_all = (
        gathered[0]
        .reshape(4, parts, groups, piece_rows, width)
        .transpose(0, 2, 1, 3, 4)
        .reshape(4 * width, width)
    )
    inputs_use = mixer_all[: 3 * width]
    outputs_use = mixer_all[3 * width :]
    expand_use = gathered[1]
    contract_use = gathered[2]

    group_images = groups * images
    asked = jnp.stack([timesteps, labels]).astype(jnp.float32)
    asked = jnp.pad(asked, ((0, 6), (0, 128 - group_images)))
    asked = swap(asked, "dp", 1, per_target=False)[:, :2, :group_images]
    steps_all, labels_all = asked.transpose(1, 0, 2).reshape(2, copies * group_images).astype(jnp.int32)
    features = time_features(steps_all, FREQ)
    class_rows = jnp.take(class_vectors, labels_all, axis=0).astype(jnp.float32)
    hidden_pre = jnp.dot(features, time_first, precision=highest)
    condition = jnp.dot(jax.nn.silu(hidden_pre), time_second, precision=highest) + class_rows
    signal_all = jax.nn.silu(condition).astype(jnp.bfloat16)
    signal = lax.dynamic_slice_in_dim(signal_all, copy * group_images, group_images)
    mods_low = jnp.concatenate(
        [modulator.astype(jnp.bfloat16), finisher.astype(jnp.bfloat16)], axis=1
    )
    steer_here, final_here = modulator.shape[1], finisher.shape[1]
    mods_part = product(signal, mods_low)
    mods_part = lax.reduce_precision(mods_part, 8, 7)
    mods_own = swap(mods_part.reshape(groups, -1, 128), "mp", 2)
    mods_own = mods_own.reshape(groups, images, steer_here + final_here).transpose(1, 0, 2)
    steering = mods_own[:, :, :steer_here].reshape(images, 6, 1, width)
    final_steer = mods_own[:, :, steer_here:].reshape(images, 2, 1, width)

    embedder_low = embedder.astype(jnp.bfloat16)
    readout_low = readout.astype(jnp.bfloat16)
    place = jnp.arange(patches)
    live = place[None, :] < own_lengths[:, None]
    root_keep = jnp.sqrt(own_alpha)[:, None, None]
    root_noise = jnp.sqrt(1.0 - own_alpha)[:, None, None]
    noisy = (root_keep * latents + root_noise * noise_draw).astype(jnp.bfloat16).reshape(rows, PIN)
    target = (root_keep * noise_draw - root_noise * latents).reshape(rows, PIN)
    residual_zero = (
        product(noisy, embedder_low).reshape(images, patches, width)
        + position_table(SIDE, width)[None]
    )
    normed_one = layer_norm(residual_zero)
    input_one = (
        (normed_one * (1.0 + steering[:, 1]) + steering[:, 0])
        .astype(jnp.bfloat16)
        .reshape(rows, width)
    )
    qkv = product_right(inputs_use, input_one).astype(jnp.bfloat16)
    mixed = attend(qkv, own_lengths, images)
    branch_one = product_left(mixed, outputs_use).reshape(images, patches, width)
    residual_one = residual_zero + steering[:, 2] * branch_one
    normed_two = layer_norm(residual_one)
    input_two = (
        (normed_two * (1.0 + steering[:, 4]) + steering[:, 3])
        .astype(jnp.bfloat16)
        .reshape(rows, width)
    )
    pre_active = product_right(input_two, expand_use)
    active = jax.nn.gelu(pre_active, approximate=True).astype(jnp.bfloat16)
    branch_two = product(active, contract_use).reshape(images, patches, width)
    residual_two = residual_one + steering[:, 5] * branch_two
    normed_final = layer_norm(residual_two)
    input_final = (
        (normed_final * (1.0 + final_steer[:, 1]) + final_steer[:, 0])
        .astype(jnp.bfloat16)
        .reshape(rows, width)
    )
    misfit = product(input_final, readout_low) - target
    live_rows = live.reshape(rows, 1)
    loss_part = jnp.sum(jnp.where(live_rows, misfit * misfit, 0.0))

    output_grad = jnp.where(live_rows, 2.0 * misfit / valid_total, 0.0).astype(jnp.bfloat16)
    readout_part = product_left(output_grad, input_final)
    final_grad = product_right(output_grad, readout_low).reshape(images, patches, width)
    final_shift_grad = jnp.sum(final_grad, axis=1)
    final_scale_grad = jnp.sum(final_grad * normed_final, axis=1)
    grad_residual = norm_back(residual_two, final_grad * (1.0 + final_steer[:, 1]))
    gate_two_grad = jnp.sum(grad_residual * branch_two, axis=1)
    branch_two_grad = (steering[:, 5] * grad_residual).astype(jnp.bfloat16).reshape(rows, width)
    contract_part = product_left(active, branch_two_grad).astype(jnp.bfloat16)
    active_grad = product_right(branch_two_grad, contract_use)
    gelu_pull = jax.vjp(lambda inner: jax.nn.gelu(inner, approximate=True), pre_active)[1]
    pre_grad = gelu_pull(active_grad)[0].astype(jnp.bfloat16)
    expand_part = product_left(pre_grad, input_two).astype(jnp.bfloat16)
    input_two_grad = product(pre_grad, expand_use).reshape(images, patches, width)
    shift_two_grad = jnp.sum(input_two_grad, axis=1)
    scale_two_grad = jnp.sum(input_two_grad * normed_two, axis=1)
    grad_residual = grad_residual + norm_back(
        residual_one, input_two_grad * (1.0 + steering[:, 4])
    )
    gate_one_grad = jnp.sum(grad_residual * branch_one, axis=1)
    branch_one_grad = (steering[:, 2] * grad_residual).astype(jnp.bfloat16).reshape(rows, width)
    outputs_part = product(mixed, branch_one_grad).astype(jnp.bfloat16)
    mixed_grad = product_right(outputs_use, branch_one_grad).astype(jnp.bfloat16)
    qkv_grad = attend_back(qkv, mixed_grad, own_lengths, images)
    inputs_part = product(qkv_grad, input_one).astype(jnp.bfloat16)
    input_one_grad = product_left(qkv_grad, inputs_use).reshape(images, patches, width)
    shift_one_grad = jnp.sum(input_one_grad, axis=1)
    scale_one_grad = jnp.sum(input_one_grad * normed_one, axis=1)
    grad_residual = grad_residual + norm_back(
        residual_zero, input_one_grad * (1.0 + steering[:, 1])
    )
    embed_part = product_left(noisy, grad_residual.reshape(rows, width).astype(jnp.bfloat16))

    mixer_part = jnp.concatenate([inputs_part, outputs_part], axis=0)
    mixer_part = (
        mixer_part.reshape(4, groups, parts, piece_rows, width)
        .transpose(0, 2, 1, 3, 4)
        .reshape(4 * width, width)
    )
    steer_back = jnp.stack(
        [
            shift_one_grad,
            scale_one_grad,
            gate_one_grad,
            shift_two_grad,
            scale_two_grad,
            gate_two_grad,
        ],
        axis=1,
    )
    steer_back = lax.reduce_precision(steer_back.reshape(images, 6 * width), 8, 7)
    final_back = jnp.stack([final_shift_grad, final_scale_grad], axis=1)
    final_back = lax.reduce_precision(final_back.reshape(images, 2 * width), 8, 7)
    back = jnp.concatenate(
        [
            steer_back.reshape(images, groups, steer_here),
            final_back.reshape(images, groups, final_here),
        ],
        axis=2,
    )
    back = back.transpose(1, 0, 2)
    shared = slabs(
        jnp.concatenate([embed_part.reshape(-1), readout_part.reshape(-1), loss_part[None]]),
        copies * groups,
    )
    contract_sum = reduce_weight(contract_part)
    expand_piece = lax.psum_scatter(
        expand_part, ("dp", "mp"), scatter_dimension=0, tiled=True
    )
    (mixer_sum,), cols_all, shared, signal_grad = reduce_weights(
        [mixer_part], back, mods_low, shared, 3
    )
    held = heads_here * HD
    inputs_sum = (
        mixer_sum[: 3 * held]
        .reshape(3, heads_here, HD, width)
        .transpose(1, 0, 2, 3)
        .reshape(3 * held, width)
    )
    outputs_sum = mixer_sum[3 * held :]
    cols_all = cols_all.astype(jnp.bfloat16).reshape(copies * group_images, -1)
    shared = shared.reshape(-1)
    embed_sum = shared[: embedder.size].reshape(embedder.shape)
    readout_sum = shared[embedder.size : embedder.size + readout.size].reshape(-1, width)
    loss_sum = shared[embedder.size + readout.size]
    signal_grad = signal_grad.reshape(copies * group_images, width)
    expand_sum = across(jnp.where(loss_sum >= 0.0, expand_piece, 0.0), "dp")
    modulator_sum = product_left(cols_all[:, :steer_here], signal_all)
    finisher_sum = product_left(cols_all[:, steer_here:], signal_all)
    hidden, hidden_pull = jax.vjp(jax.nn.silu, hidden_pre)
    condition_grad = jax.vjp(jax.nn.silu, condition)[1](signal_grad)[0]
    time_second_sum = lax.dot_general(
        hidden, condition_grad, (((0,), (0,)), ((), ())), precision=highest
    )
    hidden_grad = hidden_pull(
        lax.dot_general(condition_grad, time_second, (((1,), (1,)), ((), ())), precision=highest)
    )[0]
    time_first_sum = lax.dot_general(
        features, hidden_grad, (((0,), (0,)), ((), ())), precision=highest
    )

    gradients = (
        embed_sum,
        time_first_sum,
        time_second_sum,
        modulator_sum,
        inputs_sum,
        outputs_sum,
        expand_sum,
        contract_sum,
        finisher_sum,
        readout_sum,
    )
    weights = (
        embedder,
        time_first,
        time_second,
        modulator.T,
        mixer_input.T,
        mixer_output,
        expander.T,
        contractor,
        finisher.T,
        readout.T,
    )
    layouts = ("whole",) * 3 + ("rows",) * 6 + ("whole",)
    flipped = (False, False, False, True, True, False, True, False, True, True)
    ends = {"row": 0, "column": 0}
    row_parts = []
    column_parts = []
    whole_rows = []
    for weight, layout, flip in zip(weights, layouts, flipped):
        count = weight.shape[0]
        many = count * (groups if layout == "rows" else 1)
        own, other = ("column", "row") if flip else ("row", "column")
        states = {"row": row_states, "column": column_states}
        start = ends[own] + (member * count if layout == "rows" else 0)
        part = lax.dynamic_slice_in_dim(states[own], start, count)
        row_parts.append(jnp.pad(part, (0, width - count), constant_values=1.0))
        column_parts.append(states[other][ends[other] : ends[other] + width])
        if layout == "rows" and not flip:
            whole_rows.append(states[own][ends[own] : ends[own] + many].reshape(-1, width))
        ends[own] += many
        ends[other] += width
    row_old = jnp.concatenate([jnp.stack(row_parts)] + whole_rows)
    column_old = jnp.stack(column_parts)
    found = scales(gradients, row_old, column_old, layouts, flipped, 6)
    next_list, clipped_list, row_stats, column_stats = apply_scales(
        gradients, weights, found, layouts, flipped
    )
    next_list = [part.T if flip else part for part, flip in zip(next_list, flipped)]
    clipped_list = [part.T if flip else part for part, flip in zip(clipped_list, flipped)]
    return (
        loss_sum,
        valid_total,
        found[5][0, 0],
        *next_list,
        *clipped_list,
        row_stats,
        column_stats,
    )


def solution(mesh):
    in_specs = (
        P(("dp", "mp"), None, None),
        P(("dp", "mp"), None, None),
        P("dp"),
        P("dp"),
        P("dp"),
        P(),
        P(),
        P(),
        P(),
        P(),
        P(None, "mp"),
        P(None, "mp"),
        P("mp", None),
        P(None, "mp"),
        P("mp", None),
        P(None, "mp"),
        P(),
        P(),
        P(),
    )
    out_specs = (
        P(),
        P(),
        P(),
        P(),
        P(),
        P(),
        P(None, "mp"),
        P(None, "mp"),
        P("mp", None),
        P(None, "mp"),
        P("mp", None),
        P(None, "mp"),
        P(),
        P(),
        P(),
        P(),
        P(None, "mp"),
        P(None, "mp"),
        P("mp", None),
        P(None, "mp"),
        P("mp", None),
        P(None, "mp"),
        P(),
        P(),
        P(),
    )
    return jax.shard_map(body, mesh=mesh, in_specs=in_specs, out_specs=out_specs, check_vma=False)
```

```python
import functools
import math

import jax
import jax.numpy as jnp
from jax import lax
from jax.experimental import pallas as pl
from jax.experimental.pallas import tpu as pltpu
from jax.sharding import PartitionSpec as P

HD = 72
FREQ = 256
PIN = 16
SIDE = 16


eps_norm = 1e-06
eps_factor = 1e-30
clip_limit = 0.005
state_decay = 0.5
step_rate = 1.5
neg_large = -1e30
highest = lax.Precision.HIGHEST
MESH = pl.DeviceIdType.MESH


def product(operand, other_operand):
    return jnp.dot(operand, other_operand, preferred_element_type=jnp.float32)


def product_right(operand, other_operand):
    return lax.dot_general(
        operand, other_operand, (((1,), (1,)), ((), ())), preferred_element_type=jnp.float32
    )


def product_left(operand, other_operand):
    return lax.dot_general(
        operand, other_operand, (((0,), (0,)), ((), ())), preferred_element_type=jnp.float32
    )


def layer_norm(values):
    center = values - jnp.mean(values, axis=-1, keepdims=True)
    return center * lax.rsqrt(jnp.mean(center * center, axis=-1, keepdims=True) + eps_norm)


def norm_back(values, upstream):
    center = values - jnp.mean(values, axis=-1, keepdims=True)
    inverse = lax.rsqrt(jnp.mean(center * center, axis=-1, keepdims=True) + eps_norm)
    normed = center * inverse
    return inverse * (
        upstream
        - jnp.mean(upstream, axis=-1, keepdims=True)
        - normed * jnp.mean(upstream * normed, axis=-1, keepdims=True)
    )


def position_table(side, width):
    quarter = width // 4
    omega = jnp.exp(-math.log(10000.0) * jnp.arange(quarter, dtype=jnp.float32) / quarter)
    place = jnp.arange(side * side)
    column = (place % side).astype(jnp.float32)[:, None] * omega[None, :]
    row_angle = (place // side).astype(jnp.float32)[:, None] * omega[None, :]
    return jnp.concatenate(
        [jnp.sin(column), jnp.cos(column), jnp.sin(row_angle), jnp.cos(row_angle)], axis=1
    )


def time_features(steps, width):
    half = width // 2
    freq = jnp.exp(-math.log(10000.0) * jnp.arange(half, dtype=jnp.float32) / half)
    angle = steps.astype(jnp.float32)[:, None] * freq[None, :]
    return jnp.concatenate([jnp.cos(angle), jnp.sin(angle)], axis=1)


def peers(span):
    dp, mp = lax.axis_index("dp"), lax.axis_index("mp")
    copies, groups = lax.axis_size("dp"), lax.axis_size("mp")
    if span == "mp":
        return mp, groups, lambda place: (dp, place)
    if span == "dp":
        return dp, copies, lambda place: (place, mp)
    return dp * groups + mp, copies * groups, lambda place: (place // groups, lax.rem(place, groups))


def greet(span):
    here, size, device = peers(span)
    barrier = pltpu.get_barrier_semaphore()

    @pl.loop(1, size)
    def _(step):
        pl.semaphore_signal(
            barrier,
            inc=1,
            device_id=device(lax.rem(here + step, size)),
            device_id_type=MESH,
        )

    pl.semaphore_wait(barrier, size - 1)


def to_all(span, pick, landing, send_sems, recv_sems):
    here, size, device = peers(span)

    def copy(step):
        place = lax.rem(here + step, size)
        return pltpu.make_async_remote_copy(
            src_ref=pick(place),
            dst_ref=landing(here),
            send_sem=send_sems.at[step],
            recv_sem=recv_sems.at[step],
            device_id=device(place),
            device_id_type=MESH,
        )

    @pl.loop(1, size)
    def _(step):
        copy(step).start()

    def wait():
        @pl.loop(1, size)
        def _(step):
            copy(step).wait()

    return wait


def sum_over(ref):
    return lax.fori_loop(1, ref.shape[0], lambda index, total: total + ref[index], ref[0])


def swap_kernel(span, per_target, groups, x_ref, out_ref, send_sems, recv_sems):
    here, _, _ = peers(span)

    def pick(place):
        return x_ref.at[lax.rem(place, groups)] if per_target else x_ref

    greet(span)
    wait = to_all(span, pick, lambda place: out_ref.at[place], send_sems, recv_sems)
    out_ref[here] = x_ref[lax.rem(here, groups)] if per_target else x_ref[...]
    wait()


def group_size(span):
    sizes = {"dp": lax.axis_size("dp"), "mp": lax.axis_size("mp")}
    return sizes.get(span, sizes["dp"] * sizes["mp"])


def call(kernel, inputs, out_shapes, scratch, collective_id):
    return pl.pallas_call(
        kernel,
        out_shape=[jax.ShapeDtypeStruct(shape, jnp.float32) for shape in out_shapes],
        in_specs=[pl.BlockSpec(memory_space=pltpu.VMEM)] * len(inputs),
        out_specs=[pl.BlockSpec(memory_space=pltpu.VMEM)] * len(out_shapes),
        scratch_shapes=scratch,
        compiler_params=pltpu.CompilerParams(
            collective_id=collective_id, has_side_effects=True, vmem_limit_bytes=32 * 1024 * 1024
        ),
    )(*inputs)


def swap(values, span, collective_id, per_target=True):
    size = group_size(span)
    slab = values.shape[-2:]
    (result,) = call(
        functools.partial(swap_kernel, span, per_target, lax.axis_size("mp")),
        [values],
        [(size,) + slab],
        [pltpu.SemaphoreType.DMA((size,)), pltpu.SemaphoreType.DMA((size,))],
        collective_id,
    )
    return result


def slabs(flat, blocks):
    chunk = 1024 * blocks
    short = (-flat.shape[0]) % chunk
    return jnp.pad(flat, (0, short)).reshape(blocks, -1, 128)


def reduce_kernel(counts, *refs):
    copies, groups = counts
    lines = {"a": 4, "b": groups // 4, "y": copies // 2}
    chunks = (len(refs) - 27) // 2
    parts = refs[:chunks]
    back_ref, low_ref, shared_ref, features_ref, hidden_ref, condition_ref, second_ref = refs[
        chunks : chunks + 7
    ]
    outs = refs[chunks + 7 : 2 * chunks + 7]
    cols_out, shared_out, first_out, second_out = refs[2 * chunks + 7 : 2 * chunks + 11]
    held, twin, first_b, first_y, second, third, send_sems, recv_sems = refs[
        2 * chunks + 11 : 2 * chunks + 19
    ]
    (
        shared_land,
        signal_land,
        signal_part,
        stack,
        side_sends,
        side_recvs,
        signal_out,
        later_grad,
    ) = refs[2 * chunks + 19 :]
    splits = parts[0].shape[4]
    dp, mp = lax.axis_index("dp"), lax.axis_index("mp")
    at = {"a": mp // lines["b"], "b": lax.rem(mp, lines["b"]), "y": dp // 2}
    core = lax.rem(dp, 2)

    def device(**moved):
        place = {**at, "core": core, **moved}
        return (place["y"] * 2 + place["core"], place["a"] * lines["b"] + place["b"])

    greet("all")

    here = dp * groups + mp
    waits = []

    def side(slot, span, pick, landing):
        waits.append(to_all(span, pick, landing, side_sends.at[slot], side_recvs.at[slot]))

    def side_start():
        side(0, "all", lambda place: back_ref.at[lax.rem(place, groups)], cols_out_at)
        side(1, "all", lambda place: shared_ref.at[place], lambda place: shared_land.at[place])
        cols_out[here] = back_ref[mp]
        shared_land[here] = shared_ref[here]

    def cols_out_at(place):
        return cols_out.at[place]

    def side_signal():
        waits[0]()
        images = cols_out.shape[1]
        stack[...] = jnp.zeros_like(stack)
        for member in range(groups):
            stack[8 * member : 8 * member + images] = cols_out[dp * groups + member]
        found = product(stack[...].astype(jnp.bfloat16), low_ref[...])
        for member in range(groups):
            signal_part[member] = found[8 * member : 8 * member + images]
        signal_land[mp] = signal_part[mp]
        side(2, "mp", lambda place: signal_part.at[place], lambda place: signal_land.at[place])

    def side_show():
        waits[1]()
        shared_out[here] = sum_over(shared_land)
        side(3, "all", lambda place: shared_out.at[here], lambda place: shared_out.at[place])
        waits[2]()
        signal_out[here] = sum_over(signal_land)
        side(4, "all", lambda place: signal_out.at[here], lambda place: signal_out.at[place])

    def silu_slope(values):
        gate = lax.logistic(values)
        return gate * (1.0 + values * (1.0 - gate))

    def exact(left, right, dims):
        return lax.dot_general(
            left, right, (dims, ((), ())), precision=highest, preferred_element_type=jnp.float32
        )

    def side_second():
        waits[4]()
        images = signal_out.shape[1]
        for device_ in range(copies * groups):
            later_grad[device_ * images : (device_ + 1) * images] = signal_out[device_]
        later_grad[...] = later_grad[...] * silu_slope(condition_ref[...])
        hidden = hidden_ref[...]
        second_out[...] = exact(hidden * lax.logistic(hidden), later_grad[...], ((0,), (0,)))

    def side_hidden():
        back = exact(later_grad[...], second_ref[...], ((1,), (1,)))
        later_grad[...] = back * silu_slope(hidden_ref[...])

    def side_first():
        first_out[...] = exact(features_ref[...], later_grad[...], ((0,), (0,)))

    def side_end():
        waits[3]()

    units = [(chunk, split) for chunk in range(chunks) for split in range(splits)]
    slots = {}

    def sems(unit, name):
        slot = slots.setdefault(name, len(slots))
        return send_sems.at[unit, slot], recv_sems.at[unit, slot]

    def add_into(target, source):
        @pl.loop(0, target.shape[0])
        def _(index):
            target[index] = target[index] + source[index]

    def twin_copy(unit):
        chunk, split = units[unit]
        send, recv = sems(unit, "twin")
        return pltpu.make_async_remote_copy(
            src_ref=parts[chunk].at[:, 1 - core, :, :, split],
            dst_ref=twin.at[unit],
            send_sem=send,
            recv_sem=recv,
            device_id=device(core=1 - core),
            device_id_type=MESH,
        )

    def held_copy(unit):
        chunk, split = units[unit]
        return pltpu.make_async_copy(
            parts[chunk].at[:, core, :, :, split], held.at[unit], sems(unit, "held")[1]
        )

    def line_steps(unit, axis, name, pick, landing):
        size, here = lines[axis], at[axis]
        tasks = []

        def slot_of(up, hop):
            return 0 if size == 2 else hop - 1 + (size - 1 if up else 0)

        def copy(up, hop):
            target = here + hop if up else here - hop
            send, recv = sems(unit, (name, up, hop))
            slot = slot_of(up, hop)
            safe = lax.rem(target + size, size)
            beside = here + 1 if up else here - 1
            beside = lax.rem(beside + size, size)
            return pltpu.make_async_remote_copy(
                src_ref=pick(safe),
                dst_ref=landing(slot),
                send_sem=send,
                recv_sem=recv,
                device_id=device(**{axis: beside}),
                device_id_type=MESH,
            )

        def sends(up, hop):
            return here + hop <= size - 1 if up else here - hop >= 0

        def arrives(up, hop):
            if up:
                return (here >= 1) & (here + hop - 1 <= size - 1)
            return (here <= size - 2) & (here - hop + 1 >= 0)

        def take(up, hop):
            @pl.when(arrives(up, hop))
            def _():
                copy(up, hop).wait_recv()
                slot = slot_of(up, hop)
                target = here + hop - 1 if up else here - hop + 1
                add_into(pick(lax.rem(target + size, size)), landing(slot))

        def give(up, hop):
            @pl.when(sends(up, hop))
            def _():
                copy(up, hop).start()

        def finish(up, hop):
            @pl.when(sends(up, hop))
            def _():
                copy(up, hop).wait_send()

        for hop in range(size - 1, 0, -1):

            def begin(hop=hop):
                for up in (True, False):
                    if hop < size - 1:
                        take(up, hop + 1)
                    give(up, hop)

            tasks.append(begin)

        def close():
            for up in (True, False):
                take(up, 1)

        def drain():
            for hop in range(1, size):
                for up in (True, False):
                    finish(up, hop)

        return tasks, close, drain

    def unit_tasks(unit):
        chunk, split = units[unit]
        block = held.at[unit]
        halves = []
        drains = []
        for half, order in ((0, ("b", "y")), (1, ("y", "b"))):
            rows_a = pl.ds(2 * half, 2)

            def pick_one(target, axis=order[0], rows_a=rows_a):
                if axis == "b":
                    return block.at[:, rows_a, target]
                return block.at[target, rows_a]

            def pick_two(target, axis=order[1], rows_a=rows_a):
                if axis == "b":
                    return block.at[at["y"], rows_a, target]
                return block.at[target, rows_a, at["b"]]

            one = line_steps(
                unit,
                order[0],
                ("one", half),
                pick_one,
                lambda slot, axis=order[0]: (first_b if axis == "b" else first_y).at[unit, slot],
            )
            two = line_steps(
                unit,
                order[1],
                ("two", half),
                pick_two,
                lambda slot, half=half: second.at[unit, half, slot],
            )
            steps = list(one[0])
            joined = two[0][0]

            def pass_on(close=one[1], go=joined):
                close()
                go()

            steps += [pass_on] + list(two[0][1:])
            halves.append((steps, two[1]))
            drains += [one[2], two[2]]
        last = line_steps(
            unit,
            "a",
            "last",
            lambda target: block.at[at["y"], target, pl.ds(at["b"], 1)],
            lambda slot: third.at[unit, slot],
        )
        drains.append(last[2])
        out = outs[chunk]

        def spread_copy(owner, to):
            send, recv = sems(unit, ("spread", owner[2], to[2]))
            return pltpu.make_async_remote_copy(
                src_ref=out.at[owner[0], owner[1], split],
                dst_ref=out.at[owner[0], owner[1], split],
                send_sem=send,
                recv_sem=recv,
                device_id=device(y=to[0], core=to[1]),
                device_id_type=MESH,
            )

        size_y = lines["y"]
        me = (at["y"], core, 0)
        twin_place = (at["y"], 1 - core, "twin")

        def far(step):
            return (lax.rem(at["y"] + step, size_y), core, step)

        def start():
            held_copy(unit).wait()
            twin_copy(unit).wait_recv()

            @pl.loop(0, block.shape[0])
            def _(row):
                @pl.loop(0, block.shape[1])
                def _(group):
                    block[row, group] = block[row, group] + twin[unit, row, group]

            for steps, _ in halves:
                steps[0]()

        tasks = [start]
        for index in range(1, len(halves[0][0])):

            def middle(index=index):
                for steps, _ in halves:
                    steps[index]()

            tasks.append(middle)

        def to_last():
            for _, close in halves:
                close()
            last[0][0]()

        tasks.append(to_last)
        tasks += list(last[0][1:])

        def sum_done():
            last[1]()
            out[at["y"], core, split] = block[at["y"], at["a"], at["b"]]
            for step in range(1, size_y):
                spread_copy(me, far(step)).start()
            spread_copy(me, twin_place).start()

        tasks.append(sum_done)

        def before(step):
            return (lax.rem(at["y"] + size_y - step, size_y), core, step)

        def forward():
            for step in range(1, size_y):
                spread_copy((at["y"], core, 0), far(step)).wait_recv()
                source = before(step)
                spread_copy(source, twin_place).start()

        tasks.append(forward)

        def end():
            spread_copy(me, twin_place).wait()
            for step in range(1, size_y):
                spread_copy(before(step), twin_place).wait()
                spread_copy(me, far(step)).wait_send()
            twin_copy(unit).wait_send()
            for drain in drains:
                drain()

        tasks.append(end)
        return tasks

    for unit in range(len(units)):
        twin_copy(unit).start()
        held_copy(unit).start()
    side_start()
    queues = [unit_tasks(unit) for unit in range(len(units))]
    depth = len(queues[0])
    for tick in range(len(units) + depth - 1):
        for unit in reversed(range(len(units))):
            task = tick - unit
            if 0 <= task < depth:
                queues[unit][task]()
        if tick == 1:
            side_signal()
        if tick == 3:
            side_show()
        if tick == 6:
            side_second()
        if tick == 7:
            side_hidden()
        if tick == 8:
            side_first()
    side_end()


def reduce_weights(partials, sides, collective_id):
    copies, groups = lax.axis_size("dp"), lax.axis_size("mp")
    back, _, shared, features, _, condition, _ = sides
    rows, width = partials[0].shape
    size_b, size_y = groups // 4, copies // 2
    piece = rows // (copies * groups)
    share = 48 if piece % 48 == 0 else piece
    splits = piece // share
    shaped = [
        part.reshape(size_y, 2, 4, size_b, splits, share, width) for part in partials
    ]
    units = splits * len(partials)
    slab = (share, width)
    slots_b = 1 if size_b == 2 else 2 * (size_b - 1)
    slots_y = 1 if size_y == 2 else 2 * (size_y - 1)
    scratch = [
        pltpu.VMEM((units, size_y, 4, size_b) + slab, jnp.bfloat16),
        pltpu.VMEM((units, size_y, 4, size_b) + slab, jnp.bfloat16),
        pltpu.VMEM((units, slots_b, size_y, 2) + slab, jnp.bfloat16),
        pltpu.VMEM((units, slots_y, 2, size_b) + slab, jnp.bfloat16),
        pltpu.VMEM((units, 2, max(slots_b, slots_y), 2) + slab, jnp.bfloat16),
        pltpu.VMEM((units, 6, 1) + slab, jnp.bfloat16),
        pltpu.SemaphoreType.DMA((units, 40)),
        pltpu.SemaphoreType.DMA((units, 40)),
        pltpu.VMEM(shared.shape, jnp.float32),
        pltpu.VMEM((groups, back.shape[1], width), jnp.float32),
        pltpu.VMEM((groups, back.shape[1], width), jnp.float32),
        pltpu.VMEM((8 * groups, back.shape[2]), jnp.float32),
        pltpu.SemaphoreType.DMA((5, copies * groups)),
        pltpu.SemaphoreType.DMA((5, copies * groups)),
        pltpu.VMEM((copies * groups, back.shape[1], width), jnp.float32),
        pltpu.VMEM(condition.shape, jnp.float32),
    ]
    results = pl.pallas_call(
        functools.partial(reduce_kernel, (copies, groups)),
        out_shape=[jax.ShapeDtypeStruct((size_y, 2, splits) + slab, jnp.bfloat16)] * len(partials)
        + [
            jax.ShapeDtypeStruct((copies * groups,) + back.shape[1:], jnp.float32),
            jax.ShapeDtypeStruct(shared.shape, jnp.float32),
            jax.ShapeDtypeStruct((features.shape[1], width), jnp.float32),
            jax.ShapeDtypeStruct((width, width), jnp.float32),
        ],
        in_specs=[pl.BlockSpec(memory_space=pl.ANY)] * len(partials)
        + [pl.BlockSpec(memory_space=pltpu.VMEM)] * 7,
        out_specs=[pl.BlockSpec(memory_space=pltpu.VMEM)] * (len(partials) + 4),
        scratch_shapes=scratch,
        compiler_params=pltpu.CompilerParams(
            collective_id=collective_id, has_side_effects=True, vmem_limit_bytes=62 * 1024 * 1024
        ),
    )(*shaped, *sides)
    sums = [result.reshape(copies * piece, width) for result in results[: len(partials)]]
    return sums, *results[len(partials) :]


def gather_kernel(counts, piece_ref, out_ref, send_sems, recv_sems, local_sems):
    copies, groups = counts
    size_a, size_b, size_y = 4, groups // 4, copies // 2
    splits = piece_ref.shape[0]
    dp, mp = lax.axis_index("dp"), lax.axis_index("mp")
    a, b, y, core = mp // size_b, lax.rem(mp, size_b), dp // 2, lax.rem(dp, 2)

    def device(a=a, b=b, y=y, core=core):
        return (y * 2 + core, a * size_b + b)

    def along(axis, step):
        if axis == "a":
            return device(a=lax.rem(a + step, size_a))
        if axis == "b":
            return device(b=lax.rem(b + step, size_b))
        return device(y=lax.rem(y + step, size_y))

    lines = {"a": size_a, "b": size_b, "y": size_y}
    barrier = pltpu.get_barrier_semaphore()
    pl.semaphore_signal(barrier, inc=1, device_id=device(core=1 - core), device_id_type=MESH)
    for axis, size in lines.items():
        for step in range(1, size):
            pl.semaphore_signal(
                barrier, inc=1, device_id=along(axis, step), device_id_type=MESH
            )
    pl.semaphore_wait(barrier, 1 + sum(size - 1 for size in lines.values()))
    slots = {}

    def place(split, ys, cores, as_, bs):
        return out_ref.at[ys, cores, as_, bs, split]

    def own_copy(split):
        return pltpu.make_async_copy(
            piece_ref.at[split], place(split, y, core, a, b), local_sems.at[split]
        )

    def a_copies(split):
        copies_ = []
        for step in range(1, size_a):
            slot = slots.setdefault(("a", step), len(slots))
            copies_.append(
                pltpu.make_async_remote_copy(
                    src_ref=piece_ref.at[split],
                    dst_ref=place(split, y, core, a, b),
                    send_sem=send_sems.at[split, slot],
                    recv_sem=recv_sems.at[split, slot],
                    device_id=along("a", step),
                    device_id_type=MESH,
                )
            )
        return copies_

    low, high = pl.ds(0, 2), pl.ds(2, 2)
    every_b, every_y, every_a = pl.ds(0, size_b), pl.ds(0, size_y), pl.ds(0, size_a)

    def spread(split, name, axis, source):
        copies_ = []
        for step in range(1, lines[axis]):
            slot = slots.setdefault((name, step), len(slots))
            copies_.append(
                pltpu.make_async_remote_copy(
                    src_ref=source,
                    dst_ref=source,
                    send_sem=send_sems.at[split, slot],
                    recv_sem=recv_sems.at[split, slot],
                    device_id=along(axis, step),
                    device_id_type=MESH,
                )
            )
        return copies_

    def first(split):
        return (
            spread(split, "low_b", "b", place(split, y, core, low, b)),
            spread(split, "high_y", "y", place(split, y, core, high, b)),
        )

    def second(split):
        return (
            spread(split, "low_y", "y", place(split, y, core, low, every_b)),
            spread(split, "high_b", "b", place(split, every_y, core, high, b)),
        )

    def twin(split):
        slot = slots.setdefault("twin", len(slots))
        source = place(split, every_y, core, every_a, every_b)
        return pltpu.make_async_remote_copy(
            src_ref=source,
            dst_ref=source,
            send_sem=send_sems.at[split, slot],
            recv_sem=recv_sems.at[split, slot],
            device_id=device(core=1 - core),
            device_id_type=MESH,
        )

    for split in range(splits):
        own_copy(split).start()
        for item in a_copies(split):
            item.start()

    def to_first(split):
        own_copy(split).wait()
        for item in a_copies(split):
            item.wait_recv()
        for items in first(split):
            for item in items:
                item.start()

    def to_second(split):
        for items, following in zip(first(split), second(split)):
            for item in items:
                item.wait_recv()
            for item in following:
                item.start()

    def to_twin(split):
        for items in second(split):
            for item in items:
                item.wait_recv()
        twin(split).start()

    stages = (to_first, to_second, to_twin)
    for tick in range(splits + len(stages) - 1):
        for split in reversed(range(splits)):
            if 0 <= tick - split < len(stages):
                stages[tick - split](split)
    for split in range(splits):
        twin(split).wait()
        for item in a_copies(split):
            item.wait_send()
        for items in first(split) + second(split):
            for item in items:
                item.wait_send()


def gather_pieces(piece, collective_id):
    copies, groups = lax.axis_size("dp"), lax.axis_size("mp")
    rows, width = piece.shape
    share = 48 if rows % 48 == 0 else rows
    splits = rows // share
    size_b, size_y = groups // 4, copies // 2
    sems = 4 + 2 * (size_b + size_y)
    gathered = pl.pallas_call(
        functools.partial(gather_kernel, (copies, groups)),
        out_shape=jax.ShapeDtypeStruct(
            (size_y, 2, 4, size_b, splits, share, width), jnp.bfloat16
        ),
        in_specs=[pl.BlockSpec(memory_space=pl.ANY)],
        out_specs=pl.BlockSpec(memory_space=pl.ANY),
        scratch_shapes=[
            pltpu.SemaphoreType.DMA((splits, sems)),
            pltpu.SemaphoreType.DMA((splits, sems)),
            pltpu.SemaphoreType.DMA((splits,)),
        ],
        compiler_params=pltpu.CompilerParams(collective_id=collective_id, has_side_effects=True),
    )(piece.reshape(splits, share, width))
    return gathered.reshape(copies * groups * rows, width)


def row_block(rows):
    for block in (128, 144):
        if rows % block == 0:
            return block
    return rows


def scale_kernel(layouts, flipped, *refs):
    slots = len(layouts)
    grads = refs[:slots]
    row_old, column_old = refs[slots : slots + 2]
    row_coef, column_coef, row_new, column_new, shown, norms = refs[slots + 2 : slots + 8]
    by_row, land, mine, send_sems, recv_sems = refs[slots + 8 :]
    member, groups, _ = peers("mp")
    wide = row_old.shape[1]
    lane = lax.broadcasted_iota(jnp.int32, (1, 128), 1)
    place = lax.broadcasted_iota(jnp.int32, (1, wide), 1)
    split = [slot for slot in range(slots) if layouts[slot] != "whole"]
    one = jnp.ones((1, 1), jnp.float32)

    def all_sum(values):
        return jnp.sum(jnp.sum(values, axis=1, keepdims=True), axis=0, keepdims=True)

    greet("mp")
    by_row[...] = jnp.zeros_like(by_row)
    column_sums = []
    squares = []
    for slot in range(slots):
        count, across_ = grads[slot].shape
        block = row_block(count)

        def step(index, total, slot=slot, block=block):
            at = pl.ds(pl.multiple_of(index * block, block), block)
            values = grads[slot][at, :].astype(jnp.float32)
            square = values * values
            by_row[at, :] += jnp.where(lane == slot, jnp.sum(square, axis=1, keepdims=True), 0.0)
            return total + jnp.sum(square, axis=0, keepdims=True)

        total = lax.fori_loop(0, count // block, step, jnp.zeros((1, across_), jnp.float32))
        column_sums.append(total)
        squares.append(jnp.sum(total, axis=1, keepdims=True))
    row_sums = by_row[...].T

    mine[...] = jnp.zeros_like(mine)
    for index, slot in enumerate(split):
        mine[0, index : index + 1, :] = column_sums[slot]
    mine[0, 6:7, :] = sum(squares[slot] for slot in split) * jnp.ones((1, wide), jnp.float32)
    wait = to_all(
        "mp",
        lambda place_: mine.at[0],
        lambda place_: land.at[place_],
        send_sems.at[0],
        recv_sems.at[0],
    )
    land[member] = mine[0]
    wait()
    crossed = sum_over(land)
    local_square = sum(squares[slot] for slot in range(slots) if slot not in split)
    norm = jnp.sqrt(crossed[6:7, :1] + local_square)
    factor = clip_limit / jnp.maximum(norm, clip_limit)
    factor_square = factor * factor
    norms[...] = jnp.where(lax.broadcasted_iota(jnp.int32, (8, 128), 0) == 0, norm, factor)

    averages = []
    many = []
    next_rows = []
    next_columns = []
    inverse = [jnp.ones((1, wide), jnp.float32)] * slots
    for slot, layout in enumerate(layouts):
        count, across_ = grads[slot].shape
        many_rows = count * (groups if layout == "rows" else 1)
        many_columns = across_
        many.append((many_rows, many_columns))
        row_sum = row_sums[slot : slot + 1, :]
        column_sum = column_sums[slot]
        if layout == "rows":
            column_sum = crossed[split.index(slot) : split.index(slot) + 1, :]
        row_mean = row_sum * factor_square / many_columns + eps_factor
        column_mean = column_sum * factor_square / many_rows + eps_factor
        next_row = state_decay * row_old[slot : slot + 1, :] + (1.0 - state_decay) * row_mean
        next_column = (
            state_decay * column_old[slot : slot + 1, :across_] + (1.0 - state_decay) * column_mean
        )
        if flipped[slot]:
            average = jnp.sum(next_column, axis=1, keepdims=True) / across_
        elif layout == "rows":
            first = slots + sum(
                many[other][0] // wide for other in split if other < slot and not flipped[other]
            )
            old = row_old[first : first + many_rows // wide, :]
            average = (
                state_decay * all_sum(old) / many_rows
                + (1.0 - state_decay) * jnp.sum(column_mean, axis=1, keepdims=True) / across_
            )
        else:
            average = (
                jnp.sum(jnp.where(place < count, next_row, 0.0), axis=1, keepdims=True) / many_rows
            )
        averages.append(average)
        next_rows.append(next_row)
        next_columns.append(next_column)
        row_new[slot : slot + 1, :] = next_row
        column_new[slot : slot + 1, :] = next_column
        inverse[slot] = jnp.where(place < count, 1.0 / next_row, 0.0)
    blank = jnp.zeros((128 - slots, wide), jnp.float32)
    by_row[...] = jnp.concatenate(inverse + [blank], axis=0).T

    energies = []
    for slot in range(slots):
        count, across_ = grads[slot].shape
        block = row_block(count)
        inverse_column = 1.0 / next_columns[slot]

        def step(index, total, slot=slot, block=block, inverse_column=inverse_column):
            at = pl.ds(pl.multiple_of(index * block, block), block)
            values = grads[slot][at, :].astype(jnp.float32)
            weighted = jnp.sum(values * values * inverse_column, axis=1, keepdims=True)
            return total + jnp.sum(
                jnp.where(lane == slot, by_row[at, :], 0.0) * weighted, axis=0, keepdims=True
            )

        total = lax.fori_loop(0, count // block, step, jnp.zeros((1, 128), jnp.float32))
        energies.append(
            jnp.sum(total, axis=1, keepdims=True) * factor_square * averages[slot]
        )

    mine[1, :, :] = jnp.zeros_like(mine[1])
    for index, slot in enumerate(split):
        mine[1, index : index + 1, :] = next_rows[slot]
    spread = jnp.zeros((1, wide), jnp.float32)
    for slot in split:
        spread = jnp.where(place == slot, energies[slot], spread)
    mine[1, 6:7, :] = spread
    wait = to_all(
        "mp",
        lambda place_: mine.at[1],
        lambda place_: shown.at[place_],
        send_sems.at[1],
        recv_sems.at[1],
    )
    shown[member] = mine[1]
    wait()
    spread = sum_over(shown)[6:7, :]
    coefs = []
    for slot, layout in enumerate(layouts):
        many_rows, many_columns = many[slot]
        energy = energies[slot]
        if layout != "whole":
            energy = jnp.sum(jnp.where(place == slot, spread, 0.0), axis=1, keepdims=True)
        scale_down = jnp.maximum(one, jnp.sqrt(energy / (many_rows * many_columns)))
        shrink = (
            step_rate / math.sqrt(many[slot][1 if flipped[slot] else 0]) * factor * jnp.sqrt(averages[slot]) / scale_down
        )
        coefs.append(shrink * lax.rsqrt(next_rows[slot]))
        column_coef[slot : slot + 1, :] = lax.rsqrt(next_columns[slot])
    row_coef[...] = jnp.concatenate(coefs + [blank], axis=0).T


def scales(gradients, row_old, column_old, layouts, flipped, collective_id):
    groups = lax.axis_size("mp")
    wide = row_old.shape[1]
    shape = lambda *dims: jax.ShapeDtypeStruct(dims, jnp.float32)
    vmem = pl.BlockSpec(memory_space=pltpu.VMEM)
    return pl.pallas_call(
        functools.partial(scale_kernel, layouts, flipped),
        out_shape=[
            shape(wide, 128),
            shape(16, wide),
            shape(16, wide),
            shape(16, wide),
            shape(groups, 8, wide),
            shape(8, 128),
        ],
        in_specs=[vmem] * (len(gradients) + 2),
        out_specs=[vmem] * 6,
        scratch_shapes=[
            pltpu.VMEM((wide, 128), jnp.float32),
            pltpu.VMEM((groups, 8, wide), jnp.float32),
            pltpu.VMEM((2, 8, wide), jnp.float32),
            pltpu.SemaphoreType.DMA((2, groups)),
            pltpu.SemaphoreType.DMA((2, groups)),
        ],
        compiler_params=pltpu.CompilerParams(
            collective_id=collective_id, has_side_effects=True, vmem_limit_bytes=56 * 1024 * 1024
        ),
    )(*gradients, row_old, column_old)


def apply_kernel(layouts, flipped, groups, *refs):
    slots = len(layouts)
    grads, weights = refs[:slots], refs[slots : 2 * slots]
    row_coef, column_coef, row_new, column_new, shown, norms = refs[2 * slots : 2 * slots + 6]
    rest = refs[2 * slots + 6 :]
    nexts, clips = rest[:slots], rest[slots : 2 * slots]
    row_stats, column_stats = rest[2 * slots : 2 * slots + 2]
    held, clipped = rest[2 * slots + 2 : 3 * slots + 2], rest[3 * slots + 2 : 4 * slots + 2]
    sems = rest[4 * slots + 2]
    low = [grads[slot].dtype == jnp.bfloat16 for slot in range(slots)]
    order = sorted(range(slots), key=lambda slot: -weights[slot].size)

    def weight_in(slot):
        return pltpu.make_async_copy(weights[slot], held[slot], sems.at[0, slot])

    def grad_in(slot):
        return pltpu.make_async_copy(grads[slot], clipped[slot], sems.at[1, slot])

    def weight_out(slot):
        return pltpu.make_async_copy(held[slot], nexts[slot], sems.at[2, slot])

    def grad_out(slot):
        return pltpu.make_async_copy(clipped[slot], clips[slot], sems.at[3, slot])

    for slot in order:
        weight_in(slot).start()
        if not low[slot]:
            grad_in(slot).start()

    split = [slot for slot in range(slots) if layouts[slot] != "whole"]
    ends = [0, 0]
    for slot, layout in enumerate(layouts):
        count, across_ = weights[slot].shape
        own, other = (column_stats, row_stats) if flipped[slot] else (row_stats, column_stats)
        own_end, other_end = (1, 0) if flipped[slot] else (0, 1)
        at = ends[own_end]
        if layout == "rows":
            spot = split.index(slot)
            for member in range(groups):
                own[:, at : at + count] = shown[member, spot : spot + 1, :count]
                at += count
        else:
            own[:, at : at + count] = row_new[slot : slot + 1, :count]
            at += count
        ends[own_end] = at
        other[:, ends[other_end] : ends[other_end] + across_] = column_new[slot : slot + 1, :]
        ends[other_end] += across_

    factor = norms[1:2, :1]
    for slot in order:
        count, across_ = weights[slot].shape
        block = row_block(count)
        weight_in(slot).wait()
        if not low[slot]:
            grad_in(slot).wait()
        source = grads[slot] if low[slot] else clipped[slot]
        by_column = column_coef[slot : slot + 1, :across_]

        @pl.loop(0, count // block)
        def _(index, slot=slot, block=block, source=source, by_column=by_column):
            at = pl.ds(pl.multiple_of(index * block, block), block)
            gradient = source[at, :].astype(jnp.float32)
            step_size = row_coef[at, slot : slot + 1] * by_column
            held[slot][at, :] = held[slot][at, :] - gradient * step_size
            clipped[slot][at, :] = gradient * factor

        weight_out(slot).start()
        grad_out(slot).start()
    for slot in order:
        weight_out(slot).wait()
        grad_out(slot).wait()


def apply_scales(gradients, weights, found, layouts, flipped):
    groups = lax.axis_size("mp")
    vmem = pl.BlockSpec(memory_space=pltpu.VMEM)
    stay = pl.BlockSpec(memory_space=pl.ANY)
    many_rows = 0
    many_columns = 0
    for weight, layout, flip in zip(weights, layouts, flipped):
        extents = (weight.shape[0] * (groups if layout == "rows" else 1), weight.shape[1])
        many_rows += extents[1 if flip else 0]
        many_columns += extents[0 if flip else 1]
    shapes = [jax.ShapeDtypeStruct(weight.shape, jnp.float32) for weight in weights]
    buffers = [pltpu.VMEM(weight.shape, jnp.float32) for weight in weights]
    size = sum(weight.size for weight in weights)
    results = pl.pallas_call(
        functools.partial(apply_kernel, layouts, flipped, groups),
        out_shape=shapes
        + shapes
        + [
            jax.ShapeDtypeStruct((1, many_rows), jnp.float32),
            jax.ShapeDtypeStruct((1, many_columns), jnp.float32),
        ],
        in_specs=[vmem if part.dtype == jnp.bfloat16 else stay for part in gradients]
        + [stay] * len(weights)
        + [vmem] * 6,
        out_specs=[stay] * (2 * len(weights)) + [vmem] * 2,
        scratch_shapes=buffers + buffers + [pltpu.SemaphoreType.DMA((4, len(weights)))],
        compiler_params=pltpu.CompilerParams(vmem_limit_bytes=58 * 1024 * 1024),
        cost_estimate=pl.CostEstimate(flops=4 * size, bytes_accessed=16 * size, transcendentals=0),
    )(*gradients, *weights, *found)
    count = len(weights)
    return (
        results[:count],
        results[count : 2 * count],
        results[2 * count].reshape(-1),
        results[2 * count + 1].reshape(-1),
    )


def weights_of(keys, queries, live):
    scores = product_left(keys, queries) * HD ** (-0.5)
    scores = jnp.where(live, scores, neg_large)
    exponent = jnp.exp(scores - jnp.max(scores, axis=0, keepdims=True))
    return exponent / jnp.sum(exponent, axis=0, keepdims=True)


def attend_kernel(length_ref, q_ref, k_ref, v_ref, out_ref):
    patches = q_ref.shape[1]
    pair = 2 * HD
    live = lax.broadcasted_iota(jnp.int32, (patches, patches), 0) < length_ref[pl.program_id(0)]
    upper = lax.broadcasted_iota(jnp.int32, (pair, patches), 0) < HD

    @pl.loop(0, q_ref.shape[0] // pair, unroll=4)
    def _(index):
        rows = pl.ds(pl.multiple_of(index * pair, 16), pair)
        queries, keys, values = q_ref[rows, :], k_ref[rows, :], v_ref[rows, :]
        zero = jnp.zeros_like(queries)
        mixed = []
        for half in range(2):
            own = upper if half == 0 else ~upper
            probs = weights_of(keys, jnp.where(own, queries, zero), live)
            mixed.append(product(values, probs.astype(jnp.bfloat16)))
        out_ref[rows, :] = jnp.where(upper, mixed[0], mixed[1]).astype(jnp.bfloat16)


def attend_back_kernel(length_ref, q_ref, k_ref, v_ref, up_ref, mixed_ref, down_ref):
    down_ref[3] = mixed_ref[...]
    patches = q_ref.shape[1]
    pair = 2 * HD
    live = lax.broadcasted_iota(jnp.int32, (patches, patches), 0) < length_ref[pl.program_id(0)]
    upper = lax.broadcasted_iota(jnp.int32, (pair, patches), 0) < HD

    @pl.loop(0, q_ref.shape[0] // pair, unroll=4)
    def _(index):
        rows = pl.ds(pl.multiple_of(index * pair, 16), pair)
        queries, keys, values, upstream = (
            q_ref[rows, :],
            k_ref[rows, :],
            v_ref[rows, :],
            up_ref[rows, :],
        )
        zero = jnp.zeros_like(queries)
        found = []
        for half in range(2):
            own = upper if half == 0 else ~upper
            probs = weights_of(keys, jnp.where(own, queries, zero), live)
            probs_grad = product_left(values, jnp.where(own, upstream, zero))
            weighted = probs * probs_grad
            score_grad = (
                weighted - probs * jnp.sum(weighted, axis=0, keepdims=True)
            ).astype(jnp.bfloat16)
            found.append(
                (
                    product(keys, score_grad),
                    product_right(queries, score_grad),
                    product_right(upstream, probs.astype(jnp.bfloat16)),
                )
            )
        scale = HD ** (-0.5)
        down_ref[0, rows, :] = (jnp.where(upper, found[0][0], found[1][0]) * scale).astype(jnp.bfloat16)
        down_ref[1, rows, :] = (jnp.where(upper, found[0][1], found[1][1]) * scale).astype(jnp.bfloat16)
        down_ref[2, rows, :] = jnp.where(upper, found[0][2], found[1][2]).astype(jnp.bfloat16)


def _specs(width, patches):
    def spec(block):
        return pl.BlockSpec((width, patches), lambda image, lengths: (block, image))

    return spec


def attend(qkv, lengths, images):
    width, rows = qkv.shape[0] // 3, qkv.shape[1]
    patches = rows // images
    spec = _specs(width, patches)
    return pl.pallas_call(
        attend_kernel,
        grid_spec=pltpu.PrefetchScalarGridSpec(
            num_scalar_prefetch=1,
            grid=(images,),
            in_specs=[spec(0), spec(1), spec(2)],
            out_specs=spec(0),
        ),
        out_shape=jax.ShapeDtypeStruct((width, rows), jnp.bfloat16),
        compiler_params=pltpu.CompilerParams(vmem_limit_bytes=48 * 1024 * 1024),
        cost_estimate=pl.CostEstimate(flops=4 * rows * patches * width, bytes_accessed=8 * rows * width, transcendentals=0),
    )(lengths, qkv, qkv, qkv)


def attend_back(qkv, upstream, mixed, lengths, images):
    width, rows = upstream.shape
    patches = rows // images
    spec = _specs(width, patches)
    return pl.pallas_call(
        attend_back_kernel,
        grid_spec=pltpu.PrefetchScalarGridSpec(
            num_scalar_prefetch=1,
            grid=(images,),
            in_specs=[spec(0), spec(1), spec(2), spec(0), spec(0)],
            out_specs=pl.BlockSpec((4, width, patches), lambda image, lengths: (0, 0, image)),
        ),
        out_shape=jax.ShapeDtypeStruct((4, width, rows), jnp.bfloat16),
        compiler_params=pltpu.CompilerParams(vmem_limit_bytes=48 * 1024 * 1024),
        cost_estimate=pl.CostEstimate(flops=10 * rows * patches * width, bytes_accessed=14 * rows * width, transcendentals=0),
    )(lengths, qkv, qkv, qkv, upstream, mixed)


def mixer_weights_kernel(left_ref, input_ref, branch_ref, out_ref):
    @pl.when(pl.program_id(0) < 3)
    def _():
        out_ref[...] = product(left_ref[0], input_ref[...]).astype(jnp.bfloat16)

    @pl.when(pl.program_id(0) == 3)
    def _():
        out_ref[...] = product(left_ref[0], branch_ref[...]).astype(jnp.bfloat16)


def mixer_weights(left, input_one, branch_one_grad):
    _, width, rows = left.shape
    whole = pl.BlockSpec((rows, width), lambda part: (0, 0))
    return pl.pallas_call(
        mixer_weights_kernel,
        grid=(4,),
        in_specs=[pl.BlockSpec((1, width, rows), lambda part: (part, 0, 0)), whole, whole],
        out_specs=pl.BlockSpec((width, width), lambda part: (part, 0)),
        out_shape=jax.ShapeDtypeStruct((4 * width, width), jnp.bfloat16),
        compiler_params=pltpu.CompilerParams(vmem_limit_bytes=48 * 1024 * 1024),
        cost_estimate=pl.CostEstimate(
            flops=8 * rows * width * width, bytes_accessed=20 * rows * width, transcendentals=0
        ),
    )(left, input_one, branch_one_grad)


def input_back_kernel(
    left_ref, weight_ref, residual_ref, upstream_ref, scale_ref, noisy_ref, shift_out, scale_out, embed_out
):
    _, width, patches = left_ref.shape
    grad = product_left(left_ref[...].reshape(3 * width, patches), weight_ref[...])
    values = residual_ref[...]
    normed = layer_norm(values)
    shift_out[0] = jnp.sum(grad, axis=0, keepdims=True)
    scale_out[0] = jnp.sum(grad * normed, axis=0, keepdims=True)
    residual_grad = upstream_ref[...] + norm_back(values, grad * (1.0 + scale_ref[0]))

    @pl.when(pl.program_id(0) == 0)
    def _():
        embed_out[...] = jnp.zeros_like(embed_out)

    embed_out[...] += product_left(noisy_ref[...], residual_grad.astype(jnp.bfloat16))


def input_back(left, weights, residual_zero, grad_residual, scale_one, noisy):
    _, width, rows = left.shape
    images, patches, _ = residual_zero.shape
    by_image = pl.BlockSpec((patches, width), lambda image: (image, 0))
    vector = pl.BlockSpec((1, 1, width), lambda image: (image, 0, 0))
    return pl.pallas_call(
        input_back_kernel,
        grid=(images,),
        in_specs=[
            pl.BlockSpec((3, width, patches), lambda image: (0, 0, image)),
            pl.BlockSpec((3 * width, width), lambda image: (0, 0)),
            by_image,
            by_image,
            vector,
            pl.BlockSpec((patches, noisy.shape[1]), lambda image: (image, 0)),
        ],
        out_specs=[vector, vector, pl.BlockSpec((noisy.shape[1], width), lambda image: (0, 0))],
        out_shape=[
            jax.ShapeDtypeStruct((images, 1, width), jnp.float32),
            jax.ShapeDtypeStruct((images, 1, width), jnp.float32),
            jax.ShapeDtypeStruct((noisy.shape[1], width), jnp.float32),
        ],
        compiler_params=pltpu.CompilerParams(vmem_limit_bytes=48 * 1024 * 1024),
        cost_estimate=pl.CostEstimate(
            flops=6 * rows * width * width, bytes_accessed=20 * rows * width, transcendentals=0
        ),
    )(
        left,
        weights,
        residual_zero.reshape(rows, width),
        grad_residual.reshape(rows, width),
        scale_one.reshape(images, 1, width),
        noisy,
    )


def across(values, axes):
    return lax.all_gather(values, axes, axis=0, tiled=True)


def gather_weight(piece):
    return across(piece, ("dp", "mp"))


def reduce_weight(partial):
    piece = lax.psum_scatter(partial, ("dp", "mp"), scatter_dimension=0, tiled=True)
    return across(piece, "dp")


def body(
    latents,
    noise_draw,
    alpha_bar,
    timesteps,
    labels,
    lengths,
    class_vectors,
    embedder,
    time_first,
    time_second,
    modulator,
    mixer_input,
    mixer_output,
    expander,
    contractor,
    finisher,
    readout,
    row_states,
    column_states,
):
    copies = lax.axis_size("dp")
    groups = lax.axis_size("mp")
    copy = lax.axis_index("dp")
    member = lax.axis_index("mp")
    width = embedder.shape[1]
    patches = SIDE * SIDE
    images = latents.shape[0]
    rows = images * patches
    heads = width // HD
    heads_here = mixer_input.shape[1] // (3 * HD)
    hidden_here = expander.shape[1]
    valid_total = jnp.sum(lengths).astype(jnp.float32) * PIN
    own_lengths = lax.dynamic_slice_in_dim(lengths, (copy * groups + member) * images, images)
    own_alpha = lax.dynamic_slice_in_dim(alpha_bar, member * images, images)

    mixer_rows = (
        mixer_input.astype(jnp.bfloat16)
        .T.reshape(heads_here, 3, HD, width)
        .transpose(1, 0, 2, 3)
        .reshape(3 * heads_here * HD, width)
    )
    shards = (
        jnp.concatenate([mixer_rows, mixer_output.astype(jnp.bfloat16)], axis=0),
        expander.astype(jnp.bfloat16).T,
        contractor.astype(jnp.bfloat16),
    )
    gathered = []
    for slot, shard in enumerate(shards):
        piece_rows = shard.shape[0] // copies
        piece = lax.dynamic_slice_in_dim(shard, copy * piece_rows, piece_rows)
        gathered.append(gather_pieces(piece, 8) if slot == 0 else gather_weight(piece))
    parts = copies // 4
    piece_rows = shards[0].shape[0] // copies
    mixer_all = (
        gathered[0]
        .reshape(4, parts, groups, piece_rows, width)
        .transpose(0, 2, 1, 3, 4)
        .reshape(4 * width, width)
    )
    inputs_use = mixer_all[: 3 * width]
    outputs_use = mixer_all[3 * width :]
    expand_use = gathered[1]
    contract_use = gathered[2]

    group_images = groups * images
    asked = jnp.stack([timesteps, labels]).astype(jnp.float32)
    asked = jnp.pad(asked, ((0, 6), (0, 128 - group_images)))
    asked = swap(asked, "dp", 1, per_target=False)[:, :2, :group_images]
    steps_all, labels_all = asked.transpose(1, 0, 2).reshape(2, copies * group_images).astype(jnp.int32)
    features = time_features(steps_all, FREQ)
    class_rows = jnp.take(class_vectors, labels_all, axis=0).astype(jnp.float32)
    hidden_pre = jnp.dot(features, time_first, precision=highest)
    condition = jnp.dot(jax.nn.silu(hidden_pre), time_second, precision=highest) + class_rows
    signal_all = jax.nn.silu(condition).astype(jnp.bfloat16)
    signal = lax.dynamic_slice_in_dim(signal_all, copy * group_images, group_images)
    mods_low = jnp.concatenate(
        [modulator.T.astype(jnp.bfloat16), finisher.T.astype(jnp.bfloat16)], axis=0
    )
    steer_here, final_here = modulator.shape[1], finisher.shape[1]
    mods_part = product_right(signal, mods_low)
    mods_part = lax.reduce_precision(mods_part, 8, 7)
    mods_own = swap(mods_part.reshape(groups, -1, 128), "mp", 2)
    mods_own = mods_own.reshape(groups, images, steer_here + final_here).transpose(1, 0, 2)
    steering = mods_own[:, :, :steer_here].reshape(images, 6, 1, width)
    final_steer = mods_own[:, :, steer_here:].reshape(images, 2, 1, width)

    embedder_low = embedder.astype(jnp.bfloat16)
    readout_low = readout.astype(jnp.bfloat16)
    place = jnp.arange(patches)
    live = place[None, :] < own_lengths[:, None]
    root_keep = jnp.sqrt(own_alpha)[:, None, None]
    root_noise = jnp.sqrt(1.0 - own_alpha)[:, None, None]
    noisy = (root_keep * latents + root_noise * noise_draw).astype(jnp.bfloat16).reshape(rows, PIN)
    target = (root_keep * noise_draw - root_noise * latents).reshape(rows, PIN)
    residual_zero = (
        product(noisy, embedder_low).reshape(images, patches, width)
        + position_table(SIDE, width)[None]
    )
    normed_one = layer_norm(residual_zero)
    input_one = (
        (normed_one * (1.0 + steering[:, 1]) + steering[:, 0])
        .astype(jnp.bfloat16)
        .reshape(rows, width)
    )
    qkv = product_right(inputs_use, input_one).astype(jnp.bfloat16)
    mixed = attend(qkv, own_lengths, images)
    branch_one = product_left(mixed, outputs_use).reshape(images, patches, width)
    residual_one = residual_zero + steering[:, 2] * branch_one
    normed_two = layer_norm(residual_one)
    input_two = (
        (normed_two * (1.0 + steering[:, 4]) + steering[:, 3])
        .astype(jnp.bfloat16)
        .reshape(rows, width)
    )
    pre_active = product_right(input_two, expand_use)
    active = jax.nn.gelu(pre_active, approximate=True).astype(jnp.bfloat16)
    branch_two = product(active, contract_use).reshape(images, patches, width)
    residual_two = residual_one + steering[:, 5] * branch_two
    normed_final = layer_norm(residual_two)
    input_final = (
        (normed_final * (1.0 + final_steer[:, 1]) + final_steer[:, 0])
        .astype(jnp.bfloat16)
        .reshape(rows, width)
    )
    misfit = product(input_final, readout_low) - target
    live_rows = live.reshape(rows, 1)
    loss_part = jnp.sum(jnp.where(live_rows, misfit * misfit, 0.0))

    output_grad = jnp.where(live_rows, 2.0 * misfit / valid_total, 0.0).astype(jnp.bfloat16)
    readout_part = product_left(output_grad, input_final)
    final_grad = product_right(output_grad, readout_low).reshape(images, patches, width)
    final_shift_grad = jnp.sum(final_grad, axis=1)
    final_scale_grad = jnp.sum(final_grad * normed_final, axis=1)
    grad_residual = norm_back(residual_two, final_grad * (1.0 + final_steer[:, 1]))
    gate_two_grad = jnp.sum(grad_residual * branch_two, axis=1)
    branch_two_grad = (steering[:, 5] * grad_residual).astype(jnp.bfloat16).reshape(rows, width)
    contract_part = product_left(active, branch_two_grad).astype(jnp.bfloat16)
    active_grad = product_right(branch_two_grad, contract_use)
    gelu_pull = jax.vjp(lambda inner: jax.nn.gelu(inner, approximate=True), pre_active)[1]
    pre_grad = gelu_pull(active_grad)[0].astype(jnp.bfloat16)
    expand_part = product_left(pre_grad, input_two).astype(jnp.bfloat16)
    input_two_grad = product(pre_grad, expand_use).reshape(images, patches, width)
    shift_two_grad = jnp.sum(input_two_grad, axis=1)
    scale_two_grad = jnp.sum(input_two_grad * normed_two, axis=1)
    grad_residual = grad_residual + norm_back(
        residual_one, input_two_grad * (1.0 + steering[:, 4])
    )
    gate_one_grad = jnp.sum(grad_residual * branch_one, axis=1)
    branch_one_grad = (steering[:, 2] * grad_residual).astype(jnp.bfloat16).reshape(rows, width)
    mixed_grad = product_right(outputs_use, branch_one_grad).astype(jnp.bfloat16)
    mixer_left = attend_back(qkv, mixed_grad, mixed, own_lengths, images)
    shift_one_grad, scale_one_grad, embed_part = input_back(
        mixer_left, mixer_all, residual_zero, grad_residual, steering[:, 1], noisy
    )
    shift_one_grad = shift_one_grad.reshape(images, width)
    scale_one_grad = scale_one_grad.reshape(images, width)
    mixer_part = mixer_weights(mixer_left, input_one, branch_one_grad)

    mixer_part = (
        mixer_part.reshape(4, groups, parts, piece_rows, width)
        .transpose(0, 2, 1, 3, 4)
        .reshape(4 * width, width)
    )
    steer_back = jnp.stack(
        [
            shift_one_grad,
            scale_one_grad,
            gate_one_grad,
            shift_two_grad,
            scale_two_grad,
            gate_two_grad,
        ],
        axis=1,
    )
    steer_back = lax.reduce_precision(steer_back.reshape(images, 6 * width), 8, 7)
    final_back = jnp.stack([final_shift_grad, final_scale_grad], axis=1)
    final_back = lax.reduce_precision(final_back.reshape(images, 2 * width), 8, 7)
    back = jnp.concatenate(
        [
            steer_back.reshape(images, groups, steer_here),
            final_back.reshape(images, groups, final_here),
        ],
        axis=2,
    )
    back = back.transpose(1, 0, 2)
    shared = slabs(
        jnp.concatenate([embed_part.reshape(-1), readout_part.reshape(-1), loss_part[None]]),
        copies * groups,
    )
    contract_sum = reduce_weight(contract_part)
    sides = (back, mods_low, shared, features, hidden_pre, condition, time_second)
    together = [expand_part, mixer_part] if piece_rows % 48 == 0 else [mixer_part]
    sums, cols_all, shared, time_first_sum, time_second_sum = reduce_weights(together, sides, 3)
    expand_sum = sums[0] if len(together) == 2 else reduce_weight(expand_part)
    mixer_sum = sums[-1]
    held = heads_here * HD
    inputs_sum = (
        mixer_sum[: 3 * held]
        .reshape(3, heads_here, HD, width)
        .transpose(1, 0, 2, 3)
        .reshape(3 * held, width)
    )
    outputs_sum = mixer_sum[3 * held :]
    cols_all = cols_all.astype(jnp.bfloat16).reshape(copies * group_images, -1)
    shared = shared.reshape(-1)
    embed_sum = shared[: embedder.size].reshape(embedder.shape)
    readout_sum = shared[embedder.size : embedder.size + readout.size].reshape(-1, width)
    loss_sum = shared[embedder.size + readout.size]
    modulator_sum = product_left(cols_all[:, :steer_here], signal_all)
    finisher_sum = product_left(cols_all[:, steer_here:], signal_all)
    gradients = (
        embed_sum,
        time_first_sum,
        time_second_sum,
        modulator_sum,
        inputs_sum,
        outputs_sum,
        expand_sum,
        contract_sum,
        finisher_sum,
        readout_sum,
    )
    weights = (
        embedder,
        time_first,
        time_second,
        modulator.T,
        mixer_input.T,
        mixer_output,
        expander.T,
        contractor,
        finisher.T,
        readout.T,
    )
    layouts = ("whole",) * 3 + ("rows",) * 6 + ("whole",)
    flipped = (False, False, False, True, True, False, True, False, True, True)
    ends = {"row": 0, "column": 0}
    row_parts = []
    column_parts = []
    whole_rows = []
    for weight, layout, flip in zip(weights, layouts, flipped):
        count = weight.shape[0]
        many = count * (groups if layout == "rows" else 1)
        own, other = ("column", "row") if flip else ("row", "column")
        states = {"row": row_states, "column": column_states}
        start = ends[own] + (member * count if layout == "rows" else 0)
        part = lax.dynamic_slice_in_dim(states[own], start, count)
        row_parts.append(jnp.pad(part, (0, width - count), constant_values=1.0))
        column_parts.append(states[other][ends[other] : ends[other] + width])
        if layout == "rows" and not flip:
            whole_rows.append(states[own][ends[own] : ends[own] + many].reshape(-1, width))
        ends[own] += many
        ends[other] += width
    row_old = jnp.concatenate([jnp.stack(row_parts)] + whole_rows)
    column_old = jnp.stack(column_parts)
    found = scales(gradients, row_old, column_old, layouts, flipped, 6)
    next_list, clipped_list, row_stats, column_stats = apply_scales(
        gradients, weights, found, layouts, flipped
    )
    next_list = [part.T if flip else part for part, flip in zip(next_list, flipped)]
    clipped_list = [part.T if flip else part for part, flip in zip(clipped_list, flipped)]
    return (
        loss_sum,
        valid_total,
        found[5][0, 0],
        *next_list,
        *clipped_list,
        row_stats,
        column_stats,
    )


def solution(mesh):
    in_specs = (
        P(("dp", "mp"), None, None),
        P(("dp", "mp"), None, None),
        P("dp"),
        P("dp"),
        P("dp"),
        P(),
        P(),
        P(),
        P(),
        P(),
        P(None, "mp"),
        P(None, "mp"),
        P("mp", None),
        P(None, "mp"),
        P("mp", None),
        P(None, "mp"),
        P(),
        P(),
        P(),
    )
    out_specs = (
        P(),
        P(),
        P(),
        P(),
        P(),
        P(),
        P(None, "mp"),
        P(None, "mp"),
        P("mp", None),
        P(None, "mp"),
        P("mp", None),
        P(None, "mp"),
        P(),
        P(),
        P(),
        P(),
        P(None, "mp"),
        P(None, "mp"),
        P("mp", None),
        P(None, "mp"),
        P("mp", None),
        P(None, "mp"),
        P(),
        P(),
        P(),
    )
    return jax.shard_map(body, mesh=mesh, in_specs=in_specs, out_specs=out_specs, check_vma=False)
```

```python
import functools
import math

import jax
import jax.numpy as jnp
from jax import lax
from jax.experimental import pallas as pl
from jax.experimental.pallas import tpu as pltpu
from jax.sharding import PartitionSpec as P

HD = 72
FREQ = 256
PIN = 16
SIDE = 16


eps_norm = 1e-06
eps_factor = 1e-30
clip_limit = 0.005
state_decay = 0.5
step_rate = 1.5
neg_large = -1e30
highest = lax.Precision.HIGHEST
MESH = pl.DeviceIdType.MESH


def product(operand, other_operand):
    return jnp.dot(operand, other_operand, preferred_element_type=jnp.float32)


def product_right(operand, other_operand):
    return lax.dot_general(
        operand, other_operand, (((1,), (1,)), ((), ())), preferred_element_type=jnp.float32
    )


def product_left(operand, other_operand):
    return lax.dot_general(
        operand, other_operand, (((0,), (0,)), ((), ())), preferred_element_type=jnp.float32
    )


def layer_norm(values):
    center = values - jnp.mean(values, axis=-1, keepdims=True)
    return center * lax.rsqrt(jnp.mean(center * center, axis=-1, keepdims=True) + eps_norm)


def norm_back(values, upstream):
    center = values - jnp.mean(values, axis=-1, keepdims=True)
    inverse = lax.rsqrt(jnp.mean(center * center, axis=-1, keepdims=True) + eps_norm)
    normed = center * inverse
    return inverse * (
        upstream
        - jnp.mean(upstream, axis=-1, keepdims=True)
        - normed * jnp.mean(upstream * normed, axis=-1, keepdims=True)
    )


def position_table(side, width):
    quarter = width // 4
    omega = jnp.exp(-math.log(10000.0) * jnp.arange(quarter, dtype=jnp.float32) / quarter)
    place = jnp.arange(side * side)
    column = (place % side).astype(jnp.float32)[:, None] * omega[None, :]
    row_angle = (place // side).astype(jnp.float32)[:, None] * omega[None, :]
    return jnp.concatenate(
        [jnp.sin(column), jnp.cos(column), jnp.sin(row_angle), jnp.cos(row_angle)], axis=1
    )


def time_features(steps, width):
    half = width // 2
    freq = jnp.exp(-math.log(10000.0) * jnp.arange(half, dtype=jnp.float32) / half)
    angle = steps.astype(jnp.float32)[:, None] * freq[None, :]
    return jnp.concatenate([jnp.cos(angle), jnp.sin(angle)], axis=1)


def peers(span):
    dp, mp = lax.axis_index("dp"), lax.axis_index("mp")
    copies, groups = lax.axis_size("dp"), lax.axis_size("mp")
    if span == "mp":
        return mp, groups, lambda place: (dp, place)
    if span == "dp":
        return dp, copies, lambda place: (place, mp)
    return dp * groups + mp, copies * groups, lambda place: (place // groups, lax.rem(place, groups))


def greet(span):
    here, size, device = peers(span)
    barrier = pltpu.get_barrier_semaphore()

    @pl.loop(1, size)
    def _(step):
        pl.semaphore_signal(
            barrier,
            inc=1,
            device_id=device(lax.rem(here + step, size)),
            device_id_type=MESH,
        )

    pl.semaphore_wait(barrier, size - 1)


def to_all(span, pick, landing, send_sems, recv_sems):
    here, size, device = peers(span)

    def copy(step):
        place = lax.rem(here + step, size)
        return pltpu.make_async_remote_copy(
            src_ref=pick(place),
            dst_ref=landing(here),
            send_sem=send_sems.at[step],
            recv_sem=recv_sems.at[step],
            device_id=device(place),
            device_id_type=MESH,
        )

    @pl.loop(1, size)
    def _(step):
        copy(step).start()

    def wait():
        @pl.loop(1, size)
        def _(step):
            copy(step).wait()

    return wait


def sum_over(ref):
    return lax.fori_loop(1, ref.shape[0], lambda index, total: total + ref[index], ref[0])


def swap_kernel(span, per_target, groups, x_ref, out_ref, send_sems, recv_sems):
    here, _, _ = peers(span)

    def pick(place):
        return x_ref.at[lax.rem(place, groups)] if per_target else x_ref

    greet(span)
    wait = to_all(span, pick, lambda place: out_ref.at[place], send_sems, recv_sems)
    out_ref[here] = x_ref[lax.rem(here, groups)] if per_target else x_ref[...]
    wait()


def group_size(span):
    sizes = {"dp": lax.axis_size("dp"), "mp": lax.axis_size("mp")}
    return sizes.get(span, sizes["dp"] * sizes["mp"])


def call(kernel, inputs, out_shapes, scratch, collective_id):
    return pl.pallas_call(
        kernel,
        out_shape=[jax.ShapeDtypeStruct(shape, jnp.float32) for shape in out_shapes],
        in_specs=[pl.BlockSpec(memory_space=pltpu.VMEM)] * len(inputs),
        out_specs=[pl.BlockSpec(memory_space=pltpu.VMEM)] * len(out_shapes),
        scratch_shapes=scratch,
        compiler_params=pltpu.CompilerParams(
            collective_id=collective_id, has_side_effects=True, vmem_limit_bytes=32 * 1024 * 1024
        ),
    )(*inputs)


def swap(values, span, collective_id, per_target=True):
    size = group_size(span)
    slab = values.shape[-2:]
    (result,) = call(
        functools.partial(swap_kernel, span, per_target, lax.axis_size("mp")),
        [values],
        [(size,) + slab],
        [pltpu.SemaphoreType.DMA((size,)), pltpu.SemaphoreType.DMA((size,))],
        collective_id,
    )
    return result


def slabs(flat, blocks):
    chunk = 1024 * blocks
    short = (-flat.shape[0]) % chunk
    return jnp.pad(flat, (0, short)).reshape(blocks, -1, 128)


def reduce_kernel(counts, *refs):
    copies, groups = counts
    lines = {"a": 4, "b": groups // 4, "y": copies // 2}
    chunks = (len(refs) - 27) // 2
    parts = refs[:chunks]
    back_ref, low_ref, shared_ref, features_ref, hidden_ref, condition_ref, second_ref = refs[
        chunks : chunks + 7
    ]
    outs = refs[chunks + 7 : 2 * chunks + 7]
    cols_out, shared_out, first_out, second_out = refs[2 * chunks + 7 : 2 * chunks + 11]
    held, twin, first_b, first_y, second, third, send_sems, recv_sems = refs[
        2 * chunks + 11 : 2 * chunks + 19
    ]
    (
        shared_land,
        signal_land,
        signal_part,
        stack,
        side_sends,
        side_recvs,
        signal_out,
        later_grad,
    ) = refs[2 * chunks + 19 :]
    splits = parts[0].shape[4]
    dp, mp = lax.axis_index("dp"), lax.axis_index("mp")
    at = {"a": mp // lines["b"], "b": lax.rem(mp, lines["b"]), "y": dp // 2}
    core = lax.rem(dp, 2)

    def device(**moved):
        place = {**at, "core": core, **moved}
        return (place["y"] * 2 + place["core"], place["a"] * lines["b"] + place["b"])

    greet("all")

    here = dp * groups + mp
    waits = []

    def side(slot, span, pick, landing):
        waits.append(to_all(span, pick, landing, side_sends.at[slot], side_recvs.at[slot]))

    def side_start():
        side(0, "all", lambda place: back_ref.at[lax.rem(place, groups)], cols_out_at)
        side(1, "all", lambda place: shared_ref.at[place], lambda place: shared_land.at[place])
        cols_out[here] = back_ref[mp]
        shared_land[here] = shared_ref[here]

    def cols_out_at(place):
        return cols_out.at[place]

    def side_signal():
        waits[0]()
        images = cols_out.shape[1]
        stack[...] = jnp.zeros_like(stack)
        for member in range(groups):
            stack[8 * member : 8 * member + images] = cols_out[dp * groups + member]
        found = product(stack[...].astype(jnp.bfloat16), low_ref[...])
        for member in range(groups):
            signal_part[member] = found[8 * member : 8 * member + images]
        signal_land[mp] = signal_part[mp]
        side(2, "mp", lambda place: signal_part.at[place], lambda place: signal_land.at[place])

    def side_show():
        waits[1]()
        shared_out[here] = sum_over(shared_land)
        side(3, "all", lambda place: shared_out.at[here], lambda place: shared_out.at[place])
        waits[2]()
        signal_out[here] = sum_over(signal_land)
        side(4, "all", lambda place: signal_out.at[here], lambda place: signal_out.at[place])

    def silu_slope(values):
        gate = lax.logistic(values)
        return gate * (1.0 + values * (1.0 - gate))

    def exact(left, right, dims):
        return lax.dot_general(
            left, right, (dims, ((), ())), precision=highest, preferred_element_type=jnp.float32
        )

    def side_second():
        waits[4]()
        images = signal_out.shape[1]
        for device_ in range(copies * groups):
            later_grad[device_ * images : (device_ + 1) * images] = signal_out[device_]
        later_grad[...] = later_grad[...] * silu_slope(condition_ref[...])
        hidden = hidden_ref[...]
        second_out[...] = exact(hidden * lax.logistic(hidden), later_grad[...], ((0,), (0,)))

    def side_hidden():
        back = exact(later_grad[...], second_ref[...], ((1,), (1,)))
        later_grad[...] = back * silu_slope(hidden_ref[...])

    def side_first():
        first_out[...] = exact(features_ref[...], later_grad[...], ((0,), (0,)))

    def side_end():
        waits[3]()

    units = [(chunk, split) for chunk in range(chunks) for split in range(splits)]
    slots = {}

    def sems(unit, name):
        slot = slots.setdefault(name, len(slots))
        return send_sems.at[unit, slot], recv_sems.at[unit, slot]

    def add_into(target, source):
        @pl.loop(0, target.shape[0])
        def _(index):
            target[index] = target[index] + source[index]

    def twin_copy(unit):
        chunk, split = units[unit]
        send, recv = sems(unit, "twin")
        return pltpu.make_async_remote_copy(
            src_ref=parts[chunk].at[:, 1 - core, :, :, split],
            dst_ref=twin.at[unit],
            send_sem=send,
            recv_sem=recv,
            device_id=device(core=1 - core),
            device_id_type=MESH,
        )

    def held_copy(unit):
        chunk, split = units[unit]
        return pltpu.make_async_copy(
            parts[chunk].at[:, core, :, :, split], held.at[unit], sems(unit, "held")[1]
        )

    def line_steps(unit, axis, name, pick, landing):
        size, here = lines[axis], at[axis]
        tasks = []

        def slot_of(up, hop):
            return 0 if size == 2 else hop - 1 + (size - 1 if up else 0)

        def copy(up, hop):
            target = here + hop if up else here - hop
            send, recv = sems(unit, (name, up, hop))
            slot = slot_of(up, hop)
            safe = lax.rem(target + size, size)
            beside = here + 1 if up else here - 1
            beside = lax.rem(beside + size, size)
            return pltpu.make_async_remote_copy(
                src_ref=pick(safe),
                dst_ref=landing(slot),
                send_sem=send,
                recv_sem=recv,
                device_id=device(**{axis: beside}),
                device_id_type=MESH,
            )

        def sends(up, hop):
            return here + hop <= size - 1 if up else here - hop >= 0

        def arrives(up, hop):
            if up:
                return (here >= 1) & (here + hop - 1 <= size - 1)
            return (here <= size - 2) & (here - hop + 1 >= 0)

        def take(up, hop):
            @pl.when(arrives(up, hop))
            def _():
                copy(up, hop).wait_recv()
                slot = slot_of(up, hop)
                target = here + hop - 1 if up else here - hop + 1
                add_into(pick(lax.rem(target + size, size)), landing(slot))

        def give(up, hop):
            @pl.when(sends(up, hop))
            def _():
                copy(up, hop).start()

        def finish(up, hop):
            @pl.when(sends(up, hop))
            def _():
                copy(up, hop).wait_send()

        for hop in range(size - 1, 0, -1):

            def begin(hop=hop):
                for up in (True, False):
                    if hop < size - 1:
                        take(up, hop + 1)
                    give(up, hop)

            tasks.append(begin)

        def close():
            for up in (True, False):
                take(up, 1)

        def drain():
            for hop in range(1, size):
                for up in (True, False):
                    finish(up, hop)

        return tasks, close, drain

    def unit_tasks(unit):
        chunk, split = units[unit]
        block = held.at[unit]
        halves = []
        drains = []
        for half, order in ((0, ("b", "y")), (1, ("y", "b"))):
            rows_a = pl.ds(2 * half, 2)

            def pick_one(target, axis=order[0], rows_a=rows_a):
                if axis == "b":
                    return block.at[:, rows_a, target]
                return block.at[target, rows_a]

            def pick_two(target, axis=order[1], rows_a=rows_a):
                if axis == "b":
                    return block.at[at["y"], rows_a, target]
                return block.at[target, rows_a, at["b"]]

            one = line_steps(
                unit,
                order[0],
                ("one", half),
                pick_one,
                lambda slot, axis=order[0]: (first_b if axis == "b" else first_y).at[unit, slot],
            )
            two = line_steps(
                unit,
                order[1],
                ("two", half),
                pick_two,
                lambda slot, half=half: second.at[unit, half, slot],
            )
            steps = list(one[0])
            joined = two[0][0]

            def pass_on(close=one[1], go=joined):
                close()
                go()

            steps += [pass_on] + list(two[0][1:])
            halves.append((steps, two[1]))
            drains += [one[2], two[2]]
        last = line_steps(
            unit,
            "a",
            "last",
            lambda target: block.at[at["y"], target, pl.ds(at["b"], 1)],
            lambda slot: third.at[unit, slot],
        )
        drains.append(last[2])
        out = outs[chunk]

        def spread_copy(owner, to):
            send, recv = sems(unit, ("spread", owner[2], to[2]))
            return pltpu.make_async_remote_copy(
                src_ref=out.at[owner[0], owner[1], split],
                dst_ref=out.at[owner[0], owner[1], split],
                send_sem=send,
                recv_sem=recv,
                device_id=device(y=to[0], core=to[1]),
                device_id_type=MESH,
            )

        size_y = lines["y"]
        me = (at["y"], core, 0)
        twin_place = (at["y"], 1 - core, "twin")

        def far(step):
            return (lax.rem(at["y"] + step, size_y), core, step)

        def start():
            held_copy(unit).wait()
            twin_copy(unit).wait_recv()

            @pl.loop(0, block.shape[0])
            def _(row):
                @pl.loop(0, block.shape[1])
                def _(group):
                    block[row, group] = block[row, group] + twin[unit, row, group]

            for steps, _ in halves:
                steps[0]()

        tasks = [start]
        for index in range(1, len(halves[0][0])):

            def middle(index=index):
                for steps, _ in halves:
                    steps[index]()

            tasks.append(middle)

        def to_last():
            for _, close in halves:
                close()
            last[0][0]()

        tasks.append(to_last)
        tasks += list(last[0][1:])

        def sum_done():
            last[1]()
            out[at["y"], core, split] = block[at["y"], at["a"], at["b"]]
            for step in range(1, size_y):
                spread_copy(me, far(step)).start()
            spread_copy(me, twin_place).start()

        tasks.append(sum_done)

        def before(step):
            return (lax.rem(at["y"] + size_y - step, size_y), core, step)

        def forward():
            for step in range(1, size_y):
                spread_copy((at["y"], core, 0), far(step)).wait_recv()
                source = before(step)
                spread_copy(source, twin_place).start()

        tasks.append(forward)

        def end():
            spread_copy(me, twin_place).wait()
            for step in range(1, size_y):
                spread_copy(before(step), twin_place).wait()
                spread_copy(me, far(step)).wait_send()
            twin_copy(unit).wait_send()
            for drain in drains:
                drain()

        tasks.append(end)
        return tasks

    for unit in range(len(units)):
        twin_copy(unit).start()
        held_copy(unit).start()
    side_start()
    queues = [unit_tasks(unit) for unit in range(len(units))]
    depth = len(queues[0])
    for tick in range(len(units) + depth - 1):
        for unit in reversed(range(len(units))):
            task = tick - unit
            if 0 <= task < depth:
                queues[unit][task]()
        if tick == 1:
            side_signal()
        if tick == 3:
            side_show()
        if tick == 6:
            side_second()
        if tick == 7:
            side_hidden()
        if tick == 8:
            side_first()
    side_end()


def reduce_weights(partials, sides, collective_id):
    copies, groups = lax.axis_size("dp"), lax.axis_size("mp")
    back, _, shared, features, _, condition, _ = sides
    rows, width = partials[0].shape
    size_b, size_y = groups // 4, copies // 2
    piece = rows // (copies * groups)
    share = 48 if piece % 48 == 0 else piece
    splits = piece // share
    shaped = [
        part.reshape(size_y, 2, 4, size_b, splits, share, width) for part in partials
    ]
    units = splits * len(partials)
    slab = (share, width)
    slots_b = 1 if size_b == 2 else 2 * (size_b - 1)
    slots_y = 1 if size_y == 2 else 2 * (size_y - 1)
    scratch = [
        pltpu.VMEM((units, size_y, 4, size_b) + slab, jnp.bfloat16),
        pltpu.VMEM((units, size_y, 4, size_b) + slab, jnp.bfloat16),
        pltpu.VMEM((units, slots_b, size_y, 2) + slab, jnp.bfloat16),
        pltpu.VMEM((units, slots_y, 2, size_b) + slab, jnp.bfloat16),
        pltpu.VMEM((units, 2, max(slots_b, slots_y), 2) + slab, jnp.bfloat16),
        pltpu.VMEM((units, 6, 1) + slab, jnp.bfloat16),
        pltpu.SemaphoreType.DMA((units, 40)),
        pltpu.SemaphoreType.DMA((units, 40)),
        pltpu.VMEM(shared.shape, jnp.float32),
        pltpu.VMEM((groups, back.shape[1], width), jnp.float32),
        pltpu.VMEM((groups, back.shape[1], width), jnp.float32),
        pltpu.VMEM((8 * groups, back.shape[2]), jnp.float32),
        pltpu.SemaphoreType.DMA((5, copies * groups)),
        pltpu.SemaphoreType.DMA((5, copies * groups)),
        pltpu.VMEM((copies * groups, back.shape[1], width), jnp.float32),
        pltpu.VMEM(condition.shape, jnp.float32),
    ]
    results = pl.pallas_call(
        functools.partial(reduce_kernel, (copies, groups)),
        out_shape=[jax.ShapeDtypeStruct((size_y, 2, splits) + slab, jnp.bfloat16)] * len(partials)
        + [
            jax.ShapeDtypeStruct((copies * groups,) + back.shape[1:], jnp.float32),
            jax.ShapeDtypeStruct(shared.shape, jnp.float32),
            jax.ShapeDtypeStruct((features.shape[1], width), jnp.float32),
            jax.ShapeDtypeStruct((width, width), jnp.float32),
        ],
        in_specs=[pl.BlockSpec(memory_space=pl.ANY)] * len(partials)
        + [pl.BlockSpec(memory_space=pltpu.VMEM)] * 7,
        out_specs=[pl.BlockSpec(memory_space=pltpu.VMEM)] * (len(partials) + 4),
        scratch_shapes=scratch,
        compiler_params=pltpu.CompilerParams(
            collective_id=collective_id, has_side_effects=True, vmem_limit_bytes=62 * 1024 * 1024
        ),
    )(*shaped, *sides)
    sums = [result.reshape(copies * piece, width) for result in results[: len(partials)]]
    return sums, *results[len(partials) :]


def gather_kernel(counts, piece_ref, out_ref, send_sems, recv_sems, local_sems):
    copies, groups = counts
    size_a, size_b, size_y = 4, groups // 4, copies // 2
    splits = piece_ref.shape[0]
    dp, mp = lax.axis_index("dp"), lax.axis_index("mp")
    a, b, y, core = mp // size_b, lax.rem(mp, size_b), dp // 2, lax.rem(dp, 2)

    def device(a=a, b=b, y=y, core=core):
        return (y * 2 + core, a * size_b + b)

    def along(axis, step):
        if axis == "a":
            return device(a=lax.rem(a + step, size_a))
        if axis == "b":
            return device(b=lax.rem(b + step, size_b))
        return device(y=lax.rem(y + step, size_y))

    lines = {"a": size_a, "b": size_b, "y": size_y}
    barrier = pltpu.get_barrier_semaphore()
    pl.semaphore_signal(barrier, inc=1, device_id=device(core=1 - core), device_id_type=MESH)
    for axis, size in lines.items():
        for step in range(1, size):
            pl.semaphore_signal(
                barrier, inc=1, device_id=along(axis, step), device_id_type=MESH
            )
    pl.semaphore_wait(barrier, 1 + sum(size - 1 for size in lines.values()))
    slots = {}

    def place(split, ys, cores, as_, bs):
        return out_ref.at[ys, cores, as_, bs, split]

    def own_copy(split):
        return pltpu.make_async_copy(
            piece_ref.at[split], place(split, y, core, a, b), local_sems.at[split]
        )

    def a_copies(split):
        copies_ = []
        for step in range(1, size_a):
            slot = slots.setdefault(("a", step), len(slots))
            copies_.append(
                pltpu.make_async_remote_copy(
                    src_ref=piece_ref.at[split],
                    dst_ref=place(split, y, core, a, b),
                    send_sem=send_sems.at[split, slot],
                    recv_sem=recv_sems.at[split, slot],
                    device_id=along("a", step),
                    device_id_type=MESH,
                )
            )
        return copies_

    low, high = pl.ds(0, 2), pl.ds(2, 2)
    every_b, every_y, every_a = pl.ds(0, size_b), pl.ds(0, size_y), pl.ds(0, size_a)

    def spread(split, name, axis, source):
        copies_ = []
        for step in range(1, lines[axis]):
            slot = slots.setdefault((name, step), len(slots))
            copies_.append(
                pltpu.make_async_remote_copy(
                    src_ref=source,
                    dst_ref=source,
                    send_sem=send_sems.at[split, slot],
                    recv_sem=recv_sems.at[split, slot],
                    device_id=along(axis, step),
                    device_id_type=MESH,
                )
            )
        return copies_

    def first(split):
        return (
            spread(split, "low_b", "b", place(split, y, core, low, b)),
            spread(split, "high_y", "y", place(split, y, core, high, b)),
        )

    def second(split):
        return (
            spread(split, "low_y", "y", place(split, y, core, low, every_b)),
            spread(split, "high_b", "b", place(split, every_y, core, high, b)),
        )

    def twin(split):
        slot = slots.setdefault("twin", len(slots))
        source = place(split, every_y, core, every_a, every_b)
        return pltpu.make_async_remote_copy(
            src_ref=source,
            dst_ref=source,
            send_sem=send_sems.at[split, slot],
            recv_sem=recv_sems.at[split, slot],
            device_id=device(core=1 - core),
            device_id_type=MESH,
        )

    for split in range(splits):
        own_copy(split).start()
        for item in a_copies(split):
            item.start()

    def to_first(split):
        own_copy(split).wait()
        for item in a_copies(split):
            item.wait_recv()
        for items in first(split):
            for item in items:
                item.start()

    def to_second(split):
        for items, following in zip(first(split), second(split)):
            for item in items:
                item.wait_recv()
            for item in following:
                item.start()

    def to_twin(split):
        for items in second(split):
            for item in items:
                item.wait_recv()
        twin(split).start()

    stages = (to_first, to_second, to_twin)
    for tick in range(splits + len(stages) - 1):
        for split in reversed(range(splits)):
            if 0 <= tick - split < len(stages):
                stages[tick - split](split)
    for split in range(splits):
        twin(split).wait()
        for item in a_copies(split):
            item.wait_send()
        for items in first(split) + second(split):
            for item in items:
                item.wait_send()


def gather_pieces(piece, collective_id):
    copies, groups = lax.axis_size("dp"), lax.axis_size("mp")
    rows, width = piece.shape
    share = 48 if rows % 48 == 0 else rows
    splits = rows // share
    size_b, size_y = groups // 4, copies // 2
    sems = 4 + 2 * (size_b + size_y)
    gathered = pl.pallas_call(
        functools.partial(gather_kernel, (copies, groups)),
        out_shape=jax.ShapeDtypeStruct(
            (size_y, 2, 4, size_b, splits, share, width), jnp.bfloat16
        ),
        in_specs=[pl.BlockSpec(memory_space=pl.ANY)],
        out_specs=pl.BlockSpec(memory_space=pl.ANY),
        scratch_shapes=[
            pltpu.SemaphoreType.DMA((splits, sems)),
            pltpu.SemaphoreType.DMA((splits, sems)),
            pltpu.SemaphoreType.DMA((splits,)),
        ],
        compiler_params=pltpu.CompilerParams(collective_id=collective_id, has_side_effects=True),
    )(piece.reshape(splits, share, width))
    return gathered.reshape(copies * groups * rows, width)


def row_block(rows):
    for block in (128, 144):
        if rows % block == 0:
            return block
    return rows


def scale_kernel(layouts, flipped, *refs):
    slots = len(layouts)
    grads = refs[:slots]
    row_old, column_old = refs[slots : slots + 2]
    row_coef, column_coef, row_new, column_new, shown, norms = refs[slots + 2 : slots + 8]
    by_row, land, mine, send_sems, recv_sems = refs[slots + 8 :]
    member, groups, _ = peers("mp")
    wide = row_old.shape[1]
    lane = lax.broadcasted_iota(jnp.int32, (1, 128), 1)
    place = lax.broadcasted_iota(jnp.int32, (1, wide), 1)
    split = [slot for slot in range(slots) if layouts[slot] != "whole"]
    one = jnp.ones((1, 1), jnp.float32)

    def all_sum(values):
        return jnp.sum(jnp.sum(values, axis=1, keepdims=True), axis=0, keepdims=True)

    greet("mp")
    by_row[...] = jnp.zeros_like(by_row)
    column_sums = []
    squares = []
    for slot in range(slots):
        count, across_ = grads[slot].shape
        block = row_block(count)

        def step(index, total, slot=slot, block=block):
            at = pl.ds(pl.multiple_of(index * block, block), block)
            values = grads[slot][at, :].astype(jnp.float32)
            square = values * values
            by_row[at, :] += jnp.where(lane == slot, jnp.sum(square, axis=1, keepdims=True), 0.0)
            return total + jnp.sum(square, axis=0, keepdims=True)

        total = lax.fori_loop(0, count // block, step, jnp.zeros((1, across_), jnp.float32))
        column_sums.append(total)
        squares.append(jnp.sum(total, axis=1, keepdims=True))
    row_sums = by_row[...].T

    mine[...] = jnp.zeros_like(mine)
    for index, slot in enumerate(split):
        mine[0, index : index + 1, :] = column_sums[slot]
    mine[0, 6:7, :] = sum(squares[slot] for slot in split) * jnp.ones((1, wide), jnp.float32)
    wait = to_all(
        "mp",
        lambda place_: mine.at[0],
        lambda place_: land.at[place_],
        send_sems.at[0],
        recv_sems.at[0],
    )
    land[member] = mine[0]
    wait()
    crossed = sum_over(land)
    local_square = sum(squares[slot] for slot in range(slots) if slot not in split)
    norm = jnp.sqrt(crossed[6:7, :1] + local_square)
    factor = clip_limit / jnp.maximum(norm, clip_limit)
    factor_square = factor * factor
    norms[...] = jnp.where(lax.broadcasted_iota(jnp.int32, (8, 128), 0) == 0, norm, factor)

    averages = []
    many = []
    next_rows = []
    next_columns = []
    inverse = [jnp.ones((1, wide), jnp.float32)] * slots
    for slot, layout in enumerate(layouts):
        count, across_ = grads[slot].shape
        many_rows = count * (groups if layout == "rows" else 1)
        many_columns = across_
        many.append((many_rows, many_columns))
        row_sum = row_sums[slot : slot + 1, :]
        column_sum = column_sums[slot]
        if layout == "rows":
            column_sum = crossed[split.index(slot) : split.index(slot) + 1, :]
        row_mean = row_sum * factor_square / many_columns + eps_factor
        column_mean = column_sum * factor_square / many_rows + eps_factor
        next_row = state_decay * row_old[slot : slot + 1, :] + (1.0 - state_decay) * row_mean
        next_column = (
            state_decay * column_old[slot : slot + 1, :across_] + (1.0 - state_decay) * column_mean
        )
        if flipped[slot]:
            average = jnp.sum(next_column, axis=1, keepdims=True) / across_
        elif layout == "rows":
            first = slots + sum(
                many[other][0] // wide for other in split if other < slot and not flipped[other]
            )
            old = row_old[first : first + many_rows // wide, :]
            average = (
                state_decay * all_sum(old) / many_rows
                + (1.0 - state_decay) * jnp.sum(column_mean, axis=1, keepdims=True) / across_
            )
        else:
            average = (
                jnp.sum(jnp.where(place < count, next_row, 0.0), axis=1, keepdims=True) / many_rows
            )
        averages.append(average)
        next_rows.append(next_row)
        next_columns.append(next_column)
        row_new[slot : slot + 1, :] = next_row
        column_new[slot : slot + 1, :] = next_column
        inverse[slot] = jnp.where(place < count, 1.0 / next_row, 0.0)
    blank = jnp.zeros((128 - slots, wide), jnp.float32)
    by_row[...] = jnp.concatenate(inverse + [blank], axis=0).T

    energies = []
    for slot in range(slots):
        count, across_ = grads[slot].shape
        block = row_block(count)
        inverse_column = 1.0 / next_columns[slot]

        def step(index, total, slot=slot, block=block, inverse_column=inverse_column):
            at = pl.ds(pl.multiple_of(index * block, block), block)
            values = grads[slot][at, :].astype(jnp.float32)
            weighted = jnp.sum(values * values * inverse_column, axis=1, keepdims=True)
            return total + jnp.sum(
                jnp.where(lane == slot, by_row[at, :], 0.0) * weighted, axis=0, keepdims=True
            )

        total = lax.fori_loop(0, count // block, step, jnp.zeros((1, 128), jnp.float32))
        energies.append(
            jnp.sum(total, axis=1, keepdims=True) * factor_square * averages[slot]
        )

    mine[1, :, :] = jnp.zeros_like(mine[1])
    for index, slot in enumerate(split):
        mine[1, index : index + 1, :] = next_rows[slot]
    spread = jnp.zeros((1, wide), jnp.float32)
    for slot in split:
        spread = jnp.where(place == slot, energies[slot], spread)
    mine[1, 6:7, :] = spread
    wait = to_all(
        "mp",
        lambda place_: mine.at[1],
        lambda place_: shown.at[place_],
        send_sems.at[1],
        recv_sems.at[1],
    )
    shown[member] = mine[1]
    wait()
    spread = sum_over(shown)[6:7, :]
    coefs = []
    for slot, layout in enumerate(layouts):
        many_rows, many_columns = many[slot]
        energy = energies[slot]
        if layout != "whole":
            energy = jnp.sum(jnp.where(place == slot, spread, 0.0), axis=1, keepdims=True)
        scale_down = jnp.maximum(one, jnp.sqrt(energy / (many_rows * many_columns)))
        shrink = (
            step_rate / math.sqrt(many[slot][1 if flipped[slot] else 0]) * factor * jnp.sqrt(averages[slot]) / scale_down
        )
        coefs.append(shrink * lax.rsqrt(next_rows[slot]))
        column_coef[slot : slot + 1, :] = lax.rsqrt(next_columns[slot])
    row_coef[...] = jnp.concatenate(coefs + [blank], axis=0).T


def scales(gradients, row_old, column_old, layouts, flipped, collective_id):
    groups = lax.axis_size("mp")
    wide = row_old.shape[1]
    shape = lambda *dims: jax.ShapeDtypeStruct(dims, jnp.float32)
    vmem = pl.BlockSpec(memory_space=pltpu.VMEM)
    return pl.pallas_call(
        functools.partial(scale_kernel, layouts, flipped),
        out_shape=[
            shape(wide, 128),
            shape(16, wide),
            shape(16, wide),
            shape(16, wide),
            shape(groups, 8, wide),
            shape(8, 128),
        ],
        in_specs=[vmem] * (len(gradients) + 2),
        out_specs=[vmem] * 6,
        scratch_shapes=[
            pltpu.VMEM((wide, 128), jnp.float32),
            pltpu.VMEM((groups, 8, wide), jnp.float32),
            pltpu.VMEM((2, 8, wide), jnp.float32),
            pltpu.SemaphoreType.DMA((2, groups)),
            pltpu.SemaphoreType.DMA((2, groups)),
        ],
        compiler_params=pltpu.CompilerParams(
            collective_id=collective_id, has_side_effects=True, vmem_limit_bytes=56 * 1024 * 1024
        ),
    )(*gradients, row_old, column_old)


def apply_kernel(layouts, flipped, groups, *refs):
    slots = len(layouts)
    grads, weights = refs[:slots], refs[slots : 2 * slots]
    row_coef, column_coef, row_new, column_new, shown, norms = refs[2 * slots : 2 * slots + 6]
    rest = refs[2 * slots + 6 :]
    nexts, clips = rest[:slots], rest[slots : 2 * slots]
    row_stats, column_stats = rest[2 * slots : 2 * slots + 2]
    held, clipped = rest[2 * slots + 2 : 3 * slots + 2], rest[3 * slots + 2 : 4 * slots + 2]
    sems = rest[4 * slots + 2]
    low = [grads[slot].dtype == jnp.bfloat16 for slot in range(slots)]
    order = sorted(range(slots), key=lambda slot: -weights[slot].size)

    def weight_in(slot):
        return pltpu.make_async_copy(weights[slot], held[slot], sems.at[0, slot])

    def grad_in(slot):
        return pltpu.make_async_copy(grads[slot], clipped[slot], sems.at[1, slot])

    def weight_out(slot):
        return pltpu.make_async_copy(held[slot], nexts[slot], sems.at[2, slot])

    def grad_out(slot):
        return pltpu.make_async_copy(clipped[slot], clips[slot], sems.at[3, slot])

    for slot in order:
        weight_in(slot).start()
        if not low[slot]:
            grad_in(slot).start()

    split = [slot for slot in range(slots) if layouts[slot] != "whole"]
    ends = [0, 0]
    for slot, layout in enumerate(layouts):
        count, across_ = weights[slot].shape
        own, other = (column_stats, row_stats) if flipped[slot] else (row_stats, column_stats)
        own_end, other_end = (1, 0) if flipped[slot] else (0, 1)
        at = ends[own_end]
        if layout == "rows":
            spot = split.index(slot)
            for member in range(groups):
                own[:, at : at + count] = shown[member, spot : spot + 1, :count]
                at += count
        else:
            own[:, at : at + count] = row_new[slot : slot + 1, :count]
            at += count
        ends[own_end] = at
        other[:, ends[other_end] : ends[other_end] + across_] = column_new[slot : slot + 1, :]
        ends[other_end] += across_

    factor = norms[1:2, :1]
    for slot in order:
        count, across_ = weights[slot].shape
        block = row_block(count)
        weight_in(slot).wait()
        if not low[slot]:
            grad_in(slot).wait()
        source = grads[slot] if low[slot] else clipped[slot]
        by_column = column_coef[slot : slot + 1, :across_]

        @pl.loop(0, count // block)
        def _(index, slot=slot, block=block, source=source, by_column=by_column):
            at = pl.ds(pl.multiple_of(index * block, block), block)
            gradient = source[at, :].astype(jnp.float32)
            step_size = row_coef[at, slot : slot + 1] * by_column
            held[slot][at, :] = held[slot][at, :] - gradient * step_size
            clipped[slot][at, :] = gradient * factor

        weight_out(slot).start()
        grad_out(slot).start()
    for slot in order:
        weight_out(slot).wait()
        grad_out(slot).wait()


def apply_scales(gradients, weights, found, layouts, flipped):
    groups = lax.axis_size("mp")
    vmem = pl.BlockSpec(memory_space=pltpu.VMEM)
    stay = pl.BlockSpec(memory_space=pl.ANY)
    many_rows = 0
    many_columns = 0
    for weight, layout, flip in zip(weights, layouts, flipped):
        extents = (weight.shape[0] * (groups if layout == "rows" else 1), weight.shape[1])
        many_rows += extents[1 if flip else 0]
        many_columns += extents[0 if flip else 1]
    shapes = [jax.ShapeDtypeStruct(weight.shape, jnp.float32) for weight in weights]
    buffers = [pltpu.VMEM(weight.shape, jnp.float32) for weight in weights]
    size = sum(weight.size for weight in weights)
    results = pl.pallas_call(
        functools.partial(apply_kernel, layouts, flipped, groups),
        out_shape=shapes
        + shapes
        + [
            jax.ShapeDtypeStruct((1, many_rows), jnp.float32),
            jax.ShapeDtypeStruct((1, many_columns), jnp.float32),
        ],
        in_specs=[vmem if part.dtype == jnp.bfloat16 else stay for part in gradients]
        + [stay] * len(weights)
        + [vmem] * 6,
        out_specs=[stay] * (2 * len(weights)) + [vmem] * 2,
        scratch_shapes=buffers + buffers + [pltpu.SemaphoreType.DMA((4, len(weights)))],
        compiler_params=pltpu.CompilerParams(vmem_limit_bytes=58 * 1024 * 1024),
        cost_estimate=pl.CostEstimate(flops=4 * size, bytes_accessed=16 * size, transcendentals=0),
    )(*gradients, *weights, *found)
    count = len(weights)
    return (
        results[:count],
        results[count : 2 * count],
        results[2 * count].reshape(-1),
        results[2 * count + 1].reshape(-1),
    )


def weights_of(keys, queries, live):
    scores = product_left(keys, queries) * HD ** (-0.5)
    scores = jnp.where(live, scores, neg_large)
    exponent = jnp.exp(scores - jnp.max(scores, axis=0, keepdims=True))
    return exponent / jnp.sum(exponent, axis=0, keepdims=True)


def attend_kernel(length_ref, q_ref, k_ref, v_ref, out_ref):
    patches = q_ref.shape[1]
    pair = 2 * HD
    live = lax.broadcasted_iota(jnp.int32, (patches, patches), 0) < length_ref[pl.program_id(0)]
    upper = lax.broadcasted_iota(jnp.int32, (pair, patches), 0) < HD

    @pl.loop(0, q_ref.shape[0] // pair, unroll=8)
    def _(index):
        rows = pl.ds(pl.multiple_of(index * pair, 16), pair)
        queries, keys, values = q_ref[rows, :], k_ref[rows, :], v_ref[rows, :]
        zero = jnp.zeros_like(queries)
        mixed = []
        for half in range(2):
            own = upper if half == 0 else ~upper
            probs = weights_of(keys, jnp.where(own, queries, zero), live)
            mixed.append(product(values, probs.astype(jnp.bfloat16)))
        out_ref[rows, :] = jnp.where(upper, mixed[0], mixed[1]).astype(jnp.bfloat16)


def attend_back_kernel(length_ref, q_ref, k_ref, v_ref, up_ref, mixed_ref, down_ref):
    down_ref[3] = mixed_ref[...]
    patches = q_ref.shape[1]
    pair = 2 * HD
    live = lax.broadcasted_iota(jnp.int32, (patches, patches), 0) < length_ref[pl.program_id(0)]
    upper = lax.broadcasted_iota(jnp.int32, (pair, patches), 0) < HD

    @pl.loop(0, q_ref.shape[0] // pair, unroll=8)
    def _(index):
        rows = pl.ds(pl.multiple_of(index * pair, 16), pair)
        queries, keys, values, upstream = (
            q_ref[rows, :],
            k_ref[rows, :],
            v_ref[rows, :],
            up_ref[rows, :],
        )
        zero = jnp.zeros_like(queries)
        found = []
        for half in range(2):
            own = upper if half == 0 else ~upper
            probs = weights_of(keys, jnp.where(own, queries, zero), live)
            probs_grad = product_left(values, jnp.where(own, upstream, zero))
            weighted = probs * probs_grad
            score_grad = (
                weighted - probs * jnp.sum(weighted, axis=0, keepdims=True)
            ).astype(jnp.bfloat16)
            found.append(
                (
                    product(keys, score_grad),
                    product_right(queries, score_grad),
                    product_right(upstream, probs.astype(jnp.bfloat16)),
                )
            )
        scale = HD ** (-0.5)
        down_ref[0, rows, :] = (jnp.where(upper, found[0][0], found[1][0]) * scale).astype(jnp.bfloat16)
        down_ref[1, rows, :] = (jnp.where(upper, found[0][1], found[1][1]) * scale).astype(jnp.bfloat16)
        down_ref[2, rows, :] = jnp.where(upper, found[0][2], found[1][2]).astype(jnp.bfloat16)


def _specs(width, patches):
    def spec(block):
        return pl.BlockSpec((width, patches), lambda image, lengths: (block, image))

    return spec


def attend(qkv, lengths, images):
    width, rows = qkv.shape[0] // 3, qkv.shape[1]
    patches = rows // images
    spec = _specs(width, patches)
    return pl.pallas_call(
        attend_kernel,
        grid_spec=pltpu.PrefetchScalarGridSpec(
            num_scalar_prefetch=1,
            grid=(images,),
            in_specs=[spec(0), spec(1), spec(2)],
            out_specs=spec(0),
        ),
        out_shape=jax.ShapeDtypeStruct((width, rows), jnp.bfloat16),
        compiler_params=pltpu.CompilerParams(vmem_limit_bytes=48 * 1024 * 1024),
        cost_estimate=pl.CostEstimate(flops=4 * rows * patches * width, bytes_accessed=8 * rows * width, transcendentals=0),
    )(lengths, qkv, qkv, qkv)


def attend_back(qkv, upstream, mixed, lengths, images):
    width, rows = upstream.shape
    patches = rows // images
    spec = _specs(width, patches)
    return pl.pallas_call(
        attend_back_kernel,
        grid_spec=pltpu.PrefetchScalarGridSpec(
            num_scalar_prefetch=1,
            grid=(images,),
            in_specs=[spec(0), spec(1), spec(2), spec(0), spec(0)],
            out_specs=pl.BlockSpec((4, width, patches), lambda image, lengths: (0, 0, image)),
        ),
        out_shape=jax.ShapeDtypeStruct((4, width, rows), jnp.bfloat16),
        compiler_params=pltpu.CompilerParams(vmem_limit_bytes=48 * 1024 * 1024),
        cost_estimate=pl.CostEstimate(flops=10 * rows * patches * width, bytes_accessed=14 * rows * width, transcendentals=0),
    )(lengths, qkv, qkv, qkv, upstream, mixed)


def mixer_weights_kernel(left_ref, input_ref, branch_ref, out_ref):
    @pl.when(pl.program_id(0) < 3)
    def _():
        out_ref[...] = product(left_ref[0], input_ref[...]).astype(jnp.bfloat16)

    @pl.when(pl.program_id(0) == 3)
    def _():
        out_ref[...] = product(left_ref[0], branch_ref[...]).astype(jnp.bfloat16)


def mixer_weights(left, input_one, branch_one_grad):
    _, width, rows = left.shape
    whole = pl.BlockSpec((rows, width), lambda part: (0, 0))
    return pl.pallas_call(
        mixer_weights_kernel,
        grid=(4,),
        in_specs=[pl.BlockSpec((1, width, rows), lambda part: (part, 0, 0)), whole, whole],
        out_specs=pl.BlockSpec((width, width), lambda part: (part, 0)),
        out_shape=jax.ShapeDtypeStruct((4 * width, width), jnp.bfloat16),
        compiler_params=pltpu.CompilerParams(vmem_limit_bytes=48 * 1024 * 1024),
        cost_estimate=pl.CostEstimate(
            flops=8 * rows * width * width, bytes_accessed=20 * rows * width, transcendentals=0
        ),
    )(left, input_one, branch_one_grad)


def input_back_kernel(
    left_ref, weight_ref, residual_ref, upstream_ref, scale_ref, noisy_ref, shift_out, scale_out, embed_out
):
    _, width, patches = left_ref.shape
    grad = product_left(left_ref[...].reshape(3 * width, patches), weight_ref[...])
    values = residual_ref[...]
    normed = layer_norm(values)
    shift_out[0] = jnp.sum(grad, axis=0, keepdims=True)
    scale_out[0] = jnp.sum(grad * normed, axis=0, keepdims=True)
    residual_grad = upstream_ref[...] + norm_back(values, grad * (1.0 + scale_ref[0]))

    @pl.when(pl.program_id(0) == 0)
    def _():
        embed_out[...] = jnp.zeros_like(embed_out)

    embed_out[...] += product_left(noisy_ref[...], residual_grad.astype(jnp.bfloat16))


def input_back(left, weights, residual_zero, grad_residual, scale_one, noisy):
    _, width, rows = left.shape
    images, patches, _ = residual_zero.shape
    by_image = pl.BlockSpec((patches, width), lambda image: (image, 0))
    vector = pl.BlockSpec((1, 1, width), lambda image: (image, 0, 0))
    return pl.pallas_call(
        input_back_kernel,
        grid=(images,),
        in_specs=[
            pl.BlockSpec((3, width, patches), lambda image: (0, 0, image)),
            pl.BlockSpec((3 * width, width), lambda image: (0, 0)),
            by_image,
            by_image,
            vector,
            pl.BlockSpec((patches, noisy.shape[1]), lambda image: (image, 0)),
        ],
        out_specs=[vector, vector, pl.BlockSpec((noisy.shape[1], width), lambda image: (0, 0))],
        out_shape=[
            jax.ShapeDtypeStruct((images, 1, width), jnp.float32),
            jax.ShapeDtypeStruct((images, 1, width), jnp.float32),
            jax.ShapeDtypeStruct((noisy.shape[1], width), jnp.float32),
        ],
        compiler_params=pltpu.CompilerParams(vmem_limit_bytes=48 * 1024 * 1024),
        cost_estimate=pl.CostEstimate(
            flops=6 * rows * width * width, bytes_accessed=20 * rows * width, transcendentals=0
        ),
    )(
        left,
        weights,
        residual_zero.reshape(rows, width),
        grad_residual.reshape(rows, width),
        scale_one.reshape(images, 1, width),
        noisy,
    )


def across(values, axes):
    return lax.all_gather(values, axes, axis=0, tiled=True)


def gather_weight(piece):
    return across(piece, ("dp", "mp"))


def reduce_weight(partial):
    piece = lax.psum_scatter(partial, ("dp", "mp"), scatter_dimension=0, tiled=True)
    return across(piece, "dp")


def body(
    latents,
    noise_draw,
    alpha_bar,
    timesteps,
    labels,
    lengths,
    class_vectors,
    embedder,
    time_first,
    time_second,
    modulator,
    mixer_input,
    mixer_output,
    expander,
    contractor,
    finisher,
    readout,
    row_states,
    column_states,
):
    copies = lax.axis_size("dp")
    groups = lax.axis_size("mp")
    copy = lax.axis_index("dp")
    member = lax.axis_index("mp")
    width = embedder.shape[1]
    patches = SIDE * SIDE
    images = latents.shape[0]
    rows = images * patches
    heads = width // HD
    heads_here = mixer_input.shape[1] // (3 * HD)
    hidden_here = expander.shape[1]
    valid_total = jnp.sum(lengths).astype(jnp.float32) * PIN
    own_lengths = lax.dynamic_slice_in_dim(lengths, (copy * groups + member) * images, images)
    own_alpha = lax.dynamic_slice_in_dim(alpha_bar, member * images, images)

    mixer_rows = (
        mixer_input.astype(jnp.bfloat16)
        .T.reshape(heads_here, 3, HD, width)
        .transpose(1, 0, 2, 3)
        .reshape(3 * heads_here * HD, width)
    )
    shards = (
        jnp.concatenate([mixer_rows, mixer_output.astype(jnp.bfloat16)], axis=0),
        expander.astype(jnp.bfloat16).T,
        contractor.astype(jnp.bfloat16),
    )
    gathered = []
    for slot, shard in enumerate(shards):
        piece_rows = shard.shape[0] // copies
        piece = lax.dynamic_slice_in_dim(shard, copy * piece_rows, piece_rows)
        gathered.append(gather_pieces(piece, 8) if slot == 0 else gather_weight(piece))
    parts = copies // 4
    piece_rows = shards[0].shape[0] // copies
    mixer_all = (
        gathered[0]
        .reshape(4, parts, groups, piece_rows, width)
        .transpose(0, 2, 1, 3, 4)
        .reshape(4 * width, width)
    )
    inputs_use = mixer_all[: 3 * width]
    outputs_use = mixer_all[3 * width :]
    expand_use = gathered[1]
    contract_use = gathered[2]

    group_images = groups * images
    asked = jnp.stack([timesteps, labels]).astype(jnp.float32)
    asked = jnp.pad(asked, ((0, 6), (0, 128 - group_images)))
    asked = swap(asked, "dp", 1, per_target=False)[:, :2, :group_images]
    steps_all, labels_all = asked.transpose(1, 0, 2).reshape(2, copies * group_images).astype(jnp.int32)
    features = time_features(steps_all, FREQ)
    class_rows = jnp.take(class_vectors, labels_all, axis=0).astype(jnp.float32)
    hidden_pre = jnp.dot(features, time_first, precision=highest)
    condition = jnp.dot(jax.nn.silu(hidden_pre), time_second, precision=highest) + class_rows
    signal_all = jax.nn.silu(condition).astype(jnp.bfloat16)
    signal = lax.dynamic_slice_in_dim(signal_all, copy * group_images, group_images)
    mods_low = jnp.concatenate(
        [modulator.T.astype(jnp.bfloat16), finisher.T.astype(jnp.bfloat16)], axis=0
    )
    steer_here, final_here = modulator.shape[1], finisher.shape[1]
    mods_part = product_right(signal, mods_low)
    mods_part = lax.reduce_precision(mods_part, 8, 7)
    mods_own = swap(mods_part.reshape(groups, -1, 128), "mp", 2)
    mods_own = mods_own.reshape(groups, images, steer_here + final_here).transpose(1, 0, 2)
    steering = mods_own[:, :, :steer_here].reshape(images, 6, 1, width)
    final_steer = mods_own[:, :, steer_here:].reshape(images, 2, 1, width)

    embedder_low = embedder.astype(jnp.bfloat16)
    readout_low = readout.astype(jnp.bfloat16)
    place = jnp.arange(patches)
    live = place[None, :] < own_lengths[:, None]
    root_keep = jnp.sqrt(own_alpha)[:, None, None]
    root_noise = jnp.sqrt(1.0 - own_alpha)[:, None, None]
    noisy = (root_keep * latents + root_noise * noise_draw).astype(jnp.bfloat16).reshape(rows, PIN)
    target = (root_keep * noise_draw - root_noise * latents).reshape(rows, PIN)
    residual_zero = (
        product(noisy, embedder_low).reshape(images, patches, width)
        + position_table(SIDE, width)[None]
    )
    normed_one = layer_norm(residual_zero)
    input_one = (
        (normed_one * (1.0 + steering[:, 1]) + steering[:, 0])
        .astype(jnp.bfloat16)
        .reshape(rows, width)
    )
    qkv = product_right(inputs_use, input_one).astype(jnp.bfloat16)
    mixed = attend(qkv, own_lengths, images)
    branch_one = product_left(mixed, outputs_use).reshape(images, patches, width)
    residual_one = residual_zero + steering[:, 2] * branch_one
    normed_two = layer_norm(residual_one)
    input_two = (
        (normed_two * (1.0 + steering[:, 4]) + steering[:, 3])
        .astype(jnp.bfloat16)
        .reshape(rows, width)
    )
    pre_active = product_right(input_two, expand_use)
    active = jax.nn.gelu(pre_active, approximate=True).astype(jnp.bfloat16)
    branch_two = product(active, contract_use).reshape(images, patches, width)
    residual_two = residual_one + steering[:, 5] * branch_two
    normed_final = layer_norm(residual_two)
    input_final = (
        (normed_final * (1.0 + final_steer[:, 1]) + final_steer[:, 0])
        .astype(jnp.bfloat16)
        .reshape(rows, width)
    )
    misfit = product(input_final, readout_low) - target
    live_rows = live.reshape(rows, 1)
    loss_part = jnp.sum(jnp.where(live_rows, misfit * misfit, 0.0))

    output_grad = jnp.where(live_rows, 2.0 * misfit / valid_total, 0.0).astype(jnp.bfloat16)
    readout_part = product_left(output_grad, input_final)
    final_grad = product_right(output_grad, readout_low).reshape(images, patches, width)
    final_shift_grad = jnp.sum(final_grad, axis=1)
    final_scale_grad = jnp.sum(final_grad * normed_final, axis=1)
    grad_residual = norm_back(residual_two, final_grad * (1.0 + final_steer[:, 1]))
    gate_two_grad = jnp.sum(grad_residual * branch_two, axis=1)
    branch_two_grad = (steering[:, 5] * grad_residual).astype(jnp.bfloat16).reshape(rows, width)
    contract_part = product_left(active, branch_two_grad).astype(jnp.bfloat16)
    active_grad = product_right(branch_two_grad, contract_use)
    gelu_pull = jax.vjp(lambda inner: jax.nn.gelu(inner, approximate=True), pre_active)[1]
    pre_grad = gelu_pull(active_grad)[0].astype(jnp.bfloat16)
    expand_part = product_left(pre_grad, input_two).astype(jnp.bfloat16)
    input_two_grad = product(pre_grad, expand_use).reshape(images, patches, width)
    shift_two_grad = jnp.sum(input_two_grad, axis=1)
    scale_two_grad = jnp.sum(input_two_grad * normed_two, axis=1)
    grad_residual = grad_residual + norm_back(
        residual_one, input_two_grad * (1.0 + steering[:, 4])
    )
    gate_one_grad = jnp.sum(grad_residual * branch_one, axis=1)
    branch_one_grad = (steering[:, 2] * grad_residual).astype(jnp.bfloat16).reshape(rows, width)
    mixed_grad = product_right(outputs_use, branch_one_grad).astype(jnp.bfloat16)
    mixer_left = attend_back(qkv, mixed_grad, mixed, own_lengths, images)
    shift_one_grad, scale_one_grad, embed_part = input_back(
        mixer_left, mixer_all, residual_zero, grad_residual, steering[:, 1], noisy
    )
    shift_one_grad = shift_one_grad.reshape(images, width)
    scale_one_grad = scale_one_grad.reshape(images, width)
    mixer_part = mixer_weights(mixer_left, input_one, branch_one_grad)

    mixer_part = (
        mixer_part.reshape(4, groups, parts, piece_rows, width)
        .transpose(0, 2, 1, 3, 4)
        .reshape(4 * width, width)
    )
    steer_back = jnp.stack(
        [
            shift_one_grad,
            scale_one_grad,
            gate_one_grad,
            shift_two_grad,
            scale_two_grad,
            gate_two_grad,
        ],
        axis=1,
    )
    steer_back = lax.reduce_precision(steer_back.reshape(images, 6 * width), 8, 7)
    final_back = jnp.stack([final_shift_grad, final_scale_grad], axis=1)
    final_back = lax.reduce_precision(final_back.reshape(images, 2 * width), 8, 7)
    back = jnp.concatenate(
        [
            steer_back.reshape(images, groups, steer_here),
            final_back.reshape(images, groups, final_here),
        ],
        axis=2,
    )
    back = back.transpose(1, 0, 2)
    shared = slabs(
        jnp.concatenate([embed_part.reshape(-1), readout_part.reshape(-1), loss_part[None]]),
        copies * groups,
    )
    contract_sum = reduce_weight(contract_part)
    sides = (back, mods_low, shared, features, hidden_pre, condition, time_second)
    together = [expand_part, mixer_part] if piece_rows % 48 == 0 else [mixer_part]
    sums, cols_all, shared, time_first_sum, time_second_sum = reduce_weights(together, sides, 3)
    expand_sum = sums[0] if len(together) == 2 else reduce_weight(expand_part)
    mixer_sum = sums[-1]
    held = heads_here * HD
    inputs_sum = (
        mixer_sum[: 3 * held]
        .reshape(3, heads_here, HD, width)
        .transpose(1, 0, 2, 3)
        .reshape(3 * held, width)
    )
    outputs_sum = mixer_sum[3 * held :]
    cols_all = cols_all.astype(jnp.bfloat16).reshape(copies * group_images, -1)
    shared = shared.reshape(-1)
    embed_sum = shared[: embedder.size].reshape(embedder.shape)
    readout_sum = shared[embedder.size : embedder.size + readout.size].reshape(-1, width)
    loss_sum = shared[embedder.size + readout.size]
    modulator_sum = product_left(cols_all[:, :steer_here], signal_all)
    finisher_sum = product_left(cols_all[:, steer_here:], signal_all)
    gradients = (
        embed_sum,
        time_first_sum,
        time_second_sum,
        modulator_sum,
        inputs_sum,
        outputs_sum,
        expand_sum,
        contract_sum,
        finisher_sum,
        readout_sum,
    )
    weights = (
        embedder,
        time_first,
        time_second,
        modulator.T,
        mixer_input.T,
        mixer_output,
        expander.T,
        contractor,
        finisher.T,
        readout.T,
    )
    layouts = ("whole",) * 3 + ("rows",) * 6 + ("whole",)
    flipped = (False, False, False, True, True, False, True, False, True, True)
    ends = {"row": 0, "column": 0}
    row_parts = []
    column_parts = []
    whole_rows = []
    for weight, layout, flip in zip(weights, layouts, flipped):
        count = weight.shape[0]
        many = count * (groups if layout == "rows" else 1)
        own, other = ("column", "row") if flip else ("row", "column")
        states = {"row": row_states, "column": column_states}
        start = ends[own] + (member * count if layout == "rows" else 0)
        part = lax.dynamic_slice_in_dim(states[own], start, count)
        row_parts.append(jnp.pad(part, (0, width - count), constant_values=1.0))
        column_parts.append(states[other][ends[other] : ends[other] + width])
        if layout == "rows" and not flip:
            whole_rows.append(states[own][ends[own] : ends[own] + many].reshape(-1, width))
        ends[own] += many
        ends[other] += width
    row_old = jnp.concatenate([jnp.stack(row_parts)] + whole_rows)
    column_old = jnp.stack(column_parts)
    found = scales(gradients, row_old, column_old, layouts, flipped, 6)
    next_list, clipped_list, row_stats, column_stats = apply_scales(
        gradients, weights, found, layouts, flipped
    )
    next_list = [part.T if flip else part for part, flip in zip(next_list, flipped)]
    clipped_list = [part.T if flip else part for part, flip in zip(clipped_list, flipped)]
    return (
        loss_sum,
        valid_total,
        found[5][0, 0],
        *next_list,
        *clipped_list,
        row_stats,
        column_stats,
    )


def solution(mesh):
    in_specs = (
        P(("dp", "mp"), None, None),
        P(("dp", "mp"), None, None),
        P("dp"),
        P("dp"),
        P("dp"),
        P(),
        P(),
        P(),
        P(),
        P(),
        P(None, "mp"),
        P(None, "mp"),
        P("mp", None),
        P(None, "mp"),
        P("mp", None),
        P(None, "mp"),
        P(),
        P(),
        P(),
    )
    out_specs = (
        P(),
        P(),
        P(),
        P(),
        P(),
        P(),
        P(None, "mp"),
        P(None, "mp"),
        P("mp", None),
        P(None, "mp"),
        P("mp", None),
        P(None, "mp"),
        P(),
        P(),
        P(),
        P(),
        P(None, "mp"),
        P(None, "mp"),
        P("mp", None),
        P(None, "mp"),
        P("mp", None),
        P(None, "mp"),
        P(),
        P(),
        P(),
    )
    return jax.shard_map(body, mesh=mesh, in_specs=in_specs, out_specs=out_specs, check_vma=False)
```
